32 devices in a mesh: dp: 16 (over z, y, core), tp: 2 (over x).
Axes of the slice: x: 2, y: 2, z: 4, core: 2. Of those that a mesh axis runs over, the one named last changes fastest.
Arguments:
- x_in: bfloat16 [128, 512, 512], P('dp', 'tp'), may hold values from -6 to 6
- conv_w: bfloat16 [2, 512, 9, 512], P(None, 'tp'), may hold values from -0.09375 to 0.09375
- conv_b: bfloat16 [2, 512], P(None, 'tp'), may hold values from -3 to 3
- ln_gain: bfloat16 [2, 2, 512], P(None, None, 'tp'), may hold values from 0.099609375 to 1.8984375
- ln_bias: bfloat16 [2, 2, 512], P(None, None, 'tp'), may hold values from -2 to 2
- up_w: bfloat16 [2, 512, 512], P(None, None, 'tp'), may hold values from -0.25 to 0.25
- up_b: bfloat16 [2, 512], P(None, 'tp'), may hold values from -3 to 3
- down_w: bfloat16 [2, 512, 512], P(None, 'tp'), may hold values from -0.25 to 0.25
- down_b: bfloat16 [2, 512], P(None, 'tp'), may hold values from -3 to 3
- readout: bfloat16 [512, 6], P('tp'), may hold values from -0.25 to 0.25
- cotangent: bfloat16 [128, 512, 512], P('dp', 'tp'), may hold values from -6 to 6
- masked: int32 [128, 512], P('dp'), may hold values from 0 to 1, as said below
- species: int32 [128], P('dp'), may hold values from 0 to 7
Outputs:
- y_out: bfloat16 [128, 512, 512], P('dp', 'tp')
- grad_x: float32 [128, 512, 512], P('dp', 'tp')
- grad_conv_w: float32 [2, 512, 9, 512], P(None, 'tp')
- grad_conv_b: float32 [2, 512], P(None, 'tp')
- grad_ln_gain: float32 [2, 2, 512], P(None, None, 'tp')
- grad_ln_bias: float32 [2, 2, 512], P(None, None, 'tp')
- grad_up_w: float32 [2, 512, 512], P(None, None, 'tp')
- grad_up_b: float32 [2, 512], P(None, 'tp')
- grad_down_w: float32 [2, 512, 512], P(None, 'tp')
- grad_down_b: float32 [2, 512], P(None, 'tp')
- species_sum: float32 [8, 6], replicated
The draws below stay inside these ranges and needn't reach their ends.
Inputs may be any that keep to these rules, and one draw needn't show every extreme that they name: In each window, from 25 to 256 positions are masked; the share differs from window to window.
All inputs are finite; a program needn't handle non-finite values.
Results may differ from the reference program's by a relative error of at most 0.02.
Values may be sent and summed in bfloat16 or wider, within the bound.
No kernel may reach another device: no remote copies, remote signals or barrier semaphores. Data moves between devices by JAX's collectives and lax.ppermute only.
A program may use at most 256 MiB of HBM per device.

```python
import jax
import jax.numpy as jnp
from jax import lax

D = 512
FF = 512
KW = 9
L = 512
DILATION_FIRST = 2
DILATION_SECOND = 32
LAYERS = 2
CLASSES = 6
SPECIES = 8
WINDOWS = 128


def draw_masked(key, part):
    count_key = jax.random.fold_in(key, 11)
    order_key = jax.random.fold_in(key, 12)
    levels = jax.random.randint(count_key, (WINDOWS,), 0, 64)
    fewest = L // 20
    most_marked = L // 2
    counts = fewest + (most_marked - fewest) * levels * levels * levels // 262144
    window_ids = jnp.arange(WINDOWS, dtype=jnp.int32)
    counts = jnp.where(window_ids == 0, most_marked, counts)
    position_rank = jax.vmap(lambda sub_key: jax.random.permutation(sub_key, L))(jax.random.split(order_key, WINDOWS))
    return (position_rank.astype(jnp.int32) < counts[:, None]).astype(jnp.int32)


def set_ends(drawn, key, low, top_value):
    spot = [jax.random.randint(jax.random.fold_in(key, axis), (), 0, length) for axis, length in enumerate(drawn.shape)]
    widest = drawn.shape.index(max(drawn.shape))
    beside = spot[:widest] + [(spot[widest] + 1) % drawn.shape[widest]] + spot[widest + 1:]
    return drawn.at[tuple(spot)].set(low).at[tuple(beside)].set(top_value)


def block_levels(key, dims, pieces, smallest, high):
    level, own = 1.0, jax.random.fold_in(key, 6)
    for axis_at, shards_of in pieces:
        steps = jnp.exp(jax.random.uniform(jax.random.fold_in(own, axis_at), (shards_of,), jnp.float32, smallest / len(pieces), high / len(pieces)))
        level = level * jnp.repeat(steps, dims[axis_at] // shards_of).reshape([-1 if axis == axis_at else 1 for axis in range(len(dims))])
    return level


def scatter_about(own_key, extent, width, bound, cuts=(), kind=jnp.bfloat16):
    values = width * jax.random.normal(own_key, extent, jnp.float32)
    if cuts:
        values = values * block_levels(own_key, extent, cuts, -0.22, 0.18)
    return jnp.clip(values, -bound, bound).astype(kind)


def setup_inputs(seed: int = 0) -> dict:
    key_of = jax.random.split(jax.random.key(seed), 14)
    x_in = scatter_about(key_of[0], (WINDOWS, D, L), 1.0, 6.0, ((0, 16), (1, 2)))
    conv_w = scatter_about(key_of[1], (LAYERS, D, KW, D), (KW * D) ** -0.5, 0.09375, ((1, 2),))
    conv_b = scatter_about(key_of[2], (LAYERS, D), 0.5, 3.0, ((1, 2),))
    ln_gain = jnp.clip(1.0 + 0.18 * jax.random.normal(key_of[3], (LAYERS, 2, D), jnp.float32), 0.099609375, 1.8984375).astype(jnp.bfloat16)
    ln_bias = scatter_about(key_of[4], (LAYERS, 2, D), 0.3, 2.0, ((2, 2),))
    up_w = scatter_about(key_of[5], (LAYERS, D, FF), D ** -0.5, 0.25, ((2, 2),))
    up_b = scatter_about(key_of[6], (LAYERS, FF), 0.5, 3.0, ((1, 2),))
    down_w = scatter_about(key_of[7], (LAYERS, FF, D), FF ** -0.5, 0.25, ((1, 2),))
    down_b = scatter_about(key_of[8], (LAYERS, D), 0.5, 3.0, ((1, 2),))
    readout = scatter_about(key_of[9], (D, CLASSES), D ** -0.5, 0.25, ((0, 2),))
    cotangent = scatter_about(key_of[10], (WINDOWS, D, L), 1.0, 6.0, ((0, 16), (1, 2)))
    masked = draw_masked(jax.random.fold_in(key_of[13], 71), 0)
    species = set_ends(jax.random.randint(key_of[12], (WINDOWS,), 0, SPECIES), jax.random.fold_in(key_of[12], 1), 0, SPECIES - 1).astype(jnp.int32)
    return {"x_in": x_in, "conv_w": conv_w, "conv_b": conv_b, "ln_gain": ln_gain, "ln_bias": ln_bias, "up_w": up_w, "up_b": up_b, "down_w": down_w, "down_b": down_b, "readout": readout, "cotangent": cotangent, "masked": masked, "species": species}


EPS = 1e-05
HIGH = lax.Precision.HIGHEST

@jax.custom_vjp
def low(v):
    return lax.optimization_barrier(v.astype(jnp.bfloat16)).astype(jnp.float32)

@jax.custom_vjp
def low_back(v):
    return v

def low_keep(v):
    return (low(v), None)

def low_pass(kept, grad):
    return (grad,)

def back_keep(v):
    return (v, None)

def back_low(kept, grad):
    return (low(grad),)
low.defvjp(low_keep, low_pass)
low_back.defvjp(back_keep, back_low)

def convolution_whole(inputs, weight, dilation):
    length = inputs.shape[1]
    half = weight.shape[1] // 2
    padded = jnp.pad(inputs, ((0, 0), (half * dilation, half * dilation), (0, 0)))
    summed = jnp.zeros(inputs.shape[:2] + (weight.shape[2],), jnp.float32)
    for offset_tap in range(weight.shape[1]):
        window_part = padded[:, offset_tap * dilation:offset_tap * dilation + length]
        summed = summed + jnp.einsum('wld,de->wle', window_part, weight[:, offset_tap], precision=HIGH)
    return summed

def norm_rows(tensor):
    row_mean = lax.optimization_barrier(jnp.mean(tensor, axis=-1, keepdims=True))
    row_var = lax.optimization_barrier(jnp.mean(tensor * tensor, axis=-1, keepdims=True)) - row_mean * row_mean
    return (tensor - row_mean) * lax.rsqrt(row_var + EPS)

def block_layer(hidden, weights, dilation):
    conv_w, conv_b, gains, biases, up_w, up_b, down_w, down_b = weights
    conv_in_out = jnp.transpose(conv_w, (2, 1, 0))
    act_low = low(hidden)
    conv_out = low_back(convolution_whole(act_low, conv_in_out, dilation)) + conv_b
    middle = hidden + norm_rows(jax.nn.gelu(conv_out, approximate=False)) * gains[0] + biases[0]
    mid_low = low(middle)
    up_out = low_back(jnp.einsum('wld,df->wlf', mid_low, up_w, precision=HIGH)) + up_b
    inner_act = low(jax.nn.gelu(up_out, approximate=False))
    down_out = low_back(jnp.einsum('wlf,fe->wle', inner_act, down_w, precision=HIGH)) + down_b
    return middle + norm_rows(jax.nn.gelu(down_out, approximate=False)) * gains[1] + biases[1]

def forward(params, inputs):
    first_layer_rows = jnp.swapaxes(inputs, 1, 2)
    groups = first_layer_rows.reshape((first_layer_rows.shape[0] // 8, 8) + first_layer_rows.shape[1:])
    dilation_list = (DILATION_FIRST, DILATION_SECOND)

    def run_group(group):
        hidden = group
        for block_index in range(LAYERS):
            weights = tuple((member[block_index] for member in params))
            hidden = block_layer(hidden, weights, dilation_list[block_index])
        return hidden
    result = lax.map(jax.checkpoint(run_group), groups).reshape(first_layer_rows.shape)
    return jnp.swapaxes(result, 1, 2)

def reference(x_in, conv_w, conv_b, ln_gain, ln_bias, up_w, up_b, down_w, down_b, readout, cotangent, masked, species):
    params = tuple((member.astype(jnp.float32) for member in (conv_w, conv_b, ln_gain, ln_bias, up_w, up_b, down_w, down_b)))
    inputs = x_in.astype(jnp.float32)
    result, pullback = jax.vjp(forward, params, inputs)
    grad_params, grad_inputs = pullback(cotangent.astype(jnp.float32))
    out_low = result.astype(jnp.bfloat16)
    logits = jnp.einsum('wdl,dj->wlj', out_low.astype(jnp.float32), readout.astype(jnp.float32), precision=HIGH)
    chances = jax.nn.softmax(logits, axis=-1)
    per_window = lax.optimization_barrier(jnp.sum(chances * masked[..., None].astype(jnp.float32), axis=1))
    one_hot_bases = (species[None, :] == jnp.arange(SPECIES, dtype=jnp.int32)[:, None]).astype(jnp.float32)
    species_sum = jnp.dot(one_hot_bases, per_window, precision=HIGH) / L
    return (out_low, grad_inputs, grad_params[0], grad_params[1], grad_params[2], grad_params[3], grad_params[4], grad_params[5], grad_params[6], grad_params[7], species_sum)
```

```python
import functools

import jax
import jax.numpy as jnp
from jax import lax
from jax.experimental import pallas as pl
from jax.experimental.pallas import tpu as pltpu
from jax.sharding import Mesh
from jax.sharding import PartitionSpec as P

DILATIONS = (2, 32)
SPECIES = 8
EPS = 1e-05
BF = jnp.bfloat16
F32 = jnp.float32
DP = ("z", "y", "core")
STEP = 16
VMEM_BYTES = 58 * 2**20
CONV_B, GAIN_A, BIAS_A, UP_B, DOWN_B, GAIN_B, BIAS_B = range(7)
COLUMNS = 8


def shifted(rows, by):
    if by == 0:
        return rows
    blank = jnp.zeros((rows.shape[0], abs(by)), rows.dtype)
    if by > 0:
        return jnp.concatenate([rows[:, by:], blank], axis=1)
    return jnp.concatenate([blank, rows[:, :by]], axis=1)


def fold(tile):
    return sum(tile[at : at + 8] for at in range(0, tile.shape[0], 8))


def fold_lanes(tile):
    return sum(tile[:, at : at + 128] for at in range(0, tile.shape[1], 128))


def gelu_pair(x):
    cdf = 0.5 + 0.5 * lax.erf(x * 0.7071067811865476)
    return x * cdf, cdf + x * jnp.exp(-0.5 * x * x) * 0.3989422804014327


def nn(left, right):
    return jnp.dot(left, right, preferred_element_type=F32)


def tn(left, right):
    return lax.dot_general(left, right, (((0,), (0,)), ((), ())), preferred_element_type=F32)


def nt(left, right):
    return lax.dot_general(left, right, (((1,), (1,)), ((), ())), preferred_element_type=F32)


def steps(size):
    return [slice(at, at + STEP) for at in range(0, size, STEP)]


def place(pieces, me, target):
    ways = len(pieces)
    for back, piece in enumerate(pieces):
        size = piece.shape[1]
        spot = lax.rem(me + (ways - back), ways) * size
        target[pl.ds(pl.multiple_of(spot, size), size), :] = piece[0]


def norm_stats(total, square, width):
    mean = jnp.sum(total, axis=0, keepdims=True) / width
    var = jnp.sum(square, axis=0, keepdims=True) / width - mean * mean
    return mean, lax.rsqrt(var + EPS)


def activate_and_sum(pre, col, pc, slope_ref):
    size, length = pre.shape
    total = jnp.zeros((8, length), F32)
    square = jnp.zeros((8, length), F32)
    for rows in steps(size):
        value, slope = gelu_pair(pre[rows, :] + pc[rows, col : col + 1])
        pre[rows, :] = value
        slope_ref[0, rows, :] = slope.astype(BF)
        total = total + fold(value)
        square = square + fold(value * value)
    return norm_stats(total, square, size)


def forward_kernel(layer, n_in, n_out, taps, *refs):
    me_ref, w, pc = refs[:3]
    pieces = refs[3 : 3 + n_in]
    at = 3 + n_in
    reads = None
    if n_out:
        reads = refs[at : at + 2]
        at += 2
    outs = refs[at : at + 8]
    at += 8
    a_ref, b_ref, n1_ref, s1_ref, su_ref, v_ref, s2_ref, n2_ref = outs
    extra = refs[at : at + n_out + (1 if n_out else 0)]
    at += len(extra)
    act, wide, pre, mid = refs[at:]
    me = me_ref[0]
    size, length = act.shape
    base = layer * COLUMNS
    half = taps // 2
    place(pieces, me, act)
    a_ref[0] = act[...]
    for tap in range(taps):
        wide[tap] = shifted(act[...], (tap - half) * DILATIONS[layer])
    total = nn(w[0], wide[0])
    for tap in range(1, taps):
        total = total + nn(w[tap], wide[tap])
    pre[...] = total
    mean, inv = activate_and_sum(pre, base + CONV_B, pc, s1_ref)
    for rows in steps(size):
        normed = (pre[rows, :] - mean) * inv
        m = (
            act[rows, :].astype(F32)
            + normed * pc[rows, base + GAIN_A : base + GAIN_A + 1]
            + pc[rows, base + BIAS_A : base + BIAS_A + 1]
        )
        n1_ref[0, rows, :] = normed.astype(BF)
        s1_ref[0, rows, :] = (s1_ref[0, rows, :].astype(F32) * inv).astype(BF)
        mid[rows, :] = m
        b_ref[0, rows, :] = m.astype(BF)
    pre[...] = nn(w[taps], b_ref[0])
    for rows in steps(size):
        value, slope = gelu_pair(pre[rows, :] + pc[rows, base + UP_B : base + UP_B + 1])
        v_ref[0, rows, :] = value.astype(BF)
        su_ref[0, rows, :] = slope.astype(BF)
    pre[...] = tn(w[taps + 1], v_ref[0])
    mean, inv = activate_and_sum(pre, base + DOWN_B, pc, s2_ref)
    for rows in steps(size):
        normed = (pre[rows, :] - mean) * inv
        out = (
            mid[rows, :]
            + normed * pc[rows, base + GAIN_B : base + GAIN_B + 1]
            + pc[rows, base + BIAS_B : base + BIAS_B + 1]
        )
        n2_ref[0, rows, :] = normed.astype(BF)
        s2_ref[0, rows, :] = (s2_ref[0, rows, :].astype(F32) * inv).astype(BF)
        act[rows, :] = out.astype(BF)
    if not n_out:
        return
    readout, mask_ref = reads
    chance_ref = extra[n_out]
    part = size // n_out
    for ahead in range(n_out):
        spot = lax.rem(me + ahead, n_out) * part
        extra[ahead][0] = act[pl.ds(pl.multiple_of(spot, part), part), :]
    logits = nn(readout[...], act[...])
    seat = lax.broadcasted_iota(jnp.int32, logits.shape, 0)
    logits = jnp.where(seat < 6, logits, -1e30)
    raised = jnp.exp(logits - jnp.max(logits, axis=0, keepdims=True))
    chance = raised / jnp.sum(raised, axis=0, keepdims=True)
    chance_ref[0] = fold_lanes(chance * mask_ref[0].astype(F32))


def first_kernel(layer, n_in, taps, *refs):
    n_args = 3 + n_in
    outs = refs[n_args : n_args + 9]
    rest = refs[n_args + 9 :]
    forward_kernel(layer, n_in, 0, taps, *refs[:n_args], *outs[:8], *rest)
    outs[8][0] = rest[0][...]


def chain(layer, taps, first, last, grad, kept, w, pc, outs, work):
    b_ref, n1_ref, s1_ref, su_ref, v_ref, s2_ref, n2_ref = kept
    dc_ref, dm_ref, ff_ref, small_ref = outs
    pre, low, ff_sum, row_sums = work
    size, length = pre.shape
    base = layer * COLUMNS

    @pl.when(first)
    def _():
        ff_sum[...] = jnp.zeros_like(ff_sum)
        row_sums[...] = jnp.zeros_like(row_sums)

    def gather_q(gain_col, normed_ref, gain_slot, bias_slot):
        total = jnp.zeros((8, length), F32)
        cross = jnp.zeros((8, length), F32)
        for rows in steps(size):
            g = grad[rows, :]
            normed = normed_ref[0, rows, :].astype(F32)
            product = g * normed
            row_sums[gain_slot, rows, :] += fold_lanes(product)
            row_sums[bias_slot, rows, :] += fold_lanes(g)
            gain = pc[rows, gain_col : gain_col + 1]
            total = total + fold(g * gain)
            cross = cross + fold(product * gain)
        return (
            jnp.sum(total, axis=0, keepdims=True) / size,
            jnp.sum(cross, axis=0, keepdims=True) / size,
        )

    def back(gain_col, normed_ref, slope_ref, bias_slot, target):
        mean_q, mean_qn = gather_q(gain_col, normed_ref, bias_slot + 1, bias_slot + 2)
        for rows in steps(size):
            q = grad[rows, :] * pc[rows, gain_col : gain_col + 1]
            normed = normed_ref[0, rows, :].astype(F32)
            d = slope_ref[0, rows, :].astype(F32) * (q - mean_q - normed * mean_qn)
            row_sums[bias_slot, rows, :] += fold_lanes(d)
            target(rows, d.astype(BF))

    def put_low(rows, value):
        low[rows, :] = value

    def put_dc(rows, value):
        dc_ref[0, rows, :] = value

    back(base + GAIN_B, n2_ref, s2_ref, DOWN_B, put_low)
    pre[...] = nn(w[taps + 1], low[...])
    ff_sum[1] += nt(v_ref[0], low[...])
    for rows in steps(size):
        du = pre[rows, :] * su_ref[0, rows, :].astype(F32)
        row_sums[UP_B, rows, :] += fold_lanes(du)
        low[rows, :] = du.astype(BF)
    pre[...] = tn(w[taps], low[...])
    ff_sum[0] += nt(low[...], b_ref[0])
    for rows in steps(size):
        dm = grad[rows, :] + pre[rows, :]
        grad[rows, :] = dm
        dm_ref[0, rows, :] = dm.astype(BF)
    back(base + GAIN_A, n1_ref, s1_ref, CONV_B, put_dc)

    @pl.when(last)
    def _():
        ff_ref[...] = ff_sum[...].astype(BF)
        for rows in steps(size):
            seat = lax.broadcasted_iota(jnp.int32, (STEP, 128), 1)
            table = jnp.zeros((STEP, 128), F32)
            for slot in range(7):
                column = jnp.sum(row_sums[slot, rows, :], axis=1, keepdims=True)
                table = jnp.where(seat == slot, column, table)
            small_ref[rows, :] = table


def conv_back(layer, taps, dc, dm_ref, w, wide, grad):
    half = taps // 2
    for tap in range(taps):
        wide[tap] = shifted(dc, -(tap - half) * DILATIONS[layer])
    total = tn(w[0], wide[0])
    for tap in range(1, taps):
        total = total + tn(w[tap], wide[tap])
    grad[...] = total
    for rows in steps(grad.shape[0]):
        grad[rows, :] = grad[rows, :] + dm_ref[0, rows, :].astype(F32)


def top_kernel(layer, n_in, taps, *refs):
    me_ref, w, pc = refs[:3]
    pieces = refs[3 : 3 + n_in]
    kept = refs[3 + n_in : 10 + n_in]
    outs = refs[10 + n_in : 14 + n_in]
    grad, *work = refs[14 + n_in :]
    me = me_ref[0]
    ways = n_in
    for back, piece in enumerate(pieces):
        part = piece.shape[1]
        spot = pl.multiple_of(lax.rem(me + (ways - back), ways) * part, part)
        grad[pl.ds(spot, part), :] = piece[0].astype(F32)
    here = pl.program_id(0)
    chain(layer, taps, here == 0, here == pl.num_programs(0) - 1, grad, kept, w, pc, outs, work)


def middle_kernel(layer, taps, *refs):
    above_w, w, pc, dc_in, dm_in = refs[:5]
    kept = refs[5:12]
    outs = refs[12:16]
    grad, wide, *work = refs[16:]
    conv_back(layer + 1, taps, dc_in[0], dm_in, above_w, wide, grad)
    here = pl.program_id(0)
    chain(layer, taps, here == 0, here == pl.num_programs(0) - 1, grad, kept, w, pc, outs, work)


def bottom_kernel(layer, taps, n_out, *refs):
    me_ref, w, dc_in, dm_in = refs[:4]
    own_ref = refs[4]
    others = refs[5 : 4 + n_out]
    grad, wide = refs[4 + n_out :]
    conv_back(layer, taps, dc_in[0], dm_in, w, wide, grad)
    me = me_ref[0]
    part = own_ref.shape[1]
    own_ref[0] = grad[pl.ds(pl.multiple_of(me * part, part), part), :]
    for ahead, ref in enumerate(others, start=1):
        spot = pl.multiple_of(lax.rem(me + ahead, n_out) * part, part)
        ref[0] = grad[pl.ds(spot, part), :].astype(BF)


def weight_kernel(layer, taps, first_tap, dc, a, out):
    half = taps // 2
    for at in range(out.shape[0]):
        by = -(first_tap + at - half) * DILATIONS[layer]
        total = None
        for window in range(dc.shape[0]):
            part = nt(shifted(dc[window], by), a[window])
            total = part if total is None else total + part
        out[at] = total.astype(BF)


def whole_spec(shape):
    return pl.BlockSpec(
        shape, lambda *_: (0,) * len(shape), pipeline_mode=pl.Buffered(buffer_count=1)
    )


def window_spec(shape):
    return pl.BlockSpec((1,) + shape[1:], lambda i: (i,) + (0,) * (len(shape) - 1))


def smem_spec():
    return pl.BlockSpec(memory_space=pltpu.SMEM)


def params():
    return pltpu.CompilerParams(vmem_limit_bytes=VMEM_BYTES)


def cost(flops, nbytes):
    return pl.CostEstimate(flops=int(flops), bytes_accessed=int(nbytes), transcendentals=0)


def struct(shape, dtype):
    return jax.ShapeDtypeStruct(shape, dtype)


def rotate(value, axis, ways, by):
    return lax.ppermute(value, axis, [(i, (i + by) % ways) for i in range(ways)])


def pick(value, index, dim):
    return lax.dynamic_index_in_dim(value, index, dim, keepdims=False)


def reduce_stage(value, axis, ways, dim):
    me = lax.axis_index(axis)
    total = pick(value, me, dim).astype(F32)
    for by in range(1, ways):
        got = rotate(pick(value, lax.rem(me + by, ways), dim), axis, ways, by)
        total = total + got.astype(F32)
    return total.astype(BF)


def arrange(pieces, axis, dim):
    me = lax.axis_index(axis)
    ways = len(pieces)
    if ways == 2:
        low = jnp.where(me == 0, pieces[0], pieces[1])
        high = jnp.where(me == 0, pieces[1], pieces[0])
        return jnp.stack([low, high], axis=dim)
    shape = list(pieces[0].shape)
    shape.insert(dim, ways)
    out = jnp.zeros(shape, pieces[0].dtype)
    for back, piece in enumerate(pieces):
        spot = lax.rem(me + (ways - back), ways)
        out = lax.dynamic_update_index_in_dim(out, piece, spot, dim)
    return out


def gather_stage(value, axis, ways, dim):
    pieces = [value] + [rotate(value, axis, ways, by) for by in range(1, ways)]
    return arrange(pieces, axis, dim)


def body(sizes, *args):
    (
        x_in,
        conv_w,
        conv_b,
        ln_gain,
        ln_bias,
        up_w,
        up_b,
        down_w,
        down_b,
        readout,
        cotangent,
        masked,
        species,
    ) = args
    n_z, n_y, n_core, n_tp = sizes
    layers, part, taps, size = conv_w.shape
    windows, _, length = x_in.shape
    mine = windows // n_tp
    planes = taps + 2
    me = lax.axis_index("tp")
    me_arr = jnp.full((1,), me, jnp.int32)
    row = part // (n_core * n_y * n_z)

    packs = []
    for layer in range(layers):
        packs.append(
            jnp.concatenate(
                [
                    jnp.transpose(conv_w[layer], (1, 0, 2)),
                    jnp.transpose(up_w[layer])[None],
                    down_w[layer][None],
                ]
            )
        )

    def full_weights(pack):
        cut = pack.reshape(planes, n_core, n_y, n_z, row, size)
        own = pick(
            pick(pick(cut, lax.axis_index("core"), 1), lax.axis_index("y"), 1),
            lax.axis_index("z"),
            1,
        )
        blocks = [pack]
        for by in range(1, n_tp):
            got = rotate(own, "tp", n_tp, by)
            got = gather_stage(got, "z", n_z, 1)
            got = gather_stage(got, "y", n_y, 1)
            got = gather_stage(got, "core", n_core, 1)
            blocks.append(got.reshape(planes, part, size))
        return arrange(blocks, "tp", 1).reshape(planes, size, size)

    def to_windows(value):
        cut = value.reshape(n_tp, mine, part, length)
        pieces = [pick(cut, me, 0)]
        for by in range(1, n_tp):
            pieces.append(rotate(pick(cut, lax.rem(me + by, n_tp), 0), "tp", n_tp, by))
        return pieces

    columns = []
    for layer in range(layers):
        columns += [
            conv_b[layer],
            ln_gain[layer, 0],
            ln_bias[layer, 0],
            up_b[layer],
            down_b[layer],
            ln_gain[layer, 1],
            ln_bias[layer, 1],
            jnp.zeros((part,), BF),
        ]
    table = jnp.concatenate([jnp.stack(columns), jnp.transpose(readout)])
    table = jnp.pad(table, ((0, 2), (0, 0)))
    table = gather_stage(table, "tp", n_tp, 1).reshape(table.shape[0], size)
    pc = jnp.transpose(table[: layers * COLUMNS]).astype(F32)
    read_rows = table[layers * COLUMNS :]

    x_pieces = to_windows(x_in)
    w_full = [full_weights(packs[0])]
    cot_pieces = to_windows(cotangent)
    w_full.append(full_weights(packs[1]))

    window = (mine, size, length)
    piece_shape = (mine, part, length)
    kept_struct = [struct(window, BF)] * 8
    fwd_scratch = [
        pltpu.VMEM((size, length), BF),
        pltpu.VMEM((taps, size, length), BF),
        pltpu.VMEM((size, length), F32),
        pltpu.VMEM((size, length), F32),
    ]
    conv_flops = 2.0 * taps * size * size * length * mine
    ff_flops = 4.0 * size * size * length * mine
    first = pl.pallas_call(
        functools.partial(first_kernel, 0, n_tp, taps),
        grid=(mine,),
        in_specs=[smem_spec(), whole_spec((planes, size, size)), whole_spec(pc.shape)]
        + [window_spec(piece_shape)] * n_tp,
        out_specs=[window_spec(window)] * 9,
        out_shape=kept_struct + [struct(window, BF)],
        scratch_shapes=fwd_scratch,
        compiler_params=params(),
        cost_estimate=cost(conv_flops + ff_flops, 20e6),
        name="forward_first",
    )(me_arr, w_full[0], pc, *x_pieces)
    kept0, hidden = first[:8], first[8]

    mask_rows = lax.dynamic_slice_in_dim(masked, me * mine, mine, 0).reshape(mine, 1, length)
    second = pl.pallas_call(
        functools.partial(forward_kernel, 1, 1, n_tp, taps),
        grid=(mine,),
        in_specs=[smem_spec(), whole_spec((planes, size, size)), whole_spec(pc.shape)]
        + [window_spec(window), whole_spec(read_rows.shape), window_spec((mine, 1, length))],
        out_specs=[window_spec(window)] * 8
        + [window_spec(piece_shape)] * n_tp
        + [window_spec((mine, 8, 128))],
        out_shape=kept_struct + [struct(piece_shape, BF)] * n_tp + [struct((mine, 8, 128), F32)],
        scratch_shapes=fwd_scratch,
        compiler_params=params(),
        cost_estimate=cost(conv_flops + ff_flops, 20e6),
        name="forward_second",
    )(me_arr, w_full[1], pc, hidden, read_rows, mask_rows)
    kept1, y_pieces, chance = second[:8], second[8 : 8 + n_tp], second[8 + n_tp]

    y_back = [y_pieces[0]] + [rotate(y_pieces[by], "tp", n_tp, by) for by in range(1, n_tp)]
    y_out = arrange(y_back, "tp", 0).reshape(windows, part, length)

    per_window = jnp.sum(chance, axis=2)[:, :6]
    my_species = lax.dynamic_slice_in_dim(species, me * mine, mine, 0)
    hot = (my_species[None, :] == jnp.arange(SPECIES, dtype=jnp.int32)[:, None]).astype(F32)
    species_part = jnp.dot(hot, per_window, precision=lax.Precision.HIGHEST) / length

    chain_out_specs = [
        window_spec(window),
        window_spec(window),
        whole_spec((2, size, size)),
        whole_spec((size, 128)),
    ]
    chain_out = [
        struct(window, BF),
        struct(window, BF),
        struct((2, size, size), BF),
        struct((size, 128), F32),
    ]
    chain_scratch = [
        pltpu.VMEM((size, length), F32),
        pltpu.VMEM((size, length), BF),
        pltpu.VMEM((2, size, size), F32),
        pltpu.VMEM((7, size, 128), F32),
    ]
    grad_scratch = pltpu.VMEM((size, length), F32)
    wide_scratch = pltpu.VMEM((taps, size, length), BF)
    dc1, dm1, ff1, small1 = pl.pallas_call(
        functools.partial(top_kernel, 1, n_tp, taps),
        grid=(mine,),
        in_specs=[smem_spec(), whole_spec((planes, size, size)), whole_spec(pc.shape)]
        + [window_spec(piece_shape)] * n_tp
        + [window_spec(window)] * 7,
        out_specs=chain_out_specs,
        out_shape=chain_out,
        scratch_shapes=[grad_scratch] + chain_scratch,
        compiler_params=params(),
        cost_estimate=cost(2 * ff_flops, 20e6),
        name="chain_second",
    )(me_arr, w_full[1], pc, *cot_pieces, *kept1[1:])

    def conv_weight_grad(layer, dc, a):
        return pl.pallas_call(
            functools.partial(weight_kernel, layer, taps, 0),
            in_specs=[pl.BlockSpec(memory_space=pltpu.VMEM)] * 2,
            out_specs=pl.BlockSpec(memory_space=pltpu.VMEM),
            out_shape=struct((taps, size, size), BF),
            compiler_params=params(),
            cost_estimate=cost(conv_flops, 10e6),
            name=("weights_first", "weights_second")[layer],
        )(dc, a)

    conv1 = conv_weight_grad(1, dc1, kept1[0])

    dc0, dm0, ff0, small0 = pl.pallas_call(
        functools.partial(middle_kernel, 0, taps),
        grid=(mine,),
        in_specs=[whole_spec((planes, size, size))] * 2
        + [whole_spec(pc.shape)]
        + [window_spec(window)] * 9,
        out_specs=chain_out_specs,
        out_shape=chain_out,
        scratch_shapes=[grad_scratch, wide_scratch] + chain_scratch,
        compiler_params=params(),
        cost_estimate=cost(conv_flops + 2 * ff_flops, 20e6),
        name="chain_first",
    )(w_full[1], w_full[0], pc, dc1, dm1, *kept0[1:])

    x_grads = pl.pallas_call(
        functools.partial(bottom_kernel, 0, taps, n_tp),
        grid=(mine,),
        in_specs=[smem_spec(), whole_spec((planes, size, size))] + [window_spec(window)] * 2,
        out_specs=[window_spec(piece_shape)] * n_tp,
        out_shape=[struct(piece_shape, F32)] + [struct(piece_shape, BF)] * (n_tp - 1),
        scratch_shapes=[grad_scratch, wide_scratch],
        compiler_params=params(),
        cost_estimate=cost(conv_flops, 15e6),
        name="input_grad",
    )(me_arr, w_full[0], dc0, dm0)
    x_back = [x_grads[0]] + [
        rotate(x_grads[by], "tp", n_tp, by).astype(F32) for by in range(1, n_tp)
    ]
    grad_x = arrange(x_back, "tp", 0).reshape(windows, part, length)

    conv0 = conv_weight_grad(0, dc0, kept0[0])

    def total(value):
        count, _, width = value.shape
        value = value.reshape(count, n_tp, n_core, n_y, n_z, row, width)
        value = reduce_stage(value, "core", n_core, 2)
        value = reduce_stage(value, "tp", n_tp, 1)
        value = reduce_stage(value, "y", n_y, 1)
        value = reduce_stage(value, "z", n_z, 1)
        value = gather_stage(value, "z", n_z, 1)
        value = gather_stage(value, "y", n_y, 1)
        value = gather_stage(value, "core", n_core, 1)
        return value.reshape(count, part, width)

    spread = jnp.pad(species_part.reshape(1, SPECIES * 6, 1), ((0, 0), (0, part - SPECIES * 6), (0, 0)))
    spread = jnp.broadcast_to(spread, (n_tp, part, 1)).reshape(size, 1)
    small1 = jnp.where(jnp.arange(128)[None, :] == 7, spread, small1)
    conv1_sum, ff1_sum, small1_sum = total(conv1), total(ff1), total(small1.astype(BF)[None])
    ff0_sum, small0_sum, conv0_sum = total(ff0), total(small0.astype(BF)[None]), total(conv0)

    grad_conv_w = jnp.transpose(jnp.stack([conv0_sum, conv1_sum]), (0, 2, 1, 3)).astype(F32)
    grad_up_w = jnp.stack([jnp.transpose(ff0_sum[0]), jnp.transpose(ff1_sum[0])]).astype(F32)
    grad_down_w = jnp.stack([ff0_sum[1], ff1_sum[1]]).astype(F32)
    smalls = jnp.transpose(jnp.concatenate([small0_sum, small1_sum]), (0, 2, 1)).astype(F32)
    species_sum = smalls[1, 7, : SPECIES * 6].reshape(SPECIES, 6)
    return (
        y_out,
        grad_x,
        grad_conv_w,
        smalls[:, CONV_B],
        jnp.stack([smalls[:, GAIN_A], smalls[:, GAIN_B]], axis=1),
        jnp.stack([smalls[:, BIAS_A], smalls[:, BIAS_B]], axis=1),
        grad_up_w,
        smalls[:, UP_B],
        grad_down_w,
        smalls[:, DOWN_B],
        species_sum,
    )


def solution(mesh):
    dp, tp = mesh.shape["dp"], mesh.shape["tp"]
    n_core = n_y = 2
    n_z = dp // (n_core * n_y)
    fine = Mesh(mesh.devices.reshape(n_z, n_y, n_core, tp), DP + ("tp",))
    placed = (
        P(DP, "tp", None),
        P(None, "tp", None, None),
        P(None, "tp"),
        P(None, None, "tp"),
        P(None, None, "tp"),
        P(None, None, "tp"),
        P(None, "tp"),
        P(None, "tp", None),
        P(None, "tp"),
        P("tp", None),
        P(DP, "tp", None),
        P(DP, None),
        P(DP),
    )
    return jax.shard_map(
        functools.partial(body, (n_z, n_y, n_core, tp)),
        mesh=fine,
        in_specs=placed,
        out_specs=(
            P(DP, "tp", None),
            P(DP, "tp", None),
            P(None, "tp", None, None),
            P(None, "tp"),
            P(None, None, "tp"),
            P(None, None, "tp"),
            P(None, None, "tp"),
            P(None, "tp"),
            P(None, "tp", None),
            P(None, "tp"),
            P(),
        ),
        check_vma=False,
    )
```

```python
import functools

import jax
import jax.numpy as jnp
from jax import lax
from jax.experimental import pallas as pl
from jax.experimental.pallas import tpu as pltpu
from jax.sharding import Mesh
from jax.sharding import PartitionSpec as P

DILATIONS = (2, 32)
SPECIES = 8
EPS = 1e-05
BF = jnp.bfloat16
F32 = jnp.float32
DP = ("z", "y", "core")
STEP = 32
HALVES = 2
VMEM_BYTES = 58 * 2**20
CONV_B, GAIN_A, BIAS_A, UP_B, DOWN_B, GAIN_B, BIAS_B = range(7)
COLUMNS = 8


def shifted(rows, by):
    if by == 0:
        return rows
    blank = jnp.zeros((rows.shape[0], abs(by)), rows.dtype)
    if by > 0:
        return jnp.concatenate([rows[:, by:], blank], axis=1)
    return jnp.concatenate([blank, rows[:, :by]], axis=1)


def fold(tile):
    return sum(tile[at : at + 8] for at in range(0, tile.shape[0], 8))


def fold_lanes(tile):
    return sum(tile[:, at : at + 128] for at in range(0, tile.shape[1], 128))


def gelu_pair(x):
    cdf = 0.5 + 0.5 * lax.erf(x * 0.7071067811865476)
    return x * cdf, cdf + x * jnp.exp(-0.5 * x * x) * 0.3989422804014327


def nn(left, right):
    return jnp.dot(left, right, preferred_element_type=F32)


def tn(left, right):
    return lax.dot_general(left, right, (((0,), (0,)), ((), ())), preferred_element_type=F32)


def nt(left, right):
    return lax.dot_general(left, right, (((1,), (1,)), ((), ())), preferred_element_type=F32)


def steps(size):
    return [slice(at, at + STEP) for at in range(0, size, STEP)]


def place(pieces, me, target):
    ways = len(pieces)
    for back, piece in enumerate(pieces):
        size = piece.shape[1]
        spot = lax.rem(me + (ways - back), ways) * size
        target[pl.ds(pl.multiple_of(spot, size), size), :] = piece[0]


def norm_stats(total, square, width):
    mean = jnp.sum(total, axis=0, keepdims=True) / width
    var = jnp.sum(square, axis=0, keepdims=True) / width - mean * mean
    return mean, lax.rsqrt(var + EPS)


def activate_and_sum(pre, col, pc, slope_ref, span):
    size, length = pre.shape
    total = jnp.zeros((8, length), F32)
    square = jnp.zeros((8, length), F32)
    for rows in steps(size):
        value, slope = gelu_pair(pre[rows, :] + pc[rows, col : col + 1])
        pre[rows, :] = value
        slope_ref[0, rows, span] = slope.astype(BF)
        total = total + fold(value)
        square = square + fold(value * value)
    return norm_stats(total, square, size)


def load_weights(layer, where, blocks, pieces, full, w, sems, out_sem):
    tp, y, core = where[0], where[1], where[2]
    conv, up, down = blocks
    taps, part = conv.shape[1], conv.shape[2]
    ways = w.shape[1] // part
    here = pl.program_id(0)

    def rows(owner, at, count):
        return pl.ds(pl.multiple_of(owner * part + at, count), count)

    @pl.when(here == 0)
    def _():
        own = rows(tp, 0, part)
        copies = [
            (conv.at[layer], w.at[0:taps, own]),
            (up.at[layer], w.at[taps, own]),
            (down.at[layer], w.at[taps + 1, own]),
        ]
        quarter = part // 4
        for back in range(1, ways):
            owner = lax.rem(tp + (ways - back), ways)
            for flip in range(4):
                c = core if flip < 2 else 1 - core
                at = c * (2 * quarter) + (y if flip % 2 == 0 else 1 - y) * quarter
                copies.append((pieces[4 * (back - 1) + flip], w.at[:, rows(owner, at, quarter)]))
        moves = [pltpu.make_async_copy(src, dst, sems.at[i]) for i, (src, dst) in enumerate(copies)]
        for move in moves:
            move.start()
        for move in moves:
            move.wait()
        pltpu.make_async_copy(w, full, out_sem).start()

    @pl.when(here == pl.num_programs(0) - 1)
    def _():
        pltpu.make_async_copy(w, full, out_sem).wait()


def first_early_kernel(layer, n_in, n_pieces, taps, *refs):
    where, pc = refs[:2]
    blocks, parts = refs[2:5], refs[5 : 5 + n_pieces]
    at = 5 + n_pieces
    pieces = refs[at : at + n_in]
    at += n_in
    *kept, out = refs[at : at + 9]
    full = refs[at + 9]
    *work, w, sems, out_sem = refs[at + 10 :]
    load_weights(layer, where, blocks, parts, full, w, sems, out_sem)
    forward_window(layer, taps, where, pc, w, pieces, kept, work)
    out[0] = work[0][...]


def first_late_kernel(layer, n_in, taps, n_before, where, pc, w, *refs):
    pieces, refs = refs[:n_in], refs[n_in + n_before :]
    *kept, out = refs[:9]
    work = refs[9:]
    forward_window(layer, taps, where, pc, w, pieces, kept, work)
    out[0] = work[0][...]


def second_kernel(layer, n_in, n_pieces, taps, *refs):
    where, pc = refs[:2]
    blocks, parts = refs[2:5], refs[5 : 5 + n_pieces]
    at = 5 + n_pieces
    hidden, readout, mask_ref = refs[at : at + 3]
    cots = refs[at + 3 : at + 3 + n_in]
    at += 3 + n_in
    y_refs = refs[at : at + n_in]
    chance_ref = refs[at + n_in]
    outs = refs[at + n_in + 1 : at + n_in + 5]
    full = refs[at + n_in + 5]
    refs = refs[at + n_in + 6 :]
    act, wide, *pairs = refs[: 2 + 2 * HALVES]
    kept = refs[2 + 2 * HALVES : 9 + 2 * HALVES]
    low, high, row_sums, w, sems, out_sem = refs[9 + 2 * HALVES :]
    load_weights(layer, where, blocks, parts, full, w, sems, out_sem)
    here = pl.program_id(0)
    clear(here == 0, outs[2], row_sums)
    forward_window(layer, taps, where, pc, w, (hidden,), (None,) + kept, (act, wide, *pairs))
    me = where[0]
    part = act.shape[0] // n_in
    for ahead, ref in enumerate(y_refs):
        spot = lax.rem(me + ahead, n_in) * part
        ref[0] = act[pl.ds(pl.multiple_of(spot, part), part), :]
    logits = nn(readout[...], act[...])
    seat = lax.broadcasted_iota(jnp.int32, logits.shape, 0)
    logits = jnp.where(seat < 6, logits, -1e30)
    raised = jnp.exp(logits - jnp.max(logits, axis=0, keepdims=True))
    chance = raised / jnp.sum(raised, axis=0, keepdims=True)
    chance_ref[0] = fold_lanes(chance * mask_ref[0].astype(F32))
    grads = pairs[HALVES:]
    for back, piece in enumerate(cots):
        spot = pl.multiple_of(lax.rem(me + (n_in - back), n_in) * part, part)
        for at, grad in enumerate(grads):
            width = grad.shape[1]
            grad[pl.ds(spot, part), :] = piece[0, :, at * width : (at + 1) * width].astype(F32)
    up, down = w.at[pl.ds(taps, 1)], w.at[pl.ds(taps + 1, 1)]
    chain(layer, grads, kept, up, down, pc, outs, (low, high, row_sums, *pairs[:HALVES]))
    close(here == pl.num_programs(0) - 1, row_sums, outs[3])


def forward_window(layer, taps, where, pc, w, pieces, kept, work):
    a_ref, b_ref, n1_ref, s1_ref, su_ref, v_ref, s2_ref, n2_ref = kept
    act, wide, *pairs = work
    size, length = act.shape
    base = layer * COLUMNS
    half = taps // 2
    width = length // HALVES
    spans = [slice(at, at + width) for at in range(0, length, width)]
    pres, mids = pairs[:HALVES], pairs[HALVES:]
    place(pieces, where[0], act)
    if a_ref is not None:
        a_ref[0] = act[...]
    for tap in range(taps):
        wide[tap] = shifted(act[...], (tap - half) * DILATIONS[layer])

    def convolve(pre, span):
        total = nn(w[0], wide[0, :, span])
        for tap in range(1, taps):
            total = total + nn(w[tap], wide[tap, :, span])
        pre[...] = total

    def first_norm(pre, mid, span):
        mean, inv = activate_and_sum(pre, base + CONV_B, pc, s1_ref, span)
        for rows in steps(size):
            normed = (pre[rows, :] - mean) * inv
            m = (
                act[rows, span].astype(F32)
                + normed * pc[rows, base + GAIN_A : base + GAIN_A + 1]
                + pc[rows, base + BIAS_A : base + BIAS_A + 1]
            )
            n1_ref[0, rows, span] = normed.astype(BF)
            s1_ref[0, rows, span] = (s1_ref[0, rows, span].astype(F32) * inv).astype(BF)
            mid[rows, :] = m
            b_ref[0, rows, span] = m.astype(BF)

    def hidden(pre, span):
        for rows in steps(size):
            value, slope = gelu_pair(pre[rows, :] + pc[rows, base + UP_B : base + UP_B + 1])
            v_ref[0, rows, span] = value.astype(BF)
            su_ref[0, rows, span] = slope.astype(BF)

    def second_norm(pre, mid, span):
        mean, inv = activate_and_sum(pre, base + DOWN_B, pc, s2_ref, span)
        for rows in steps(size):
            normed = (pre[rows, :] - mean) * inv
            out = (
                mid[rows, :]
                + normed * pc[rows, base + GAIN_B : base + GAIN_B + 1]
                + pc[rows, base + BIAS_B : base + BIAS_B + 1]
            )
            n2_ref[0, rows, span] = normed.astype(BF)
            s2_ref[0, rows, span] = (s2_ref[0, rows, span].astype(F32) * inv).astype(BF)
            act[rows, span] = out.astype(BF)

    for pre, span in zip(pres, spans):
        convolve(pre, span)
    for pre, mid, span in zip(pres, mids, spans):
        first_norm(pre, mid, span)
        pre[...] = nn(w[taps], b_ref[0, :, span])
        hidden(pre, span)
        pre[...] = tn(w[taps + 1], v_ref[0, :, span])
        second_norm(pre, mid, span)

def clear(first, ff_sum, row_sums):
    @pl.when(first)
    def _():
        ff_sum[...] = jnp.zeros_like(ff_sum)
        row_sums[...] = jnp.zeros_like(row_sums)


def close(last, row_sums, small_ref):
    @pl.when(last)
    def _():
        for rows in steps(small_ref.shape[0]):
            seat = lax.broadcasted_iota(jnp.int32, (STEP, 128), 1)
            table = jnp.zeros((STEP, 128), F32)
            for slot in range(7):
                column = jnp.sum(row_sums[slot, rows, :], axis=1, keepdims=True)
                table = jnp.where(seat == slot, column, table)
            small_ref[rows, :] = table


def chain(layer, grads, kept, up, down, pc, outs, work):
    b_ref, n1_ref, s1_ref, su_ref, v_ref, s2_ref, n2_ref = kept
    dc_ref, dm_ref, ff_sum, _ = outs
    low, high, row_sums, *pres = work
    size, width = pres[0].shape
    base = layer * COLUMNS
    spans = [slice(at, at + width) for at in range(0, low.shape[1], width)]

    def back(grad, span, gain_col, normed_ref, slope_ref, slot, target):
        total = jnp.zeros((8, width), F32)
        cross = jnp.zeros((8, width), F32)
        for rows in steps(size):
            g = grad[rows, :]
            product = g * normed_ref[0, rows, span].astype(F32)
            row_sums[slot + 1, rows, :] += fold_lanes(product)
            row_sums[slot + 2, rows, :] += fold_lanes(g)
            gain = pc[rows, gain_col : gain_col + 1]
            total = total + fold(g * gain)
            cross = cross + fold(product * gain)
        mean_q = jnp.sum(total, axis=0, keepdims=True) / size
        mean_qn = jnp.sum(cross, axis=0, keepdims=True) / size
        for rows in steps(size):
            q = grad[rows, :] * pc[rows, gain_col : gain_col + 1]
            normed = normed_ref[0, rows, span].astype(F32)
            d = slope_ref[0, rows, span].astype(F32) * (q - mean_q - normed * mean_qn)
            row_sums[slot, rows, :] += fold_lanes(d)
            target[rows, span] = d.astype(BF)

    for grad, pre, span in zip(grads, pres, spans):
        back(grad, span, base + GAIN_B, n2_ref, s2_ref, DOWN_B, low)
        pre[...] = nn(down[0], low[:, span])
        for rows in steps(size):
            du = pre[rows, :] * su_ref[0, rows, span].astype(F32)
            row_sums[UP_B, rows, :] += fold_lanes(du)
            high[rows, span] = du.astype(BF)
        pre[...] = tn(up[0], high[:, span])
        for rows in steps(size):
            dm = grad[rows, :] + pre[rows, :]
            grad[rows, :] = dm
            dm_ref[0, rows, span] = dm.astype(BF)
        back(grad, span, base + GAIN_A, n1_ref, s1_ref, CONV_B, dc_ref.at[0])
    ff_sum[0] += nt(high[...], b_ref[0])
    ff_sum[1] += nt(v_ref[0], low[...])


def conv_back(layer, taps, dc, dm_ref, w, wide, grads):
    half = taps // 2
    width = grads[0].shape[1]
    for tap in range(taps):
        wide[tap] = shifted(dc, -(tap - half) * DILATIONS[layer])
    for at, grad in enumerate(grads):
        span = slice(at * width, (at + 1) * width)
        total = tn(w[0], wide[0, :, span])
        for tap in range(1, taps):
            total = total + tn(w[tap], wide[tap, :, span])
        grad[...] = total + dm_ref[0, :, span].astype(F32)


def middle_kernel(layer, taps, *refs):
    above_w, up, down, pc, dc_in, dm_in = refs[:6]
    kept = refs[6:13]
    outs = refs[13:17]
    wide, grads, work = refs[17], refs[18 : 18 + HALVES], refs[18 + HALVES :]

    here = pl.program_id(0)
    clear(here == 0, outs[2], work[2])
    conv_back(layer + 1, taps, dc_in[0], dm_in, above_w, wide, grads)
    chain(layer, grads, kept, up, down, pc, outs, work)
    close(here == pl.num_programs(0) - 1, work[2], outs[3])


def bottom_kernel(layer, taps, n_out, where, w, dc_in, dm_in, own_ref, *refs):
    others = refs[: n_out - 1]
    wide, *grads = refs[n_out - 1 :]
    conv_back(layer, taps, dc_in[0], dm_in, w, wide, grads)
    me = where[0]
    part = own_ref.shape[1]
    for at, grad in enumerate(grads):
        width = grad.shape[1]
        span = slice(at * width, (at + 1) * width)
        own_ref[0, :, span] = grad[pl.ds(pl.multiple_of(me * part, part), part), :]
        for ahead, ref in enumerate(others, start=1):
            spot = pl.multiple_of(lax.rem(me + ahead, n_out) * part, part)
            ref[0, :, span] = grad[pl.ds(spot, part), :].astype(BF)


def weight_kernel(layer, taps, chosen, with_rest, where, dc, a, *refs):
    if with_rest:
        ff, small = refs[:2]
        refs = refs[2:]
    keep, send, total = refs
    core = where[2]
    half = taps // 2
    blocks, rows, _ = keep.shape
    size = total.shape[1]

    def put(source, at, width):
        for block in range(blocks):
            first = block * 2 * rows
            mine = pl.multiple_of(first + core * rows, rows)
            other = pl.multiple_of(first + (1 - core) * rows, rows)
            keep[block, :, at : at + width] = source[pl.ds(mine, rows), :].astype(BF)
            send[block, :, at : at + width] = source[pl.ds(other, rows), :].astype(BF)

    skip = 0
    if with_rest:
        put(ff.at[0], 0, size)
        put(ff.at[1], size, size)
        put(small, 2 * size, small.shape[1])
        skip = 2 * size + small.shape[1]
    for at, tap in enumerate(chosen):
        by = -(tap - half) * DILATIONS[layer]
        acc = None
        for window in range(dc.shape[0]):
            part = nt(shifted(dc[window], by), a[window])
            acc = part if acc is None else acc + part
        total[at % 2] = acc
        put(total.at[at % 2], skip + at * size, size)


def pack_kernel(layers, where, conv, up, down, up_t, *refs):
    shares, sems = refs[:layers], refs[layers]
    tp, y, core, z = where[0], where[1], where[2], where[3]
    taps = conv.shape[1]
    moves = []
    for layer in range(layers):
        count = shares[layer].shape[1]
        quarter = up.shape[2] // 4
        at = core * (2 * quarter) + y * quarter
        if count < quarter:
            at = at + z * count
        rows = pl.ds(pl.multiple_of(at, count), count)
        moves.append((conv.at[layer, :, rows], shares[layer].at[0:taps]))
        moves.append((down.at[layer, rows], shares[layer].at[taps + 1]))
    moves = [pltpu.make_async_copy(src, dst, sems.at[i]) for i, (src, dst) in enumerate(moves)]
    for move in moves:
        move.start()
    for layer in range(layers):
        up_t[layer] = jnp.transpose(up[layer])
    for layer in range(layers):
        count = shares[layer].shape[1]
        quarter = up.shape[2] // 4
        at = core * (2 * quarter) + y * quarter
        if count < quarter:
            at = at + z * count
        shares[layer][taps] = up_t[layer, pl.ds(pl.multiple_of(at, count), count), :]
    for move in moves:
        move.wait()


def settle_conv(layer, first_tap, where, pieces, out, wide, sems, skip):
    count, rows, size = wide.shape[1:]
    moves = []
    for flip, piece in enumerate(pieces):
        c = where[2] if flip < 2 else 1 - where[2]
        y = where[1] if flip % 2 == 0 else 1 - where[1]
        at = pl.multiple_of(c * (2 * rows) + y * rows, rows)
        for tap in range(count):
            begin = skip + tap * size
            wide[flip, tap] = piece[:, begin : begin + size].astype(F32)
        target = out.at[layer, first_tap : first_tap + count, pl.ds(at, rows)]
        moves.append(pltpu.make_async_copy(wide.at[flip], target, sems.at[flip]))
        moves[-1].start()
    return moves


def settle_kernel(layer, first_tap, n_before, where, *refs):
    pieces = refs[:4]
    out, wide, sems = refs[4 + n_before :]
    for move in settle_conv(layer, first_tap, where, pieces, out, wide, sems, 0):
        move.wait()


def settle_rest_kernel(layer, n_before, where, *refs):
    pieces = refs[:4]
    out, rest, wide, sems = refs[4 + n_before :]
    skip = rest.shape[1]
    moves = settle_conv(layer, 0, where, pieces, out, wide, sems, skip)
    rows = pieces[0].shape[0]
    for flip, piece in enumerate(pieces):
        c = where[2] if flip < 2 else 1 - where[2]
        y = where[1] if flip % 2 == 0 else 1 - where[1]
        at = pl.multiple_of(c * (2 * rows) + y * rows, rows)
        rest[pl.ds(at, rows), :] = piece[:, :skip].astype(F32)
    for move in moves:
        move.wait()


def finish_kernel(rest0, rest1, up, down, conv_b, gain, bias, up_b, down_b):
    size = down.shape[2]
    for layer, rest in enumerate((rest0, rest1)):
        up[layer] = jnp.transpose(rest[:, :size])
        down[layer] = rest[:, size : 2 * size]
        small = jnp.transpose(rest[:, 2 * size :])
        conv_b[layer : layer + 1, :] = small[CONV_B : CONV_B + 1]
        up_b[layer : layer + 1, :] = small[UP_B : UP_B + 1]
        down_b[layer : layer + 1, :] = small[DOWN_B : DOWN_B + 1]
        for at, (g, b) in enumerate(((GAIN_A, BIAS_A), (GAIN_B, BIAS_B))):
            gain[layer, at : at + 1, :] = small[g : g + 1]
            bias[layer, at : at + 1, :] = small[b : b + 1]


def whole_spec(shape):
    return pl.BlockSpec(
        shape, lambda *_: (0,) * len(shape), pipeline_mode=pl.Buffered(buffer_count=1)
    )


def window_spec(shape, first=0):
    return pl.BlockSpec((1,) + shape[1:], lambda i: (i + first,) + (0,) * (len(shape) - 1))


def plane_spec(block, index):
    return pl.BlockSpec(
        block,
        lambda *_: (index,) + (0,) * (len(block) - 1),
        pipeline_mode=pl.Buffered(buffer_count=1),
    )


def any_spec():
    return pl.BlockSpec(memory_space=pl.ANY)


def smem_spec():
    return pl.BlockSpec(memory_space=pltpu.SMEM)


def params():
    return pltpu.CompilerParams(vmem_limit_bytes=VMEM_BYTES)


def cost(flops, nbytes):
    return pl.CostEstimate(flops=int(8 * flops), bytes_accessed=int(nbytes), transcendentals=0)


def struct(shape, dtype):
    return jax.ShapeDtypeStruct(shape, dtype)


def rotate(value, axis, ways, by):
    return lax.ppermute(value, axis, [(i, (i + by) % ways) for i in range(ways)])


def pick(value, index, dim):
    return lax.dynamic_index_in_dim(value, index, dim, keepdims=False)


def tie(value, *after):
    return lax.optimization_barrier((value,) + after)[0]


def add_up(terms):
    return sum(term.astype(F32) for term in terms).astype(BF)


def arrange(pieces, axis, dim):
    me = lax.axis_index(axis)
    ways = len(pieces)
    if ways == 2:
        low = jnp.where(me == 0, pieces[0], pieces[1])
        high = jnp.where(me == 0, pieces[1], pieces[0])
        return jnp.stack([low, high], axis=dim)
    shape = list(pieces[0].shape)
    shape.insert(dim, ways)
    out = jnp.zeros(shape, pieces[0].dtype)
    for back, piece in enumerate(pieces):
        spot = lax.rem(me + (ways - back), ways)
        out = lax.dynamic_update_index_in_dim(out, piece, spot, dim)
    return out


class Order:
    def __init__(self):
        self.last = ()

    def __call__(self, step, *values):
        values = lax.optimization_barrier(values + self.last)[: len(values)]
        result = step(*values)
        self.last = (jax.tree.leaves(result)[0],)
        return result


class Chunk:
    def __init__(self, order, sizes, keep, send):
        self.order = order
        self.ways = dict(zip(DP + ("tp",), sizes))
        blocks, rows, width = keep.shape
        self.rows, self.width = rows, width
        y, z = self.ways["y"], self.ways["z"]
        self.shape = (blocks, y, z, rows // (y * z), width)
        sent = rotate(send, "core", 2, 1)
        self.terms = [(keep.reshape(self.shape), ()), (sent.reshape(self.shape), ())]

    def total(self, values, *last):
        cut = []
        for value, (_, at) in zip(values, self.terms):
            for index in at + last:
                value = pick(value, index, 0)
            cut.append(value)
        return add_up(cut)

    def scatter(self, axis):
        me, count = lax.axis_index(axis), self.ways[axis]

        def step(*values):
            return [self.total(values, lax.rem(me + by, count)) for by in range(1, count)]

        outs = self.order(step, *[term for term, _ in self.terms])
        got = [rotate(out, axis, count, by) for by, out in enumerate(outs, start=1)]
        self.terms = [(term, at + (me,)) for term, at in self.terms] + [(g, ()) for g in got]

    def meet(self):
        piece = self.order(lambda *values: self.total(values), *[term for term, _ in self.terms])
        count = self.ways["z"]
        self.groups = [piece] + [rotate(piece, "z", count, by) for by in range(1, count)]

    def spread(self):
        quarter = self.order(lambda *groups: arrange(list(groups), "z", 0), *self.groups)
        quarter = quarter.reshape(self.rows // self.ways["y"], self.width)
        self.quarters = [quarter, rotate(quarter, "y", 2, 1)]

    def cross(self):
        self.quarters += [rotate(quarter, "core", 2, 1) for quarter in self.quarters]


class Pair(Chunk):
    def __init__(self, one, two):
        self.order, self.ways, self.rows = one.order, one.ways, one.rows
        self.width = one.width + two.width
        self.halves = (one, two)
        self.split = len(one.terms)
        self.terms = None

    def scatter(self, axis):
        if self.terms is not None:
            super().scatter(axis)
            return
        one, two = self.halves
        me, count = lax.axis_index(axis), self.ways[axis]
        values = [term for term, _ in one.terms + two.terms]

        def joined(values, spot):
            parts = [
                side.total(values[at : at + self.split], spot)
                for side, at in ((one, 0), (two, self.split))
            ]
            return jnp.concatenate(parts, axis=-1)

        def step(*values):
            sends = [joined(values, lax.rem(me + by, count)) for by in range(1, count)]
            return sends + [joined(values, me)]

        *outs, own = self.order(step, *values)
        got = [rotate(out, axis, count, by) for by, out in enumerate(outs, start=1)]
        self.terms = [(own, ())] + [(g, ()) for g in got]


def body(sizes, *args):
    (
        x_in,
        conv_w,
        conv_b,
        ln_gain,
        ln_bias,
        up_w,
        up_b,
        down_w,
        down_b,
        readout,
        cotangent,
        masked,
        species,
    ) = args
    n_z, n_y, n_core, n_tp = sizes
    layers, part, taps, size = conv_w.shape
    windows, _, length = x_in.shape
    mine = windows // n_tp
    planes = taps + 2
    me, my_y, my_core, my_z = (lax.axis_index(axis) for axis in ("tp", "y", "core", "z"))
    where = jnp.stack([me, my_y, my_core, my_z]).astype(jnp.int32)
    quarter = part // 4
    order = Order()
    conv_t = jnp.transpose(conv_w, (0, 2, 1, 3))

    vmem = pl.BlockSpec(memory_space=pltpu.VMEM)
    z_split = n_z if quarter // n_z >= 16 else 1
    up_t, first_share, second_share = order(
        pl.pallas_call(
            functools.partial(pack_kernel, layers),
            in_specs=[smem_spec(), any_spec(), vmem, any_spec()],
            out_specs=[vmem] * 3,
            out_shape=[
                struct((layers, part, size), BF),
                struct((planes, quarter, size), BF),
                struct((planes, quarter // z_split, size), BF),
            ],
            scratch_shapes=[pltpu.SemaphoreType.DMA((2 * layers,))],
            compiler_params=params(),
            name="pack_shares",
        ),
        where,
        conv_t,
        up_w,
        down_w,
    )

    def to_send(value):
        cut = value.reshape(n_tp, mine, part, length)
        return [pick(cut, me if by == 0 else lax.rem(me + by, n_tp), 0) for by in range(n_tp)]

    def exchange(sends, *after):
        return [
            rotate(tie(piece, *after), "tp", n_tp, by) for by, piece in enumerate(sends, start=1)
        ]

    def beside_quarter(own):
        return [own, rotate(own, "y", 2, 1)]

    def four_quarters(pair, *after):
        return pair + [rotate(tie(piece, *after), "core", 2, 1) for piece in pair]

    second_got = [rotate(second_share, "tp", n_tp, by) for by in range(1, n_tp)]
    first_got = [rotate(tie(first_share, *second_got), "tp", n_tp, by) for by in range(1, n_tp)]

    columns = []
    for layer in range(layers):
        columns += [
            conv_b[layer],
            ln_gain[layer, 0],
            ln_bias[layer, 0],
            up_b[layer],
            down_b[layer],
            ln_gain[layer, 1],
            ln_bias[layer, 1],
            jnp.zeros((part,), BF),
        ]
    table = jnp.concatenate([jnp.stack(columns), jnp.transpose(readout)])
    table = jnp.pad(table, ((0, 2), (0, 0)))
    table = arrange(
        [table] + [rotate(table, "tp", n_tp, by) for by in range(1, n_tp)], "tp", 1
    ).reshape(table.shape[0], size)
    pc = jnp.transpose(table[: layers * COLUMNS]).astype(F32)
    read_rows = table[layers * COLUMNS :]

    early = mine // 2 if mine >= 4 else mine
    x_send = order(to_send, x_in)
    x_early = exchange([piece[:early] for piece in x_send[1:]], *first_got)
    x_late = x_early
    if early < mine:
        x_late = exchange([piece[early:] for piece in x_send[1:]], *x_early)
    first_pairs = [beside_quarter(got) for got in first_got]
    first_parts = [piece for pair in first_pairs for piece in four_quarters(pair, pair[1])]
    second_pairs = []
    for got in second_got:
        if z_split > 1:
            groups = [got] + [rotate(got, "z", n_z, by) for by in range(1, n_z)]
            groups[0] = tie(got, *[pair[1] for pair in first_pairs])
            got = order(lambda *groups: arrange(list(groups), "z", 1), *groups)
            got = got.reshape(planes, quarter, size)
        second_pairs.append(beside_quarter(got))
    cot_send = order(to_send, cotangent)
    cot_pieces = [cot_send[0]] + exchange(cot_send[1:], *x_late)

    window = (mine, size, length)
    piece_shape = (mine, part, length)
    n_pieces = 4 * (n_tp - 1)
    kept_struct = [struct(window, BF)] * 8
    w_struct = struct((planes, size, size), BF)
    fwd_scratch = [
        pltpu.VMEM((size, length), BF),
        pltpu.VMEM((taps, size, length), BF),
    ] + [pltpu.VMEM((size, length // HALVES), F32)] * (2 * HALVES)
    load_scratch = [
        pltpu.VMEM((planes, size, size), BF),
        pltpu.SemaphoreType.DMA((3 + n_pieces,)),
        pltpu.SemaphoreType.DMA,
    ]
    conv_flops = 2.0 * taps * size * size * length * mine
    ff_flops = 4.0 * size * size * length * mine
    weight_specs = [smem_spec(), whole_spec(pc.shape)] + [any_spec()] * (3 + n_pieces)
    first = order(
        pl.pallas_call(
            functools.partial(first_early_kernel, 0, n_tp, n_pieces, taps),
            grid=(early,),
            in_specs=weight_specs + [window_spec(piece_shape)] * n_tp,
            out_specs=[window_spec(window)] * 9 + [any_spec()],
            out_shape=kept_struct + [struct(window, BF), w_struct],
            scratch_shapes=fwd_scratch + load_scratch,
            compiler_params=params(),
            cost_estimate=cost((conv_flops + ff_flops) / 2, 20e6),
            name="forward_first_early",
        ),
        where,
        pc,
        conv_t,
        up_t,
        down_w,
        *first_parts,
        x_send[0],
        *x_early,
    )
    w0 = first[9]
    *kept0, hidden = first[:9]
    second_parts = [p for pair in second_pairs for p in four_quarters(pair, hidden)]
    if early < mine:
        *kept0, hidden = order(
            pl.pallas_call(
                functools.partial(first_late_kernel, 0, n_tp, taps, 9),
                grid=(mine - early,),
                in_specs=[smem_spec(), whole_spec(pc.shape), whole_spec(w_struct.shape)]
                + [window_spec(piece_shape, early)]
                + [window_spec(piece_shape)] * (n_tp - 1)
                + [any_spec()] * 9,
                out_specs=[window_spec(window, early)] * 9,
                out_shape=kept_struct + [struct(window, BF)],
                scratch_shapes=fwd_scratch,
                input_output_aliases={3 + n_tp + at: at for at in range(9)},
                compiler_params=params(),
                cost_estimate=cost((conv_flops + ff_flops) / 2, 20e6),
                name="forward_first_late",
            ),
            where,
            pc,
            w0,
            x_send[0],
            *x_late,
            *first[:9],
        )

    mask_rows = lax.dynamic_slice_in_dim(masked, me * mine, mine, 0).reshape(mine, 1, length)
    chain_out_specs = [
        window_spec(window),
        window_spec(window),
        whole_spec((2, size, size)),
        whole_spec((size, 128)),
    ]
    chain_out = [
        struct(window, BF),
        struct(window, BF),
        struct((2, size, size), F32),
        struct((size, 128), F32),
    ]
    half_scratch = [pltpu.VMEM((size, length // HALVES), F32)] * HALVES
    chain_scratch = [
        pltpu.VMEM((size, length), BF),
        pltpu.VMEM((size, length), BF),
        pltpu.VMEM((7, size, 128), F32),
    ] + half_scratch
    wide_scratch = [pltpu.VMEM((taps, size, length), BF)]
    ff_specs = [plane_spec((1, size, size), taps), plane_spec((1, size, size), taps + 1)]
    conv_spec = plane_spec((taps, size, size), 0)
    *y_pieces, chance, dc1, dm1, ff1, small1, w1 = order(
        pl.pallas_call(
            functools.partial(second_kernel, 1, n_tp, n_pieces, taps),
            grid=(mine,),
            in_specs=weight_specs
            + [window_spec(window), whole_spec(read_rows.shape), window_spec((mine, 1, length))]
            + [window_spec(piece_shape)] * n_tp,
            out_specs=[window_spec(piece_shape)] * n_tp
            + [window_spec((mine, 8, 128))]
            + chain_out_specs
            + [any_spec()],
            out_shape=[struct(piece_shape, BF)] * n_tp
            + [struct((mine, 8, 128), F32)]
            + chain_out
            + [w_struct],
            scratch_shapes=fwd_scratch
            + [pltpu.VMEM((1, size, length), BF)] * 7
            + chain_scratch[:3]
            + load_scratch,
            compiler_params=params(),
            cost_estimate=cost(conv_flops + 3 * ff_flops, 20e6),
            name="second_layer",
        ),
        where,
        pc,
        conv_t,
        up_t,
        down_w,
        *second_parts,
        hidden,
        read_rows,
        mask_rows,
        *cot_pieces,
    )

    per_window = jnp.sum(chance, axis=2)[:, :6]
    my_species = lax.dynamic_slice_in_dim(species, me * mine, mine, 0)
    hot = (my_species[None, :] == jnp.arange(SPECIES, dtype=jnp.int32)[:, None]).astype(F32)
    species_part = jnp.dot(hot, per_window, precision=lax.Precision.HIGHEST) / length

    def weight_grads(layer, chosen, dc, a, rest, name):
        width = len(chosen) * size + (2 * size + 128 if rest else 0)
        return order(pl.pallas_call(
            functools.partial(weight_kernel, layer, taps, chosen, bool(rest)),
            in_specs=[smem_spec()] + [pl.BlockSpec(memory_space=pltpu.VMEM)] * (2 + len(rest)),
            out_specs=[pl.BlockSpec(memory_space=pltpu.VMEM)] * 2,
            out_shape=[struct((n_tp, part // 2, width), BF)] * 2,
            scratch_shapes=[pltpu.VMEM((2, size, size), F32)],
            compiler_params=params(),
            cost_estimate=cost(conv_flops * len(chosen) / taps, 10e6),
            name=name,
        ), where, dc, a, *rest)

    spot = jnp.arange(size) % part
    spread = jnp.where(
        spot < SPECIES * 6, jnp.tile(jnp.pad(species_part.reshape(-1), (0, part - SPECIES * 6)), n_tp), 0.0
    )
    small1 = jnp.where(jnp.arange(128)[None, :] == 7, spread[:, None], small1)

    split = (taps + 1) // 2
    low_taps, high_taps = tuple(range(split)), tuple(range(split, taps))

    def chunk(layer, chosen, dc, a, rest, name):
        return Chunk(order, sizes, *weight_grads(layer, chosen, dc, a, rest, name))

    low1 = chunk(1, low_taps, dc1, hidden, (ff1, small1), "weights_second_low")
    high1 = chunk(1, high_taps, dc1, hidden, (), "weights_second_high")
    low1.scatter("tp")
    high1.scatter("tp")

    dc0, dm0, ff0, small0 = order(
        pl.pallas_call(
            functools.partial(middle_kernel, 0, taps),
            grid=(mine,),
            in_specs=[conv_spec] + ff_specs + [whole_spec(pc.shape)] + [window_spec(window)] * 9,
            out_specs=chain_out_specs,
            out_shape=chain_out,
            scratch_shapes=wide_scratch + half_scratch + chain_scratch,
            compiler_params=params(),
            cost_estimate=cost(conv_flops + 2 * ff_flops, 20e6),
            name="chain_first",
        ),
        w1,
        w0,
        w0,
        pc,
        dc1,
        dm1,
        *kept0[1:],
    )
    y_back = [y_pieces[0]] + [
        rotate(tie(y_pieces[by], high1.terms[2][0]), "tp", n_tp, by) for by in range(1, n_tp)
    ]
    both1 = Pair(low1, high1)
    both1.scatter("y")
    low0 = chunk(0, low_taps, dc0, kept0[0], (ff0, small0), "weights_first_low")
    high0 = chunk(0, high_taps, dc0, kept0[0], (), "weights_first_high")
    both1.scatter("z")
    y_out = order(lambda *pieces: arrange(list(pieces), "tp", 0), *y_back)
    y_out = y_out.reshape(windows, part, length)
    low0.scatter("tp")
    high0.scatter("tp")
    x_grads = order(
        pl.pallas_call(
            functools.partial(bottom_kernel, 0, taps, n_tp),
            grid=(mine,),
            in_specs=[smem_spec(), conv_spec] + [window_spec(window)] * 2,
            out_specs=[window_spec(piece_shape)] * n_tp,
            out_shape=[struct(piece_shape, F32)] + [struct(piece_shape, BF)] * (n_tp - 1),
            scratch_shapes=wide_scratch + [pltpu.VMEM((size, length), F32)],
            compiler_params=params(),
            cost_estimate=cost(conv_flops, 15e6),
            name="input_grad",
        ),
        where,
        w0,
        dc0,
        dm0,
    )
    both1.meet()
    low0.scatter("y")
    both1.spread()
    low0.scatter("z")
    high0.scatter("y")
    x_back = [x_grads[0]] + [
        rotate(tie(x_grads[by], high0.terms[2][0]), "tp", n_tp, by) for by in range(1, n_tp)
    ]
    low0.meet()
    high0.scatter("z")
    both1.cross()
    low0.spread()
    high0.meet()

    conv_struct = struct((layers, taps, part, size), F32)
    skip = 2 * size + 128

    def settle(layer, chosen, quarters, before, rest, name):
        n = len(quarters)
        scratch = [
            pltpu.VMEM((n, len(chosen), part // n, size), F32),
            pltpu.SemaphoreType.DMA((n,)),
        ]
        if rest:
            kernel = functools.partial(settle_rest_kernel, layer, len(before))
        else:
            kernel = functools.partial(settle_kernel, layer, chosen[0], len(before))
        return order(
            pl.pallas_call(
                kernel,
                in_specs=[smem_spec()] + [vmem] * n + [any_spec()] * len(before),
                out_specs=[any_spec()] + [vmem] * rest,
                out_shape=[conv_struct] + [struct((part, skip), F32)] * rest,
                scratch_shapes=scratch,
                input_output_aliases={1 + n: 0} if before else {},
                compiler_params=params(),
                name=name,
            ),
            where,
            *quarters,
            *before,
        )

    grad_x = order(
        lambda *pieces: arrange([piece.astype(F32) for piece in pieces], "tp", 0), *x_back
    ).reshape(windows, part, length)
    grad_conv, rest1 = settle(1, low_taps + high_taps, both1.quarters, (), 1, "settle_second")
    low0.cross()
    high0.spread()
    high0.cross()
    grad_conv, rest0 = settle(0, low_taps, low0.quarters, (grad_conv,), 1, "settle_first_low")
    grad_up_w, grad_down_w, g_conv_b, g_gain, g_bias, g_up_b, g_down_b = order(
        pl.pallas_call(
            finish_kernel,
            in_specs=[vmem] * 2,
            out_specs=[vmem] * 7,
            out_shape=[
                struct((layers, size, part), F32),
                struct((layers, part, size), F32),
                struct((layers, part), F32),
                struct((layers, 2, part), F32),
                struct((layers, 2, part), F32),
                struct((layers, part), F32),
                struct((layers, part), F32),
            ],
            compiler_params=params(),
            name="finish_rest",
        ),
        rest0,
        rest1,
    )
    (grad_conv,) = settle(0, high_taps, high0.quarters, (grad_conv,), 0, "settle_first_high")

    grad_conv_w = jnp.transpose(grad_conv, (0, 2, 1, 3))
    species_sum = rest1[: SPECIES * 6, 2 * size + 7].reshape(SPECIES, 6)
    return (
        y_out,
        grad_x,
        grad_conv_w,
        g_conv_b,
        g_gain,
        g_bias,
        grad_up_w,
        g_up_b,
        grad_down_w,
        g_down_b,
        species_sum,
    )


def solution(mesh):
    dp, tp = mesh.shape["dp"], mesh.shape["tp"]
    n_core = n_y = 2
    n_z = dp // (n_core * n_y)
    fine = Mesh(mesh.devices.reshape(n_z, n_y, n_core, tp), DP + ("tp",))
    placed = (
        P(DP, "tp", None),
        P(None, "tp", None, None),
        P(None, "tp"),
        P(None, None, "tp"),
        P(None, None, "tp"),
        P(None, None, "tp"),
        P(None, "tp"),
        P(None, "tp", None),
        P(None, "tp"),
        P("tp", None),
        P(DP, "tp", None),
        P(DP, None),
        P(DP),
    )
    return jax.shard_map(
        functools.partial(body, (n_z, n_y, n_core, tp)),
        mesh=fine,
        in_specs=placed,
        out_specs=(
            P(DP, "tp", None),
            P(DP, "tp", None),
            P(None, "tp", None, None),
            P(None, "tp"),
            P(None, None, "tp"),
            P(None, None, "tp"),
            P(None, None, "tp"),
            P(None, "tp"),
            P(None, "tp", None),
            P(None, "tp"),
            P(),
        ),
        check_vma=False,
    )
```

```python
import functools

import jax
import jax.numpy as jnp
from jax import lax
from jax.experimental import pallas as pl
from jax.experimental.pallas import tpu as pltpu
from jax.sharding import Mesh
from jax.sharding import PartitionSpec as P

DILATIONS = (2, 32)
SPECIES = 8
CLASSES = 6
EPS = 1e-05
BF = jnp.bfloat16
F32 = jnp.float32
DP = ("z", "y", "core")
STEP = 32
HALVES = 2
VMEM_BYTES = 58 * 2**20
CONV_B, GAIN_A, BIAS_A, UP_B, DOWN_B, GAIN_B, BIAS_B = range(7)
COLUMNS = 8


def shifted(rows, by):
    if by == 0:
        return rows
    blank = jnp.zeros((rows.shape[0], abs(by)), rows.dtype)
    if by > 0:
        return jnp.concatenate([rows[:, by:], blank], axis=1)
    return jnp.concatenate([blank, rows[:, :by]], axis=1)


def fold(tile):
    return sum(tile[at : at + 8] for at in range(0, tile.shape[0], 8))


def fold_lanes(tile):
    return sum(tile[:, at : at + 128] for at in range(0, tile.shape[1], 128))


def gelu_pair(x):
    cdf = 0.5 + 0.5 * lax.erf(x * 0.7071067811865476)
    return x * cdf, cdf + x * jnp.exp(-0.5 * x * x) * 0.3989422804014327


def nn(left, right):
    return jnp.dot(left, right, preferred_element_type=F32)


def tn(left, right):
    return lax.dot_general(left, right, (((0,), (0,)), ((), ())), preferred_element_type=F32)


def nt(left, right):
    return lax.dot_general(left, right, (((1,), (1,)), ((), ())), preferred_element_type=F32)


def steps(size):
    return [slice(at, at + STEP) for at in range(0, size, STEP)]


def place(pieces, me, target):
    ways = len(pieces)
    for back, piece in enumerate(pieces):
        size = piece.shape[1]
        spot = lax.rem(me + (ways - back), ways) * size
        target[pl.ds(pl.multiple_of(spot, size), size), :] = piece[0]


def norm_stats(total, square, width):
    mean = jnp.sum(total, axis=0, keepdims=True) / width
    var = jnp.sum(square, axis=0, keepdims=True) / width - mean * mean
    return mean, lax.rsqrt(var + EPS)


def activate_and_sum(pre, col, pc, slope_ref, span):
    size, length = pre.shape
    total = jnp.zeros((8, length), F32)
    square = jnp.zeros((8, length), F32)
    for rows in steps(size):
        value, slope = gelu_pair(pre[rows, :] + pc[rows, col : col + 1])
        pre[rows, :] = value
        slope_ref[0, rows, span] = slope.astype(BF)
        total = total + fold(value)
        square = square + fold(value * value)
    return norm_stats(total, square, size)


def load_weights(layer, where, blocks, pieces, full, w, sems, out_sem):
    tp, y, core = where[0], where[1], where[2]
    conv, up, down = blocks
    taps, part = conv.shape[1], conv.shape[2]
    ways = w.shape[1] // part
    here = pl.program_id(0)

    def rows(owner, at, count):
        return pl.ds(pl.multiple_of(owner * part + at, count), count)

    @pl.when(here == 0)
    def _():
        own = rows(tp, 0, part)
        copies = [
            (conv.at[layer], w.at[0:taps, own]),
            (up.at[layer], w.at[taps, own]),
            (down.at[layer], w.at[taps + 1, own]),
        ]
        quarter = part // 4
        for back in range(1, ways):
            owner = lax.rem(tp + (ways - back), ways)
            for flip in range(4):
                c = core if flip < 2 else 1 - core
                at = c * (2 * quarter) + (y if flip % 2 == 0 else 1 - y) * quarter
                copies.append((pieces[4 * (back - 1) + flip], w.at[:, rows(owner, at, quarter)]))
        moves = [pltpu.make_async_copy(src, dst, sems.at[i]) for i, (src, dst) in enumerate(copies)]
        for move in moves:
            move.start()
        for move in moves:
            move.wait()
        pltpu.make_async_copy(w, full, out_sem).start()

    @pl.when(here == pl.num_programs(0) - 1)
    def _():
        pltpu.make_async_copy(w, full, out_sem).wait()


def first_early_kernel(layer, n_in, n_pieces, taps, *refs):
    where, pc = refs[:2]
    blocks, parts = refs[2:5], refs[5 : 5 + n_pieces]
    at = 5 + n_pieces
    pieces = refs[at : at + n_in]
    at += n_in
    *kept, out = refs[at : at + 9]
    full = refs[at + 9]
    *work, w, sems, out_sem = refs[at + 10 :]
    load_weights(layer, where, blocks, parts, full, w, sems, out_sem)
    forward_window(layer, taps, where, pc, w, pieces, kept, work)
    out[0] = work[0][...]


def first_late_kernel(layer, n_in, taps, n_before, where, pc, w, *refs):
    pieces, refs = refs[:n_in], refs[n_in + n_before :]
    *kept, out = refs[:9]
    work = refs[9:]
    forward_window(layer, taps, where, pc, w, pieces, kept, work)
    out[0] = work[0][...]


def second_kernel(layer, n_in, n_pieces, taps, *refs):
    where, pc = refs[:2]
    blocks, parts = refs[2:5], refs[5 : 5 + n_pieces]
    at = 5 + n_pieces
    hidden, readout, mask_ref, kinds = refs[at : at + 4]
    cots = refs[at + 4 : at + 4 + n_in]
    at += 4 + n_in
    y_refs = refs[at : at + n_in]
    dc_ref, dm_ref, ff_sum, small, full = refs[at + n_in : at + n_in + 5]
    refs = refs[at + n_in + 5 :]
    act, wide, *pairs = refs[: 2 + 2 * HALVES]
    kept = refs[2 + 2 * HALVES : 9 + 2 * HALVES]
    low, high, row_sums, shares, w, sems, out_sem = refs[9 + 2 * HALVES :]
    load_weights(layer, where, blocks, parts, full, w, sems, out_sem)
    here = pl.program_id(0)
    clear(here == 0, ff_sum, row_sums, shares)
    forward_window(layer, taps, where, pc, w, (hidden,), (None,) + kept, (act, wide, *pairs))
    me = where[0]
    part = act.shape[0] // n_in
    for ahead, ref in enumerate(y_refs):
        spot = lax.rem(me + ahead, n_in) * part
        ref[0] = act[pl.ds(pl.multiple_of(spot, part), part), :]
    logits = nn(readout[...], act[...])
    seat = lax.broadcasted_iota(jnp.int32, logits.shape, 0)
    logits = jnp.where(seat < CLASSES, logits, -1e30)
    raised = jnp.exp(logits - jnp.max(logits, axis=0, keepdims=True))
    chance = raised / jnp.sum(raised, axis=0, keepdims=True)
    chance = fold_lanes(chance * mask_ref[0].astype(F32))
    for kind in range(SPECIES):
        shares[8 * kind : 8 * kind + 8, :] += jnp.where(kinds[here] == kind, chance, 0.0)
    grads = pairs[HALVES:]
    for back, piece in enumerate(cots):
        spot = pl.multiple_of(lax.rem(me + (n_in - back), n_in) * part, part)
        for at, grad in enumerate(grads):
            width = grad.shape[1]
            grad[pl.ds(spot, part), :] = piece[0, :, at * width : (at + 1) * width].astype(F32)
    up, down = w.at[pl.ds(taps, 1)], w.at[pl.ds(taps + 1, 1)]
    outs = (dc_ref, dm_ref, ff_sum)
    chain(layer, grads, kept, up, down, pc, outs, (low, high, row_sums, *pairs[:HALVES]))

    @pl.when(here == pl.num_programs(0) - 1)
    def _():
        close(row_sums, small, shares, part)


def forward_window(layer, taps, where, pc, w, pieces, kept, work):
    a_ref, b_ref, n1_ref, s1_ref, su_ref, v_ref, s2_ref, n2_ref = kept
    act, wide, *pairs = work
    size, length = act.shape
    base = layer * COLUMNS
    half = taps // 2
    width = length // HALVES
    spans = [slice(at, at + width) for at in range(0, length, width)]
    pres, mids = pairs[:HALVES], pairs[HALVES:]
    place(pieces, where[0], act)
    if a_ref is not None:
        a_ref[0] = act[...]
    for tap in range(taps):
        wide[tap] = shifted(act[...], (tap - half) * DILATIONS[layer])

    def convolve(pre, span):
        total = nn(w[0], wide[0, :, span])
        for tap in range(1, taps):
            total = total + nn(w[tap], wide[tap, :, span])
        pre[...] = total

    def first_norm(pre, mid, span):
        mean, inv = activate_and_sum(pre, base + CONV_B, pc, s1_ref, span)
        for rows in steps(size):
            normed = (pre[rows, :] - mean) * inv
            m = (
                act[rows, span].astype(F32)
                + normed * pc[rows, base + GAIN_A : base + GAIN_A + 1]
                + pc[rows, base + BIAS_A : base + BIAS_A + 1]
            )
            n1_ref[0, rows, span] = normed.astype(BF)
            s1_ref[0, rows, span] = (s1_ref[0, rows, span].astype(F32) * inv).astype(BF)
            mid[rows, :] = m
            b_ref[0, rows, span] = m.astype(BF)

    def hidden(pre, span):
        for rows in steps(size):
            value, slope = gelu_pair(pre[rows, :] + pc[rows, base + UP_B : base + UP_B + 1])
            v_ref[0, rows, span] = value.astype(BF)
            su_ref[0, rows, span] = slope.astype(BF)

    def second_norm(pre, mid, span):
        mean, inv = activate_and_sum(pre, base + DOWN_B, pc, s2_ref, span)
        for rows in steps(size):
            normed = (pre[rows, :] - mean) * inv
            out = (
                mid[rows, :]
                + normed * pc[rows, base + GAIN_B : base + GAIN_B + 1]
                + pc[rows, base + BIAS_B : base + BIAS_B + 1]
            )
            n2_ref[0, rows, span] = normed.astype(BF)
            s2_ref[0, rows, span] = (s2_ref[0, rows, span].astype(F32) * inv).astype(BF)
            act[rows, span] = out.astype(BF)

    for pre, span in zip(pres, spans):
        convolve(pre, span)
    for pre, mid, span in zip(pres, mids, spans):
        first_norm(pre, mid, span)
        pre[...] = nn(w[taps], b_ref[0, :, span])
        hidden(pre, span)
        pre[...] = tn(w[taps + 1], v_ref[0, :, span])
        second_norm(pre, mid, span)

def clear(first, *sums):
    @pl.when(first)
    def _():
        for ref in sums:
            ref[...] = jnp.zeros_like(ref)


def close(row_sums, small_ref, shares=None, part=0):
    for rows in steps(small_ref.shape[0]):
        seat = lax.broadcasted_iota(jnp.int32, (STEP, 128), 1)
        table = jnp.zeros((STEP, 128), F32)
        for slot in range(7):
            column = jnp.sum(row_sums[slot, rows, :], axis=1, keepdims=True)
            table = jnp.where(seat == slot, column, table)
        if shares is not None and rows.start % part < 8 * SPECIES:
            at = rows.start % part
            column = jnp.sum(shares[at : at + STEP, :], axis=1, keepdims=True)
            table = jnp.where(seat == 7, column, table)
        small_ref[rows, :] = table


def chain(layer, grads, kept, up, down, pc, outs, work):
    b_ref, n1_ref, s1_ref, su_ref, v_ref, s2_ref, n2_ref = kept
    dc_ref, dm_ref, ff_sum = outs
    low, high, row_sums, *pres = work
    size, width = pres[0].shape
    base = layer * COLUMNS
    spans = [slice(at, at + width) for at in range(0, low.shape[1], width)]

    def back(grad, span, gain_col, normed_ref, slope_ref, slot, target):
        total = jnp.zeros((8, width), F32)
        cross = jnp.zeros((8, width), F32)
        for rows in steps(size):
            g = grad[rows, :]
            product = g * normed_ref[0, rows, span].astype(F32)
            row_sums[slot + 1, rows, :] += fold_lanes(product)
            row_sums[slot + 2, rows, :] += fold_lanes(g)
            gain = pc[rows, gain_col : gain_col + 1]
            total = total + fold(g * gain)
            cross = cross + fold(product * gain)
        mean_q = jnp.sum(total, axis=0, keepdims=True) / size
        mean_qn = jnp.sum(cross, axis=0, keepdims=True) / size
        for rows in steps(size):
            q = grad[rows, :] * pc[rows, gain_col : gain_col + 1]
            normed = normed_ref[0, rows, span].astype(F32)
            d = slope_ref[0, rows, span].astype(F32) * (q - mean_q - normed * mean_qn)
            row_sums[slot, rows, :] += fold_lanes(d)
            target[rows, span] = d.astype(BF)

    for grad, pre, span in zip(grads, pres, spans):
        back(grad, span, base + GAIN_B, n2_ref, s2_ref, DOWN_B, low)
        pre[...] = nn(down[0], low[:, span])
        for rows in steps(size):
            du = pre[rows, :] * su_ref[0, rows, span].astype(F32)
            row_sums[UP_B, rows, :] += fold_lanes(du)
            high[rows, span] = du.astype(BF)
        pre[...] = tn(up[0], high[:, span])
        for rows in steps(size):
            dm = grad[rows, :] + pre[rows, :]
            grad[rows, :] = dm
            dm_ref[0, rows, span] = dm.astype(BF)
        back(grad, span, base + GAIN_A, n1_ref, s1_ref, CONV_B, dc_ref.at[0])
    ff_sum[0] += nt(high[...], b_ref[0])
    ff_sum[1] += nt(v_ref[0], low[...])


def conv_back(layer, taps, dc, dm_ref, w, wide, grads):
    half = taps // 2
    width = grads[0].shape[1]
    for tap in range(taps):
        wide[tap] = shifted(dc, -(tap - half) * DILATIONS[layer])
    for at, grad in enumerate(grads):
        span = slice(at * width, (at + 1) * width)
        total = tn(w[0], wide[0, :, span])
        for tap in range(1, taps):
            total = total + tn(w[tap], wide[tap, :, span])
        grad[...] = total + dm_ref[0, :, span].astype(F32)


def middle_kernel(layer, taps, *refs):
    above_w, up, down, pc, dc_in, dm_in = refs[:6]
    kept = refs[6:13]
    dc_ref, dm_ref, ff_sum, small = refs[13:17]
    wide, grads = refs[17], refs[18 : 18 + HALVES]
    low, high, row_sums, *pres = refs[18 + HALVES :]
    here = pl.program_id(0)
    clear(here == 0, ff_sum, row_sums)
    conv_back(layer + 1, taps, dc_in[0], dm_in, above_w, wide, grads)
    outs = (dc_ref, dm_ref, ff_sum)
    chain(layer, grads, kept, up, down, pc, outs, (low, high, row_sums, *pres))

    @pl.when(here == pl.num_programs(0) - 1)
    def _():
        close(row_sums, small)


def bottom_kernel(layer, taps, n_out, where, w, dc_in, dm_in, own_ref, *refs):
    others = refs[: n_out - 1]
    wide, *grads = refs[n_out - 1 :]
    conv_back(layer, taps, dc_in[0], dm_in, w, wide, grads)
    me = where[0]
    part = own_ref.shape[1]
    for at, grad in enumerate(grads):
        width = grad.shape[1]
        span = slice(at * width, (at + 1) * width)
        own_ref[0, :, span] = grad[pl.ds(pl.multiple_of(me * part, part), part), :]
        for ahead, ref in enumerate(others, start=1):
            spot = pl.multiple_of(lax.rem(me + ahead, n_out) * part, part)
            ref[0, :, span] = grad[pl.ds(spot, part), :].astype(BF)


def weight_part(layer, taps, chosen, core, dc, a, rest, keep, send, total):
    half = taps // 2
    blocks, rows, _ = keep.shape
    size = total.shape[1]

    def put(source, at, width):
        for block in range(blocks):
            first = block * 2 * rows
            mine = pl.multiple_of(first + core * rows, rows)
            other = pl.multiple_of(first + (1 - core) * rows, rows)
            keep[block, :, at : at + width] = source[pl.ds(mine, rows), :].astype(BF)
            send[block, :, at : at + width] = source[pl.ds(other, rows), :].astype(BF)

    skip = 0
    if rest:
        ff, small = rest
        put(ff.at[0], 0, size)
        put(ff.at[1], size, size)
        put(small, 2 * size, small.shape[1])
        skip = 2 * size + small.shape[1]
    for at, tap in enumerate(chosen):
        by = -(tap - half) * DILATIONS[layer]
        acc = None
        for window in range(dc.shape[0]):
            part = nt(shifted(dc[window], by), a[window])
            acc = part if acc is None else acc + part
        total[at % 2] = acc
        put(total.at[at % 2], skip + at * size, size)


def weight_kernel(layer, taps, chosen, where, dc, a, *refs):
    rest, (keep, send, total) = refs[:-3], refs[-3:]
    weight_part(layer, taps, chosen, where[2], dc, a, rest, keep, send, total)


def pack_kernel(layers, where, conv, up, down, up_t, *refs):
    shares, sems = refs[:layers], refs[layers]
    tp, y, core, z = where[0], where[1], where[2], where[3]
    taps = conv.shape[1]
    moves = []
    for layer in range(layers):
        count = shares[layer].shape[1]
        quarter = up.shape[2] // 4
        at = core * (2 * quarter) + y * quarter
        if count < quarter:
            at = at + z * count
        rows = pl.ds(pl.multiple_of(at, count), count)
        moves.append((conv.at[layer, :, rows], shares[layer].at[0:taps]))
        moves.append((down.at[layer, rows], shares[layer].at[taps + 1]))
    moves = [pltpu.make_async_copy(src, dst, sems.at[i]) for i, (src, dst) in enumerate(moves)]
    for move in moves:
        move.start()
    for layer in range(layers):
        up_t[layer] = jnp.transpose(up[layer])
    for layer in range(layers):
        count = shares[layer].shape[1]
        quarter = up.shape[2] // 4
        at = core * (2 * quarter) + y * quarter
        if count < quarter:
            at = at + z * count
        shares[layer][taps] = up_t[layer, pl.ds(pl.multiple_of(at, count), count), :]
    for move in moves:
        move.wait()


def settle_conv(layer, first_tap, where, pieces, out, wide, sems, skip):
    count, rows, size = wide.shape[1:]
    moves = []
    for flip, piece in enumerate(pieces):
        c = where[2] if flip < 2 else 1 - where[2]
        y = where[1] if flip % 2 == 0 else 1 - where[1]
        at = pl.multiple_of(c * (2 * rows) + y * rows, rows)
        for tap in range(count):
            begin = skip + tap * size
            wide[flip, tap] = piece[:, begin : begin + size].astype(F32)
        target = out.at[layer, first_tap : first_tap + count, pl.ds(at, rows)]
        moves.append(pltpu.make_async_copy(wide.at[flip], target, sems.at[flip]))
        moves[-1].start()
    return moves


def settle_rest_kernel(layer, where, *refs):
    pieces = refs[:4]
    out, rest, wide, sems = refs[4:]
    skip = rest.shape[1]
    moves = settle_conv(layer, 0, where, pieces, out, wide, sems, skip)
    rows = pieces[0].shape[0]
    for flip, piece in enumerate(pieces):
        c = where[2] if flip < 2 else 1 - where[2]
        y = where[1] if flip % 2 == 0 else 1 - where[1]
        at = pl.multiple_of(c * (2 * rows) + y * rows, rows)
        rest[pl.ds(at, rows), :] = piece[:, :skip].astype(F32)
    for move in moves:
        move.wait()


def settle_last_kernel(layer, split, where, *refs):
    low, high, (other,) = refs[:4], refs[4:8], refs[8:9]
    out, up, down, conv_b, gain, bias, up_b, down_b = refs[10:18]
    rest, wide_low, wide_high, sems_low, sems_high = refs[18:]
    skip = rest.shape[1]
    moves = settle_conv(layer, 0, where, low, out, wide_low, sems_low, skip)
    moves += settle_conv(layer, split, where, high, out, wide_high, sems_high, 0)
    rows = low[0].shape[0]
    for flip, piece in enumerate(low):
        c = where[2] if flip < 2 else 1 - where[2]
        y = where[1] if flip % 2 == 0 else 1 - where[1]
        at = pl.multiple_of(c * (2 * rows) + y * rows, rows)
        rest[pl.ds(at, rows), :] = piece[:, :skip].astype(F32)
    size = down.shape[2]
    for at_layer, source in ((layer, rest), (1 - layer, other)):
        one = slice(at_layer, at_layer + 1)
        up[at_layer] = jnp.transpose(source[:, :size])
        down[at_layer] = source[:, size : 2 * size]
        small = jnp.transpose(source[:, 2 * size :])
        conv_b[one, :] = small[CONV_B : CONV_B + 1]
        up_b[one, :] = small[UP_B : UP_B + 1]
        down_b[one, :] = small[DOWN_B : DOWN_B + 1]
        for at, (g, b) in enumerate(((GAIN_A, BIAS_A), (GAIN_B, BIAS_B))):
            gain[at_layer, at : at + 1, :] = small[g : g + 1]
            bias[at_layer, at : at + 1, :] = small[b : b + 1]
    for move in moves:
        move.wait()


def whole_spec(shape):
    return pl.BlockSpec(
        shape, lambda *_: (0,) * len(shape), pipeline_mode=pl.Buffered(buffer_count=1)
    )


def window_spec(shape, first=0):
    return pl.BlockSpec((1,) + shape[1:], lambda i: (i + first,) + (0,) * (len(shape) - 1))


def plane_spec(block, index):
    return pl.BlockSpec(
        block,
        lambda *_: (index,) + (0,) * (len(block) - 1),
        pipeline_mode=pl.Buffered(buffer_count=1),
    )


def any_spec():
    return pl.BlockSpec(memory_space=pl.ANY)


def smem_spec():
    return pl.BlockSpec(memory_space=pltpu.SMEM)


def params():
    return pltpu.CompilerParams(vmem_limit_bytes=VMEM_BYTES)


def cost(flops, nbytes):
    return pl.CostEstimate(flops=int(8 * flops), bytes_accessed=int(nbytes), transcendentals=0)


def struct(shape, dtype):
    return jax.ShapeDtypeStruct(shape, dtype)


def rotate(value, axis, ways, by):
    return lax.ppermute(value, axis, [(i, (i + by) % ways) for i in range(ways)])


def pick(value, index, dim):
    return lax.dynamic_index_in_dim(value, index, dim, keepdims=False)


def tie(value, *after):
    return lax.optimization_barrier((value,) + after)[0]


def add_up(terms):
    return sum(term.astype(F32) for term in terms).astype(BF)


def arrange(pieces, axis, dim):
    me = lax.axis_index(axis)
    ways = len(pieces)
    if ways == 2:
        low = jnp.where(me == 0, pieces[0], pieces[1])
        high = jnp.where(me == 0, pieces[1], pieces[0])
        return jnp.stack([low, high], axis=dim)
    shape = list(pieces[0].shape)
    shape.insert(dim, ways)
    out = jnp.zeros(shape, pieces[0].dtype)
    for back, piece in enumerate(pieces):
        spot = lax.rem(me + (ways - back), ways)
        out = lax.dynamic_update_index_in_dim(out, piece, spot, dim)
    return out


class Order:
    def __init__(self):
        self.last = ()

    def __call__(self, step, *values):
        values = lax.optimization_barrier(values + self.last)[: len(values)]
        result = step(*values)
        self.last = (jax.tree.leaves(result)[0],)
        return result


class Chunk:
    def __init__(self, order, sizes, keep, send):
        self.order = order
        self.ways = dict(zip(DP + ("tp",), sizes))
        blocks, rows, width = keep.shape
        self.rows, self.width = rows, width
        y, z = self.ways["y"], self.ways["z"]
        self.shape = (blocks, y, z, rows // (y * z), width)
        self.left = ["tp", "y", "z"]
        sent = rotate(send, "core", 2, 1)
        self.terms = [(keep.reshape(self.shape), ()), (sent.reshape(self.shape), ())]

    def total(self, values, *last):
        cut = []
        for value, (_, at) in zip(values, self.terms):
            for dim, index in at + last:
                value = pick(value, index, dim)
            cut.append(value)
        return add_up(cut)

    def scatter(self, axis):
        me, count = lax.axis_index(axis), self.ways[axis]
        dim = self.left.index(axis)

        def step(*values):
            return [self.total(values, (dim, lax.rem(me + by, count))) for by in range(1, count)]

        outs = self.order(step, *[term for term, _ in self.terms])
        got = [rotate(out, axis, count, by) for by, out in enumerate(outs, start=1)]
        self.terms = [(term, at + ((dim, me),)) for term, at in self.terms]
        self.terms += [(g, ()) for g in got]
        self.left.remove(axis)

    def meet(self):
        piece = self.order(lambda *values: self.total(values), *[term for term, _ in self.terms])
        count = self.ways["z"]
        self.groups = [piece] + [rotate(piece, "z", count, by) for by in range(1, count)]

    def spread(self):
        quarter = self.order(lambda *groups: arrange(list(groups), "z", 0), *self.groups)
        quarter = quarter.reshape(self.rows // self.ways["y"], self.width)
        self.quarters = [quarter, rotate(quarter, "y", 2, 1)]

    def cross(self):
        self.quarters += [rotate(quarter, "core", 2, 1) for quarter in self.quarters]


class Pair(Chunk):
    def __init__(self, one, two):
        self.order, self.ways, self.rows = one.order, one.ways, one.rows
        self.width = one.width + two.width
        self.halves = (one, two)
        self.left = list(one.left)
        self.split = len(one.terms)
        self.terms = None

    def scatter(self, axis):
        if self.terms is not None:
            super().scatter(axis)
            return
        one, two = self.halves
        me, count = lax.axis_index(axis), self.ways[axis]
        dim = self.left.index(axis)
        values = [term for term, _ in one.terms + two.terms]

        def joined(values, spot):
            parts = [
                side.total(values[at : at + self.split], (dim, spot))
                for side, at in ((one, 0), (two, self.split))
            ]
            return jnp.concatenate(parts, axis=-1)

        def step(*values):
            sends = [joined(values, lax.rem(me + by, count)) for by in range(1, count)]
            return sends + [joined(values, me)]

        *outs, own = self.order(step, *values)
        got = [rotate(out, axis, count, by) for by, out in enumerate(outs, start=1)]
        self.terms = [(own, ())] + [(g, ()) for g in got]
        self.left.remove(axis)


def body(sizes, *args):
    (
        x_in,
        conv_w,
        conv_b,
        ln_gain,
        ln_bias,
        up_w,
        up_b,
        down_w,
        down_b,
        readout,
        cotangent,
        masked,
        species,
    ) = args
    n_z, n_y, n_core, n_tp = sizes
    layers, part, taps, size = conv_w.shape
    windows, _, length = x_in.shape
    mine = windows // n_tp
    planes = taps + 2
    me, my_y, my_core, my_z = (lax.axis_index(axis) for axis in ("tp", "y", "core", "z"))
    where = jnp.stack([me, my_y, my_core, my_z]).astype(jnp.int32)
    quarter = part // 4
    order = Order()
    conv_t = jnp.transpose(conv_w, (0, 2, 1, 3))

    vmem = pl.BlockSpec(memory_space=pltpu.VMEM)
    z_split = n_z if quarter // n_z >= 16 else 1
    up_t, first_share, second_share = order(
        pl.pallas_call(
            functools.partial(pack_kernel, layers),
            in_specs=[smem_spec(), any_spec(), vmem, any_spec()],
            out_specs=[vmem] * 3,
            out_shape=[
                struct((layers, part, size), BF),
                struct((planes, quarter, size), BF),
                struct((planes, quarter // z_split, size), BF),
            ],
            scratch_shapes=[pltpu.SemaphoreType.DMA((2 * layers,))],
            compiler_params=params(),
            name="pack_shares",
        ),
        where,
        conv_t,
        up_w,
        down_w,
    )

    def to_send(value):
        cut = value.reshape(n_tp, mine, part, length)
        return [pick(cut, me if by == 0 else lax.rem(me + by, n_tp), 0) for by in range(n_tp)]

    def exchange(sends, *after):
        return [
            rotate(tie(piece, *after), "tp", n_tp, by) for by, piece in enumerate(sends, start=1)
        ]

    def beside_quarter(own):
        return [own, rotate(own, "y", 2, 1)]

    def four_quarters(pair, *after):
        return pair + [rotate(tie(piece, *after), "core", 2, 1) for piece in pair]

    second_got = [rotate(second_share, "tp", n_tp, by) for by in range(1, n_tp)]
    first_got = [rotate(tie(first_share, *second_got), "tp", n_tp, by) for by in range(1, n_tp)]

    columns = []
    for layer in range(layers):
        columns += [
            conv_b[layer],
            ln_gain[layer, 0],
            ln_bias[layer, 0],
            up_b[layer],
            down_b[layer],
            ln_gain[layer, 1],
            ln_bias[layer, 1],
            jnp.zeros((part,), BF),
        ]
    table = jnp.concatenate([jnp.stack(columns), jnp.transpose(readout)])
    table = jnp.pad(table, ((0, 2), (0, 0)))
    table = arrange(
        [table] + [rotate(table, "tp", n_tp, by) for by in range(1, n_tp)], "tp", 1
    ).reshape(table.shape[0], size)
    pc = jnp.transpose(table[: layers * COLUMNS]).astype(F32)
    read_rows = table[layers * COLUMNS :]

    early = mine // 2 if mine >= 4 else mine
    x_send = order(to_send, x_in)
    x_early = exchange([piece[:early] for piece in x_send[1:]], *first_got)
    x_late = x_early
    if early < mine:
        x_late = exchange([piece[early:] for piece in x_send[1:]], *x_early)
    first_pairs = [beside_quarter(got) for got in first_got]
    first_parts = [piece for pair in first_pairs for piece in four_quarters(pair, pair[1])]
    second_pairs = []
    for got in second_got:
        if z_split > 1:
            groups = [got] + [rotate(got, "z", n_z, by) for by in range(1, n_z)]
            groups[0] = tie(got, *[pair[1] for pair in first_pairs])
            got = order(lambda *groups: arrange(list(groups), "z", 1), *groups)
            got = got.reshape(planes, quarter, size)
        second_pairs.append(beside_quarter(got))
    cot_send = order(to_send, cotangent)
    cot_pieces = [cot_send[0]] + exchange(cot_send[1:], *x_late)

    window = (mine, size, length)
    piece_shape = (mine, part, length)
    n_pieces = 4 * (n_tp - 1)
    kept_struct = [struct(window, BF)] * 8
    w_struct = struct((planes, size, size), BF)
    fwd_scratch = [
        pltpu.VMEM((size, length), BF),
        pltpu.VMEM((taps, size, length), BF),
    ] + [pltpu.VMEM((size, length // HALVES), F32)] * (2 * HALVES)
    load_scratch = [
        pltpu.VMEM((planes, size, size), BF),
        pltpu.SemaphoreType.DMA((3 + n_pieces,)),
        pltpu.SemaphoreType.DMA,
    ]
    conv_flops = 2.0 * taps * size * size * length * mine
    ff_flops = 4.0 * size * size * length * mine
    weight_specs = [smem_spec(), whole_spec(pc.shape)] + [any_spec()] * (3 + n_pieces)
    first = order(
        pl.pallas_call(
            functools.partial(first_early_kernel, 0, n_tp, n_pieces, taps),
            grid=(early,),
            in_specs=weight_specs + [window_spec(piece_shape)] * n_tp,
            out_specs=[window_spec(window)] * 9 + [any_spec()],
            out_shape=kept_struct + [struct(window, BF), w_struct],
            scratch_shapes=fwd_scratch + load_scratch,
            compiler_params=params(),
            cost_estimate=cost((conv_flops + ff_flops) / 2, 20e6),
            name="forward_first_early",
        ),
        where,
        pc,
        conv_t,
        up_t,
        down_w,
        *first_parts,
        x_send[0],
        *x_early,
    )
    w0 = first[9]
    *kept0, hidden = first[:9]
    second_parts = [p for pair in second_pairs for p in four_quarters(pair, hidden)]
    if early < mine:
        *kept0, hidden = order(
            pl.pallas_call(
                functools.partial(first_late_kernel, 0, n_tp, taps, 9),
                grid=(mine - early,),
                in_specs=[smem_spec(), whole_spec(pc.shape), whole_spec(w_struct.shape)]
                + [window_spec(piece_shape, early)]
                + [window_spec(piece_shape)] * (n_tp - 1)
                + [any_spec()] * 9,
                out_specs=[window_spec(window, early)] * 9,
                out_shape=kept_struct + [struct(window, BF)],
                scratch_shapes=fwd_scratch,
                input_output_aliases={3 + n_tp + at: at for at in range(9)},
                compiler_params=params(),
                cost_estimate=cost((conv_flops + ff_flops) / 2, 20e6),
                name="forward_first_late",
            ),
            where,
            pc,
            w0,
            x_send[0],
            *x_late,
            *first[:9],
        )

    mask_rows = lax.dynamic_slice_in_dim(masked, me * mine, mine, 0).reshape(mine, 1, length)
    split = taps // 2
    low_taps, high_taps = tuple(range(split)), tuple(range(split, taps))
    skip = 2 * size + 128
    low_struct = struct((n_tp, part // 2, skip + split * size), BF)
    high_struct = struct((n_tp, part // 2, (taps - split) * size), BF)
    chain_out_specs = [window_spec(window)] * 2 + [
        whole_spec((2, size, size)),
        whole_spec((size, 128)),
    ]
    chain_out = [struct(window, BF)] * 2 + [
        struct((2, size, size), F32),
        struct((size, 128), F32),
    ]
    half_scratch = [pltpu.VMEM((size, length // HALVES), F32)] * HALVES
    chain_scratch = [
        pltpu.VMEM((size, length), BF),
        pltpu.VMEM((size, length), BF),
        pltpu.VMEM((7, size, 128), F32),
    ]
    wide_scratch = [pltpu.VMEM((taps, size, length), BF)]
    ff_specs = [plane_spec((1, size, size), taps), plane_spec((1, size, size), taps + 1)]
    conv_spec = plane_spec((taps, size, size), 0)
    kinds = lax.dynamic_slice_in_dim(species, me * mine, mine, 0)
    *y_pieces, dc1, dm1, ff1, small1, w1 = order(
        pl.pallas_call(
            functools.partial(second_kernel, 1, n_tp, n_pieces, taps),
            grid=(mine,),
            in_specs=weight_specs
            + [window_spec(window), whole_spec(read_rows.shape), window_spec((mine, 1, length))]
            + [smem_spec()]
            + [window_spec(piece_shape)] * n_tp,
            out_specs=[window_spec(piece_shape)] * n_tp
            + chain_out_specs
            + [any_spec()],
            out_shape=[struct(piece_shape, BF)] * n_tp
            + chain_out
            + [w_struct],
            scratch_shapes=fwd_scratch
            + [pltpu.VMEM((1, size, length), BF)] * 7
            + chain_scratch
            + [pltpu.VMEM((8 * SPECIES, 128), F32)]
            + load_scratch,
            compiler_params=params(),
            cost_estimate=cost(conv_flops + 3 * ff_flops, 20e6),
            name="second_layer",
        ),
        where,
        pc,
        conv_t,
        up_t,
        down_w,
        *second_parts,
        hidden,
        read_rows,
        mask_rows,
        kinds,
        *cot_pieces,
    )

    def chunk(layer, chosen, shape, dc, a, rest, name):
        keep, send = order(
            pl.pallas_call(
                functools.partial(weight_kernel, layer, taps, chosen),
                in_specs=[smem_spec()] + [vmem] * (2 + len(rest)),
                out_specs=[vmem] * 2,
                out_shape=[shape] * 2,
                scratch_shapes=[pltpu.VMEM((2, size, size), F32)],
                compiler_params=params(),
                cost_estimate=cost(conv_flops * len(chosen) / taps, 10e6),
                name=name,
            ),
            where,
            dc,
            a,
            *rest,
        )
        return Chunk(order, sizes, keep, send)

    low1 = chunk(1, low_taps, low_struct, dc1, hidden, (ff1, small1), "weights_second_low")
    high1 = chunk(1, high_taps, high_struct, dc1, hidden, (), "weights_second_high")
    low1.scatter("tp")
    high1.scatter("tp")

    dc0, dm0, ff0, small0 = order(
        pl.pallas_call(
            functools.partial(middle_kernel, 0, taps),
            grid=(mine,),
            in_specs=[conv_spec] + ff_specs + [whole_spec(pc.shape)] + [window_spec(window)] * 9,
            out_specs=chain_out_specs,
            out_shape=chain_out,
            scratch_shapes=wide_scratch + half_scratch + chain_scratch + half_scratch,
            compiler_params=params(),
            cost_estimate=cost(conv_flops + 2 * ff_flops, 20e6),
            name="chain_first",
        ),
        w1,
        w0,
        w0,
        pc,
        dc1,
        dm1,
        *kept0[1:],
    )
    y_back = [y_pieces[0]] + [
        rotate(tie(y_pieces[by], high1.terms[2][0]), "tp", n_tp, by) for by in range(1, n_tp)
    ]
    both1 = Pair(low1, high1)
    both1.scatter("y")
    high0 = chunk(0, high_taps, high_struct, dc0, kept0[0], (), "weights_first_high")
    low0 = chunk(0, low_taps, low_struct, dc0, kept0[0], (ff0, small0), "weights_first_low")
    both1.scatter("z")
    y_out = order(lambda *pieces: arrange(list(pieces), "tp", 0), *y_back)
    y_out = y_out.reshape(windows, part, length)
    high0.scatter("tp")
    low0.scatter("y")
    x_grads = order(
        pl.pallas_call(
            functools.partial(bottom_kernel, 0, taps, n_tp),
            grid=(mine,),
            in_specs=[smem_spec(), conv_spec] + [window_spec(window)] * 2,
            out_specs=[window_spec(piece_shape)] * n_tp,
            out_shape=[struct(piece_shape, F32)] + [struct(piece_shape, BF)] * (n_tp - 1),
            scratch_shapes=wide_scratch + [pltpu.VMEM((size, length), F32)],
            compiler_params=params(),
            cost_estimate=cost(conv_flops, 15e6),
            name="input_grad",
        ),
        where,
        w0,
        dc0,
        dm0,
    )
    high0.scatter("y")
    low0.scatter("tp")
    both1.meet()
    low0.scatter("z")
    x_back = [x_grads[0]] + [
        rotate(tie(x_grads[by], low0.terms[3][0]), "tp", n_tp, by) for by in range(1, n_tp)
    ]
    high0.scatter("z")
    both1.spread()
    low0.meet()
    high0.meet()
    both1.cross()
    low0.spread()

    conv_struct = struct((layers, taps, part, size), F32)

    grad_conv, rest1 = order(
        pl.pallas_call(
            functools.partial(settle_rest_kernel, 1),
            in_specs=[smem_spec()] + [vmem] * 4,
            out_specs=[any_spec(), vmem],
            out_shape=[conv_struct, struct((part, skip), F32)],
            scratch_shapes=[
                pltpu.VMEM((4, taps, quarter, size), F32),
                pltpu.SemaphoreType.DMA((4,)),
            ],
            compiler_params=params(),
            name="settle_second",
        ),
        where,
        *both1.quarters,
    )
    grad_x = order(
        lambda *pieces: arrange([piece.astype(F32) for piece in pieces], "tp", 0), *x_back
    ).reshape(windows, part, length)
    high0.spread()
    low0.cross()
    high0.cross()
    grad_conv, grad_up_w, grad_down_w, g_conv_b, g_gain, g_bias, g_up_b, g_down_b = order(
        pl.pallas_call(
            functools.partial(settle_last_kernel, 0, split),
            in_specs=[smem_spec()] + [vmem] * 9 + [any_spec()],
            out_specs=[any_spec()] + [vmem] * 7,
            out_shape=[
                conv_struct,
                struct((layers, size, part), F32),
                struct((layers, part, size), F32),
                struct((layers, part), F32),
                struct((layers, 2, part), F32),
                struct((layers, 2, part), F32),
                struct((layers, part), F32),
                struct((layers, part), F32),
            ],
            scratch_shapes=[
                pltpu.VMEM((part, skip), F32),
                pltpu.VMEM((4, split, quarter, size), F32),
                pltpu.VMEM((4, taps - split, quarter, size), F32),
                pltpu.SemaphoreType.DMA((4,)),
                pltpu.SemaphoreType.DMA((4,)),
            ],
            input_output_aliases={10: 0},
            compiler_params=params(),
            name="settle_last",
        ),
        where,
        *low0.quarters,
        *high0.quarters,
        rest1,
        grad_conv,
    )

    grad_conv_w = jnp.transpose(grad_conv, (0, 2, 1, 3))
    species_sum = rest1[: 8 * SPECIES, 2 * size + 7].reshape(SPECIES, 8)[:, :CLASSES] / length
    return (
        y_out,
        grad_x,
        grad_conv_w,
        g_conv_b,
        g_gain,
        g_bias,
        grad_up_w,
        g_up_b,
        grad_down_w,
        g_down_b,
        species_sum,
    )


def solution(mesh):
    dp, tp = mesh.shape["dp"], mesh.shape["tp"]
    n_core = n_y = 2
    n_z = dp // (n_core * n_y)
    fine = Mesh(mesh.devices.reshape(n_z, n_y, n_core, tp), DP + ("tp",))
    placed = (
        P(DP, "tp", None),
        P(None, "tp", None, None),
        P(None, "tp"),
        P(None, None, "tp"),
        P(None, None, "tp"),
        P(None, None, "tp"),
        P(None, "tp"),
        P(None, "tp", None),
        P(None, "tp"),
        P("tp", None),
        P(DP, "tp", None),
        P(DP, None),
        P(DP),
    )
    return jax.shard_map(
        functools.partial(body, (n_z, n_y, n_core, tp)),
        mesh=fine,
        in_specs=placed,
        out_specs=(
            P(DP, "tp", None),
            P(DP, "tp", None),
            P(None, "tp", None, None),
            P(None, "tp"),
            P(None, None, "tp"),
            P(None, None, "tp"),
            P(None, None, "tp"),
            P(None, "tp"),
            P(None, "tp", None),
            P(None, "tp"),
            P(),
        ),
        check_vma=False,
    )
```

```python
import functools

import jax
import jax.numpy as jnp
from jax import lax
from jax.experimental import pallas as pl
from jax.experimental.pallas import tpu as pltpu
from jax.sharding import Mesh
from jax.sharding import PartitionSpec as P

DILATIONS = (2, 32)
SPECIES = 8
CLASSES = 6
EPS = 1e-05
BF = jnp.bfloat16
F32 = jnp.float32
DP = ("zh", "zl", "y", "core")
STEP = 32
HALVES = 2
VMEM_BYTES = 58 * 2**20
CONV_B, GAIN_A, BIAS_A, UP_B, DOWN_B, GAIN_B, BIAS_B = range(7)
COLUMNS = 8


def shifted(rows, by):
    if by == 0:
        return rows
    blank = jnp.zeros((rows.shape[0], abs(by)), rows.dtype)
    if by > 0:
        return jnp.concatenate([rows[:, by:], blank], axis=1)
    return jnp.concatenate([blank, rows[:, :by]], axis=1)


def fold(tile):
    return sum(tile[at : at + 8] for at in range(0, tile.shape[0], 8))


def fold_lanes(tile):
    return sum(tile[:, at : at + 128] for at in range(0, tile.shape[1], 128))


def gelu_pair(x):
    cdf = 0.5 + 0.5 * lax.erf(x * 0.7071067811865476)
    return x * cdf, cdf + x * jnp.exp(-0.5 * x * x) * 0.3989422804014327


def nn(left, right):
    return jnp.dot(left, right, preferred_element_type=F32)


def tn(left, right):
    return lax.dot_general(left, right, (((0,), (0,)), ((), ())), preferred_element_type=F32)


def nt(left, right):
    return lax.dot_general(left, right, (((1,), (1,)), ((), ())), preferred_element_type=F32)


def steps(size):
    return [slice(at, at + STEP) for at in range(0, size, STEP)]


def place(pieces, me, target):
    ways = len(pieces)
    for back, piece in enumerate(pieces):
        size = piece.shape[1]
        spot = lax.rem(me + (ways - back), ways) * size
        target[pl.ds(pl.multiple_of(spot, size), size), :] = piece[0]


def norm_stats(total, square, width):
    mean = jnp.sum(total, axis=0, keepdims=True) / width
    var = jnp.sum(square, axis=0, keepdims=True) / width - mean * mean
    return mean, lax.rsqrt(var + EPS)


def activate_and_sum(pre, col, pc, slope_ref, span):
    size, length = pre.shape
    total = jnp.zeros((8, length), F32)
    square = jnp.zeros((8, length), F32)
    for rows in steps(size):
        value, slope = gelu_pair(pre[rows, :] + pc[rows, col : col + 1])
        pre[rows, :] = value
        slope_ref[0, rows, span] = slope.astype(BF)
        total = total + fold(value)
        square = square + fold(value * value)
    return norm_stats(total, square, size)


def load_weights(layer, where, blocks, pieces, full, w, sems, out_sem):
    tp, y, core = where[0], where[1], where[2]
    conv, up, down = blocks
    taps, part = conv.shape[1], conv.shape[2]
    ways = w.shape[1] // part
    here = pl.program_id(0)

    def rows(owner, at, count):
        return pl.ds(pl.multiple_of(owner * part + at, count), count)

    @pl.when(here == 0)
    def _():
        own = rows(tp, 0, part)
        copies = [
            (conv.at[layer], w.at[0:taps, own]),
            (up.at[layer], w.at[taps, own]),
            (down.at[layer], w.at[taps + 1, own]),
        ]
        quarter = part // 4
        for back in range(1, ways):
            owner = lax.rem(tp + (ways - back), ways)
            for flip in range(4):
                c = core if flip < 2 else 1 - core
                at = c * (2 * quarter) + (y if flip % 2 == 0 else 1 - y) * quarter
                copies.append((pieces[4 * (back - 1) + flip], w.at[:, rows(owner, at, quarter)]))
        moves = [pltpu.make_async_copy(src, dst, sems.at[i]) for i, (src, dst) in enumerate(copies)]
        for move in moves:
            move.start()
        for move in moves:
            move.wait()
        pltpu.make_async_copy(w, full, out_sem).start()

    @pl.when(here == pl.num_programs(0) - 1)
    def _():
        pltpu.make_async_copy(w, full, out_sem).wait()


def first_early_kernel(layer, n_in, n_pieces, taps, *refs):
    where, pc = refs[:2]
    blocks, parts = refs[2:5], refs[5 : 5 + n_pieces]
    at = 5 + n_pieces
    pieces = refs[at : at + n_in]
    at += n_in
    *kept, out = refs[at : at + 9]
    full = refs[at + 9]
    *work, w, sems, out_sem = refs[at + 10 :]
    load_weights(layer, where, blocks, parts, full, w, sems, out_sem)
    forward_window(layer, taps, where, pc, w, pieces, kept, work)
    out[0] = work[0][...]


def first_late_kernel(layer, n_in, taps, n_before, where, pc, w, *refs):
    pieces, refs = refs[:n_in], refs[n_in + n_before :]
    *kept, out = refs[:9]
    work = refs[9:]
    forward_window(layer, taps, where, pc, w, pieces, kept, work)
    out[0] = work[0][...]


def second_kernel(layer, n_in, n_pieces, taps, *refs):
    where, pc = refs[:2]
    blocks, parts = refs[2:5], refs[5 : 5 + n_pieces]
    at = 5 + n_pieces
    hidden, readout, mask_ref, kinds = refs[at : at + 4]
    cots = refs[at + 4 : at + 4 + n_in]
    at += 4 + n_in
    y_refs = refs[at : at + n_in]
    dc_ref, dm_ref, ff_sum, small, full = refs[at + n_in : at + n_in + 5]
    refs = refs[at + n_in + 5 :]
    act, wide, *pairs = refs[: 2 + 2 * HALVES]
    kept = refs[2 + 2 * HALVES : 9 + 2 * HALVES]
    low, high, row_sums, shares, w, sems, out_sem = refs[9 + 2 * HALVES :]
    load_weights(layer, where, blocks, parts, full, w, sems, out_sem)
    here = pl.program_id(0)
    clear(here == 0, ff_sum, row_sums, shares)
    forward_window(layer, taps, where, pc, w, (hidden,), (None,) + kept, (act, wide, *pairs))
    me = where[0]
    part = act.shape[0] // n_in
    for ahead, ref in enumerate(y_refs):
        spot = lax.rem(me + ahead, n_in) * part
        ref[0] = act[pl.ds(pl.multiple_of(spot, part), part), :]
    logits = nn(readout[...], act[...])
    seat = lax.broadcasted_iota(jnp.int32, logits.shape, 0)
    logits = jnp.where(seat < CLASSES, logits, -1e30)
    raised = jnp.exp(logits - jnp.max(logits, axis=0, keepdims=True))
    chance = raised / jnp.sum(raised, axis=0, keepdims=True)
    chance = fold_lanes(chance * mask_ref[0].astype(F32))
    for kind in range(SPECIES):
        shares[8 * kind : 8 * kind + 8, :] += jnp.where(kinds[here] == kind, chance, 0.0)
    grads = pairs[HALVES:]
    for back, piece in enumerate(cots):
        spot = pl.multiple_of(lax.rem(me + (n_in - back), n_in) * part, part)
        for at, grad in enumerate(grads):
            width = grad.shape[1]
            grad[pl.ds(spot, part), :] = piece[0, :, at * width : (at + 1) * width].astype(F32)
    up, down = w.at[pl.ds(taps, 1)], w.at[pl.ds(taps + 1, 1)]
    outs = (dc_ref, dm_ref, ff_sum)
    chain(layer, grads, kept, up, down, pc, outs, (low, high, row_sums, *pairs[:HALVES]))

    @pl.when(here == pl.num_programs(0) - 1)
    def _():
        close(row_sums, small, shares, part)


def forward_window(layer, taps, where, pc, w, pieces, kept, work):
    a_ref, b_ref, n1_ref, s1_ref, su_ref, v_ref, s2_ref, n2_ref = kept
    act, wide, *pairs = work
    size, length = act.shape
    base = layer * COLUMNS
    half = taps // 2
    width = length // HALVES
    spans = [slice(at, at + width) for at in range(0, length, width)]
    pres, mids = pairs[:HALVES], pairs[HALVES:]
    place(pieces, where[0], act)
    if a_ref is not None:
        a_ref[0] = act[...]
    for tap in range(taps):
        wide[tap] = shifted(act[...], (tap - half) * DILATIONS[layer])

    def convolve(pre, span):
        total = nn(w[0], wide[0, :, span])
        for tap in range(1, taps):
            total = total + nn(w[tap], wide[tap, :, span])
        pre[...] = total

    def first_norm(pre, mid, span):
        mean, inv = activate_and_sum(pre, base + CONV_B, pc, s1_ref, span)
        for rows in steps(size):
            normed = (pre[rows, :] - mean) * inv
            m = (
                act[rows, span].astype(F32)
                + normed * pc[rows, base + GAIN_A : base + GAIN_A + 1]
                + pc[rows, base + BIAS_A : base + BIAS_A + 1]
            )
            n1_ref[0, rows, span] = normed.astype(BF)
            s1_ref[0, rows, span] = (s1_ref[0, rows, span].astype(F32) * inv).astype(BF)
            mid[rows, :] = m
            b_ref[0, rows, span] = m.astype(BF)

    def hidden(pre, span):
        for rows in steps(size):
            value, slope = gelu_pair(pre[rows, :] + pc[rows, base + UP_B : base + UP_B + 1])
            v_ref[0, rows, span] = value.astype(BF)
            su_ref[0, rows, span] = slope.astype(BF)

    def second_norm(pre, mid, span):
        mean, inv = activate_and_sum(pre, base + DOWN_B, pc, s2_ref, span)
        for rows in steps(size):
            normed = (pre[rows, :] - mean) * inv
            out = (
                mid[rows, :]
                + normed * pc[rows, base + GAIN_B : base + GAIN_B + 1]
                + pc[rows, base + BIAS_B : base + BIAS_B + 1]
            )
            n2_ref[0, rows, span] = normed.astype(BF)
            s2_ref[0, rows, span] = (s2_ref[0, rows, span].astype(F32) * inv).astype(BF)
            act[rows, span] = out.astype(BF)

    for pre, span in zip(pres, spans):
        convolve(pre, span)
    for pre, mid, span in zip(pres, mids, spans):
        first_norm(pre, mid, span)
        pre[...] = nn(w[taps], b_ref[0, :, span])
        hidden(pre, span)
        pre[...] = tn(w[taps + 1], v_ref[0, :, span])
        second_norm(pre, mid, span)

def clear(first, *sums):
    @pl.when(first)
    def _():
        for ref in sums:
            ref[...] = jnp.zeros_like(ref)


def close(row_sums, small_ref, shares=None, part=0):
    for rows in steps(small_ref.shape[0]):
        seat = lax.broadcasted_iota(jnp.int32, (STEP, 128), 1)
        table = jnp.zeros((STEP, 128), F32)
        for slot in range(7):
            column = jnp.sum(row_sums[slot, rows, :], axis=1, keepdims=True)
            table = jnp.where(seat == slot, column, table)
        if shares is not None and rows.start % part < 8 * SPECIES:
            at = rows.start % part
            column = jnp.sum(shares[at : at + STEP, :], axis=1, keepdims=True)
            table = jnp.where(seat == 7, column, table)
        small_ref[rows, :] = table


def chain(layer, grads, kept, up, down, pc, outs, work):
    b_ref, n1_ref, s1_ref, su_ref, v_ref, s2_ref, n2_ref = kept
    dc_ref, dm_ref, ff_sum = outs
    low, high, row_sums, *pres = work
    size, width = pres[0].shape
    base = layer * COLUMNS
    spans = [slice(at, at + width) for at in range(0, low.shape[1], width)]

    def back(grad, span, gain_col, normed_ref, slope_ref, slot, target):
        total = jnp.zeros((8, width), F32)
        cross = jnp.zeros((8, width), F32)
        for rows in steps(size):
            g = grad[rows, :]
            product = g * normed_ref[0, rows, span].astype(F32)
            row_sums[slot + 1, rows, :] += fold_lanes(product)
            row_sums[slot + 2, rows, :] += fold_lanes(g)
            gain = pc[rows, gain_col : gain_col + 1]
            total = total + fold(g * gain)
            cross = cross + fold(product * gain)
        mean_q = jnp.sum(total, axis=0, keepdims=True) / size
        mean_qn = jnp.sum(cross, axis=0, keepdims=True) / size
        for rows in steps(size):
            q = grad[rows, :] * pc[rows, gain_col : gain_col + 1]
            normed = normed_ref[0, rows, span].astype(F32)
            d = slope_ref[0, rows, span].astype(F32) * (q - mean_q - normed * mean_qn)
            row_sums[slot, rows, :] += fold_lanes(d)
            target[rows, span] = d.astype(BF)

    for grad, pre, span in zip(grads, pres, spans):
        back(grad, span, base + GAIN_B, n2_ref, s2_ref, DOWN_B, low)
        pre[...] = nn(down[0], low[:, span])
        for rows in steps(size):
            du = pre[rows, :] * su_ref[0, rows, span].astype(F32)
            row_sums[UP_B, rows, :] += fold_lanes(du)
            high[rows, span] = du.astype(BF)
        pre[...] = tn(up[0], high[:, span])
        for rows in steps(size):
            dm = grad[rows, :] + pre[rows, :]
            grad[rows, :] = dm
            dm_ref[0, rows, span] = dm.astype(BF)
        back(grad, span, base + GAIN_A, n1_ref, s1_ref, CONV_B, dc_ref.at[0])
    ff_sum[0] += nt(high[...], b_ref[0])
    ff_sum[1] += nt(v_ref[0], low[...])


def conv_back(layer, taps, dc, dm_ref, w, wide, grads):
    half = taps // 2
    width = grads[0].shape[1]
    for tap in range(taps):
        wide[tap] = shifted(dc, -(tap - half) * DILATIONS[layer])
    for at, grad in enumerate(grads):
        span = slice(at * width, (at + 1) * width)
        total = tn(w[0], wide[0, :, span])
        for tap in range(1, taps):
            total = total + tn(w[tap], wide[tap, :, span])
        grad[...] = total + dm_ref[0, :, span].astype(F32)


def middle_kernel(layer, taps, *refs):
    above_w, up, down, pc, dc_in, dm_in = refs[:6]
    kept = refs[6:13]
    dc_ref, dm_ref, ff_sum, small = refs[13:17]
    wide, grads = refs[17], refs[18 : 18 + HALVES]
    low, high, row_sums, *pres = refs[18 + HALVES :]
    here = pl.program_id(0)
    clear(here == 0, ff_sum, row_sums)
    conv_back(layer + 1, taps, dc_in[0], dm_in, above_w, wide, grads)
    outs = (dc_ref, dm_ref, ff_sum)
    chain(layer, grads, kept, up, down, pc, outs, (low, high, row_sums, *pres))

    @pl.when(here == pl.num_programs(0) - 1)
    def _():
        close(row_sums, small)


def bottom_kernel(layer, taps, n_out, where, w, dc_in, dm_in, own_ref, *refs):
    others = refs[: n_out - 1]
    wide, *grads = refs[n_out - 1 :]
    conv_back(layer, taps, dc_in[0], dm_in, w, wide, grads)
    me = where[0]
    part = own_ref.shape[1]
    for at, grad in enumerate(grads):
        width = grad.shape[1]
        span = slice(at * width, (at + 1) * width)
        own_ref[0, :, span] = grad[pl.ds(pl.multiple_of(me * part, part), part), :]
        for ahead, ref in enumerate(others, start=1):
            spot = pl.multiple_of(lax.rem(me + ahead, n_out) * part, part)
            ref[0, :, span] = grad[pl.ds(spot, part), :].astype(BF)


def weight_part(layer, taps, chosen, core, dc, a, rest, keep, send, total):
    half = taps // 2
    blocks, rows, _ = keep.shape
    size = total.shape[1]

    def put(source, at, width):
        for block in range(blocks):
            first = block * 2 * rows
            mine = pl.multiple_of(first + core * rows, rows)
            other = pl.multiple_of(first + (1 - core) * rows, rows)
            keep[block, :, at : at + width] = source[pl.ds(mine, rows), :].astype(BF)
            send[block, :, at : at + width] = source[pl.ds(other, rows), :].astype(BF)

    skip = 0
    if rest:
        ff, small = rest
        put(ff.at[0], 0, size)
        put(ff.at[1], size, size)
        put(small, 2 * size, small.shape[1])
        skip = 2 * size + small.shape[1]
    for at, tap in enumerate(chosen):
        by = -(tap - half) * DILATIONS[layer]
        acc = None
        for window in range(dc.shape[0]):
            part = nt(shifted(dc[window], by), a[window])
            acc = part if acc is None else acc + part
        total[at % 2] = acc
        put(total.at[at % 2], skip + at * size, size)


def weight_kernel(layer, taps, chosen, where, dc, a, *refs):
    rest, (keep, send, total) = refs[:-3], refs[-3:]
    weight_part(layer, taps, chosen, where[2], dc, a, rest, keep, send, total)


def pack_kernel(layers, where, conv, up, down, up_t, *refs):
    shares, sems = refs[:layers], refs[layers]
    tp, y, core, z = where[0], where[1], where[2], where[3]
    taps = conv.shape[1]
    moves = []
    for layer in range(layers):
        count = shares[layer].shape[1]
        quarter = up.shape[2] // 4
        at = core * (2 * quarter) + y * quarter
        if count < quarter:
            at = at + z * count
        rows = pl.ds(pl.multiple_of(at, count), count)
        moves.append((conv.at[layer, :, rows], shares[layer].at[0:taps]))
        moves.append((down.at[layer, rows], shares[layer].at[taps + 1]))
    moves = [pltpu.make_async_copy(src, dst, sems.at[i]) for i, (src, dst) in enumerate(moves)]
    for move in moves:
        move.start()
    for layer in range(layers):
        up_t[layer] = jnp.transpose(up[layer])
    for layer in range(layers):
        count = shares[layer].shape[1]
        quarter = up.shape[2] // 4
        at = core * (2 * quarter) + y * quarter
        if count < quarter:
            at = at + z * count
        shares[layer][taps] = up_t[layer, pl.ds(pl.multiple_of(at, count), count), :]
    for move in moves:
        move.wait()


def settle_conv(layer, first_tap, where, pieces, out, wide, sems, skip):
    count, rows, size = wide.shape[1:]
    moves = []
    for flip, piece in enumerate(pieces):
        c = where[2] if flip < 2 else 1 - where[2]
        y = where[1] if flip % 2 == 0 else 1 - where[1]
        at = pl.multiple_of(c * (2 * rows) + y * rows, rows)
        for tap in range(count):
            begin = skip + tap * size
            wide[flip, tap] = piece[:, begin : begin + size].astype(F32)
        target = out.at[layer, first_tap : first_tap + count, pl.ds(at, rows)]
        moves.append(pltpu.make_async_copy(wide.at[flip], target, sems.at[flip]))
        moves[-1].start()
    return moves


def settle_rest_kernel(layer, where, *refs):
    pieces = refs[:4]
    out, rest, wide, sems = refs[4:]
    skip = rest.shape[1]
    moves = settle_conv(layer, 0, where, pieces, out, wide, sems, skip)
    rows = pieces[0].shape[0]
    for flip, piece in enumerate(pieces):
        c = where[2] if flip < 2 else 1 - where[2]
        y = where[1] if flip % 2 == 0 else 1 - where[1]
        at = pl.multiple_of(c * (2 * rows) + y * rows, rows)
        rest[pl.ds(at, rows), :] = piece[:, :skip].astype(F32)
    for move in moves:
        move.wait()


def settle_last_kernel(layer, split, where, *refs):
    low, high, (other,) = refs[:4], refs[4:8], refs[8:9]
    out, up, down, conv_b, gain, bias, up_b, down_b = refs[10:18]
    rest, wide_low, wide_high, sems_low, sems_high = refs[18:]
    skip = rest.shape[1]
    moves = settle_conv(layer, 0, where, low, out, wide_low, sems_low, skip)
    moves += settle_conv(layer, split, where, high, out, wide_high, sems_high, 0)
    rows = low[0].shape[0]
    for flip, piece in enumerate(low):
        c = where[2] if flip < 2 else 1 - where[2]
        y = where[1] if flip % 2 == 0 else 1 - where[1]
        at = pl.multiple_of(c * (2 * rows) + y * rows, rows)
        rest[pl.ds(at, rows), :] = piece[:, :skip].astype(F32)
    size = down.shape[2]
    for at_layer, source in ((layer, rest), (1 - layer, other)):
        one = slice(at_layer, at_layer + 1)
        up[at_layer] = jnp.transpose(source[:, :size])
        down[at_layer] = source[:, size : 2 * size]
        small = jnp.transpose(source[:, 2 * size :])
        conv_b[one, :] = small[CONV_B : CONV_B + 1]
        up_b[one, :] = small[UP_B : UP_B + 1]
        down_b[one, :] = small[DOWN_B : DOWN_B + 1]
        for at, (g, b) in enumerate(((GAIN_A, BIAS_A), (GAIN_B, BIAS_B))):
            gain[at_layer, at : at + 1, :] = small[g : g + 1]
            bias[at_layer, at : at + 1, :] = small[b : b + 1]
    for move in moves:
        move.wait()


def whole_spec(shape):
    return pl.BlockSpec(
        shape, lambda *_: (0,) * len(shape), pipeline_mode=pl.Buffered(buffer_count=1)
    )


def window_spec(shape, first=0):
    return pl.BlockSpec((1,) + shape[1:], lambda i: (i + first,) + (0,) * (len(shape) - 1))


def plane_spec(block, index):
    return pl.BlockSpec(
        block,
        lambda *_: (index,) + (0,) * (len(block) - 1),
        pipeline_mode=pl.Buffered(buffer_count=1),
    )


def any_spec():
    return pl.BlockSpec(memory_space=pl.ANY)


def smem_spec():
    return pl.BlockSpec(memory_space=pltpu.SMEM)


def params():
    return pltpu.CompilerParams(vmem_limit_bytes=VMEM_BYTES)


def cost(flops, nbytes):
    return pl.CostEstimate(flops=int(8 * flops), bytes_accessed=int(nbytes), transcendentals=0)


def struct(shape, dtype):
    return jax.ShapeDtypeStruct(shape, dtype)


def rotate(value, axis, ways, by):
    return lax.ppermute(value, axis, [(i, (i + by) % ways) for i in range(ways)])


def pick(value, index, dim):
    return lax.dynamic_index_in_dim(value, index, dim, keepdims=False)


def tie(value, *after):
    return lax.optimization_barrier((value,) + after)[0]


def add_up(terms):
    return sum(term.astype(F32) for term in terms).astype(BF)


def arrange(pieces, axis, dim):
    me = lax.axis_index(axis)
    ways = len(pieces)
    if ways == 2:
        low = jnp.where(me == 0, pieces[0], pieces[1])
        high = jnp.where(me == 0, pieces[1], pieces[0])
        return jnp.stack([low, high], axis=dim)
    shape = list(pieces[0].shape)
    shape.insert(dim, ways)
    out = jnp.zeros(shape, pieces[0].dtype)
    for back, piece in enumerate(pieces):
        spot = lax.rem(me + (ways - back), ways)
        out = lax.dynamic_update_index_in_dim(out, piece, spot, dim)
    return out


class Order:
    def __init__(self):
        self.last = ()

    def __call__(self, step, *values):
        values = lax.optimization_barrier(values + self.last)[: len(values)]
        result = step(*values)
        self.last = (jax.tree.leaves(result)[0],)
        return result


class Chunk:
    def __init__(self, order, sizes, keep, send):
        self.order = order
        self.ways = dict(zip(DP + ("tp",), sizes))
        blocks, rows, width = keep.shape
        self.rows, self.width = rows, width
        y, zh, zl = self.ways["y"], self.ways["zh"], self.ways["zl"]
        self.shape = (blocks, y, zh, zl, rows // (y * zh * zl), width)
        self.left = ["tp", "y", "zh", "zl"]
        sent = rotate(send, "core", 2, 1)
        self.terms = [(keep.reshape(self.shape), ()), (sent.reshape(self.shape), ())]

    def total(self, values, *last):
        cut = []
        for value, (_, at) in zip(values, self.terms):
            for dim, index in at + last:
                value = pick(value, index, dim)
            cut.append(value)
        return add_up(cut)

    def scatter(self, axis):
        me, count = lax.axis_index(axis), self.ways[axis]
        dim = self.left.index(axis)

        def step(*values):
            return [self.total(values, (dim, lax.rem(me + by, count))) for by in range(1, count)]

        outs = self.order(step, *[term for term, _ in self.terms])
        got = [rotate(out, axis, count, by) for by, out in enumerate(outs, start=1)]
        self.terms = [(term, at + ((dim, me),)) for term, at in self.terms]
        self.terms += [(g, ()) for g in got]
        self.left.remove(axis)

    def meet(self):
        piece = self.order(lambda *values: self.total(values), *[term for term, _ in self.terms])
        count = self.ways["zh"]
        self.groups = [piece] + [rotate(piece, "zh", count, by) for by in range(1, count)]

    def widen(self):
        pieces = self.order(lambda *groups: arrange(list(groups), "zh", 0), *self.groups)
        self.groups = [pieces, rotate(pieces, "zl", 2, 1)]

    def spread(self):
        quarter = self.order(lambda *groups: arrange(list(groups), "zl", 1), *self.groups)
        quarter = quarter.reshape(self.rows // self.ways["y"], self.width)
        self.quarters = [quarter, rotate(quarter, "y", 2, 1)]

    def cross(self):
        self.quarters += [rotate(quarter, "core", 2, 1) for quarter in self.quarters]


class Pair(Chunk):
    def __init__(self, one, two):
        self.order, self.ways, self.rows = one.order, one.ways, one.rows
        self.width = one.width + two.width
        self.halves = (one, two)
        self.left = list(one.left)
        self.split = len(one.terms)
        self.terms = None

    def scatter(self, axis):
        if self.terms is not None:
            super().scatter(axis)
            return
        one, two = self.halves
        me, count = lax.axis_index(axis), self.ways[axis]
        dim = self.left.index(axis)
        values = [term for term, _ in one.terms + two.terms]

        def joined(values, spot):
            parts = [
                side.total(values[at : at + self.split], (dim, spot))
                for side, at in ((one, 0), (two, self.split))
            ]
            return jnp.concatenate(parts, axis=-1)

        def step(*values):
            sends = [joined(values, lax.rem(me + by, count)) for by in range(1, count)]
            return sends + [joined(values, me)]

        *outs, own = self.order(step, *values)
        got = [rotate(out, axis, count, by) for by, out in enumerate(outs, start=1)]
        self.terms = [(own, ())] + [(g, ()) for g in got]
        self.left.remove(axis)


def body(sizes, *args):
    (
        x_in,
        conv_w,
        conv_b,
        ln_gain,
        ln_bias,
        up_w,
        up_b,
        down_w,
        down_b,
        readout,
        cotangent,
        masked,
        species,
    ) = args
    n_zh, n_zl, n_y, n_core, n_tp = sizes
    n_z = n_zh * n_zl
    layers, part, taps, size = conv_w.shape
    windows, _, length = x_in.shape
    mine = windows // n_tp
    planes = taps + 2
    me, my_y, my_core = (lax.axis_index(axis) for axis in ("tp", "y", "core"))
    my_z = lax.axis_index("zh") * n_zl + lax.axis_index("zl")
    where = jnp.stack([me, my_y, my_core, my_z]).astype(jnp.int32)
    quarter = part // 4
    order = Order()
    conv_t = jnp.transpose(conv_w, (0, 2, 1, 3))

    vmem = pl.BlockSpec(memory_space=pltpu.VMEM)
    z_split = n_z if quarter // n_z >= 16 else 1
    up_t, first_share, second_share = order(
        pl.pallas_call(
            functools.partial(pack_kernel, layers),
            in_specs=[smem_spec(), any_spec(), vmem, any_spec()],
            out_specs=[vmem] * 3,
            out_shape=[
                struct((layers, part, size), BF),
                struct((planes, quarter, size), BF),
                struct((planes, quarter // z_split, size), BF),
            ],
            scratch_shapes=[pltpu.SemaphoreType.DMA((2 * layers,))],
            compiler_params=params(),
            name="pack_shares",
        ),
        where,
        conv_t,
        up_w,
        down_w,
    )

    def to_send(value):
        cut = value.reshape(n_tp, mine, part, length)
        return [pick(cut, me if by == 0 else lax.rem(me + by, n_tp), 0) for by in range(n_tp)]

    def exchange(sends, *after):
        return [
            rotate(tie(piece, *after), "tp", n_tp, by) for by, piece in enumerate(sends, start=1)
        ]

    def beside_quarter(own):
        return [own, rotate(own, "y", 2, 1)]

    def four_quarters(pair, *after):
        return pair + [rotate(tie(piece, *after), "core", 2, 1) for piece in pair]

    second_got = [rotate(second_share, "tp", n_tp, by) for by in range(1, n_tp)]
    first_got = [rotate(tie(first_share, *second_got), "tp", n_tp, by) for by in range(1, n_tp)]

    columns = []
    for layer in range(layers):
        columns += [
            conv_b[layer],
            ln_gain[layer, 0],
            ln_bias[layer, 0],
            up_b[layer],
            down_b[layer],
            ln_gain[layer, 1],
            ln_bias[layer, 1],
            jnp.zeros((part,), BF),
        ]
    table = jnp.concatenate([jnp.stack(columns), jnp.transpose(readout)])
    table = jnp.pad(table, ((0, 2), (0, 0)))
    table = arrange(
        [table] + [rotate(table, "tp", n_tp, by) for by in range(1, n_tp)], "tp", 1
    ).reshape(table.shape[0], size)
    pc = jnp.transpose(table[: layers * COLUMNS]).astype(F32)
    read_rows = table[layers * COLUMNS :]

    early = mine // 2 if mine >= 4 else mine
    x_send = order(to_send, x_in)
    x_early = exchange([piece[:early] for piece in x_send[1:]], *first_got)
    x_late = x_early
    if early < mine:
        x_late = exchange([piece[early:] for piece in x_send[1:]], *x_early)
    first_pairs = [beside_quarter(got) for got in first_got]
    first_parts = [piece for pair in first_pairs for piece in four_quarters(pair, pair[1])]
    second_pairs = []
    for got in second_got:
        if z_split > 1:
            z_axes = ("zh", "zl")
            groups = [got] + [rotate(got, z_axes, n_z, by) for by in range(1, n_z)]
            groups[0] = tie(got, *[pair[1] for pair in first_pairs])
            got = order(lambda *groups: arrange(list(groups), z_axes, 1), *groups)
            got = got.reshape(planes, quarter, size)
        second_pairs.append(beside_quarter(got))
    cot_send = order(to_send, cotangent)
    cot_pieces = [cot_send[0]] + exchange(cot_send[1:], *x_late)

    window = (mine, size, length)
    piece_shape = (mine, part, length)
    n_pieces = 4 * (n_tp - 1)
    kept_struct = [struct(window, BF)] * 8
    w_struct = struct((planes, size, size), BF)
    fwd_scratch = [
        pltpu.VMEM((size, length), BF),
        pltpu.VMEM((taps, size, length), BF),
    ] + [pltpu.VMEM((size, length // HALVES), F32)] * (2 * HALVES)
    load_scratch = [
        pltpu.VMEM((planes, size, size), BF),
        pltpu.SemaphoreType.DMA((3 + n_pieces,)),
        pltpu.SemaphoreType.DMA,
    ]
    conv_flops = 2.0 * taps * size * size * length * mine
    ff_flops = 4.0 * size * size * length * mine
    weight_specs = [smem_spec(), whole_spec(pc.shape)] + [any_spec()] * (3 + n_pieces)
    first = order(
        pl.pallas_call(
            functools.partial(first_early_kernel, 0, n_tp, n_pieces, taps),
            grid=(early,),
            in_specs=weight_specs + [window_spec(piece_shape)] * n_tp,
            out_specs=[window_spec(window)] * 9 + [any_spec()],
            out_shape=kept_struct + [struct(window, BF), w_struct],
            scratch_shapes=fwd_scratch + load_scratch,
            compiler_params=params(),
            cost_estimate=cost((conv_flops + ff_flops) / 2, 20e6),
            name="forward_first_early",
        ),
        where,
        pc,
        conv_t,
        up_t,
        down_w,
        *first_parts,
        x_send[0],
        *x_early,
    )
    w0 = first[9]
    *kept0, hidden = first[:9]
    second_parts = [p for pair in second_pairs for p in four_quarters(pair, hidden)]
    if early < mine:
        *kept0, hidden = order(
            pl.pallas_call(
                functools.partial(first_late_kernel, 0, n_tp, taps, 9),
                grid=(mine - early,),
                in_specs=[smem_spec(), whole_spec(pc.shape), whole_spec(w_struct.shape)]
                + [window_spec(piece_shape, early)]
                + [window_spec(piece_shape)] * (n_tp - 1)
                + [any_spec()] * 9,
                out_specs=[window_spec(window, early)] * 9,
                out_shape=kept_struct + [struct(window, BF)],
                scratch_shapes=fwd_scratch,
                input_output_aliases={3 + n_tp + at: at for at in range(9)},
                compiler_params=params(),
                cost_estimate=cost((conv_flops + ff_flops) / 2, 20e6),
                name="forward_first_late",
            ),
            where,
            pc,
            w0,
            x_send[0],
            *x_late,
            *first[:9],
        )

    mask_rows = lax.dynamic_slice_in_dim(masked, me * mine, mine, 0).reshape(mine, 1, length)
    split = taps // 2
    low_taps, high_taps = tuple(range(split)), tuple(range(split, taps))
    skip = 2 * size + 128
    low_struct = struct((n_tp, part // 2, skip + split * size), BF)
    high_struct = struct((n_tp, part // 2, (taps - split) * size), BF)
    chain_out_specs = [window_spec(window)] * 2 + [
        whole_spec((2, size, size)),
        whole_spec((size, 128)),
    ]
    chain_out = [struct(window, BF)] * 2 + [
        struct((2, size, size), F32),
        struct((size, 128), F32),
    ]
    half_scratch = [pltpu.VMEM((size, length // HALVES), F32)] * HALVES
    chain_scratch = [
        pltpu.VMEM((size, length), BF),
        pltpu.VMEM((size, length), BF),
        pltpu.VMEM((7, size, 128), F32),
    ]
    wide_scratch = [pltpu.VMEM((taps, size, length), BF)]
    ff_specs = [plane_spec((1, size, size), taps), plane_spec((1, size, size), taps + 1)]
    conv_spec = plane_spec((taps, size, size), 0)
    kinds = lax.dynamic_slice_in_dim(species, me * mine, mine, 0)
    *y_pieces, dc1, dm1, ff1, small1, w1 = order(
        pl.pallas_call(
            functools.partial(second_kernel, 1, n_tp, n_pieces, taps),
            grid=(mine,),
            in_specs=weight_specs
            + [window_spec(window), whole_spec(read_rows.shape), window_spec((mine, 1, length))]
            + [smem_spec()]
            + [window_spec(piece_shape)] * n_tp,
            out_specs=[window_spec(piece_shape)] * n_tp
            + chain_out_specs
            + [any_spec()],
            out_shape=[struct(piece_shape, BF)] * n_tp
            + chain_out
            + [w_struct],
            scratch_shapes=fwd_scratch
            + [pltpu.VMEM((1, size, length), BF)] * 7
            + chain_scratch
            + [pltpu.VMEM((8 * SPECIES, 128), F32)]
            + load_scratch,
            compiler_params=params(),
            cost_estimate=cost(conv_flops + 3 * ff_flops, 20e6),
            name="second_layer",
        ),
        where,
        pc,
        conv_t,
        up_t,
        down_w,
        *second_parts,
        hidden,
        read_rows,
        mask_rows,
        kinds,
        *cot_pieces,
    )

    def chunk(layer, chosen, shape, dc, a, rest, name):
        keep, send = order(
            pl.pallas_call(
                functools.partial(weight_kernel, layer, taps, chosen),
                in_specs=[smem_spec()] + [vmem] * (2 + len(rest)),
                out_specs=[vmem] * 2,
                out_shape=[shape] * 2,
                scratch_shapes=[pltpu.VMEM((2, size, size), F32)],
                compiler_params=params(),
                cost_estimate=cost(conv_flops * len(chosen) / taps, 10e6),
                name=name,
            ),
            where,
            dc,
            a,
            *rest,
        )
        return Chunk(order, sizes, keep, send)

    low1 = chunk(1, low_taps, low_struct, dc1, hidden, (ff1, small1), "weights_second_low")
    high1 = chunk(1, high_taps, high_struct, dc1, hidden, (), "weights_second_high")
    low1.scatter("tp")
    high1.scatter("tp")

    dc0, dm0, ff0, small0 = order(
        pl.pallas_call(
            functools.partial(middle_kernel, 0, taps),
            grid=(mine,),
            in_specs=[conv_spec] + ff_specs + [whole_spec(pc.shape)] + [window_spec(window)] * 9,
            out_specs=chain_out_specs,
            out_shape=chain_out,
            scratch_shapes=wide_scratch + half_scratch + chain_scratch + half_scratch,
            compiler_params=params(),
            cost_estimate=cost(conv_flops + 2 * ff_flops, 20e6),
            name="chain_first",
        ),
        w1,
        w0,
        w0,
        pc,
        dc1,
        dm1,
        *kept0[1:],
    )
    y_back = [y_pieces[0]] + [
        rotate(tie(y_pieces[by], high1.terms[2][0]), "tp", n_tp, by) for by in range(1, n_tp)
    ]
    both1 = Pair(low1, high1)
    both1.scatter("y")
    high0 = chunk(0, high_taps, high_struct, dc0, kept0[0], (), "weights_first_high")
    low0 = chunk(0, low_taps, low_struct, dc0, kept0[0], (ff0, small0), "weights_first_low")
    both1.scatter("zl")
    y_out = order(lambda *pieces: arrange(list(pieces), "tp", 0), *y_back)
    y_out = y_out.reshape(windows, part, length)
    high0.scatter("tp")
    low0.scatter("y")
    both1.scatter("zh")
    x_grads = order(
        pl.pallas_call(
            functools.partial(bottom_kernel, 0, taps, n_tp),
            grid=(mine,),
            in_specs=[smem_spec(), conv_spec] + [window_spec(window)] * 2,
            out_specs=[window_spec(piece_shape)] * n_tp,
            out_shape=[struct(piece_shape, F32)] + [struct(piece_shape, BF)] * (n_tp - 1),
            scratch_shapes=wide_scratch + [pltpu.VMEM((size, length), F32)],
            compiler_params=params(),
            cost_estimate=cost(conv_flops, 15e6),
            name="input_grad",
        ),
        where,
        w0,
        dc0,
        dm0,
    )
    high0.scatter("y")
    low0.scatter("tp")
    both1.meet()
    low0.scatter("zl")
    x_back = [x_grads[0]] + [
        rotate(tie(x_grads[by], low0.terms[3][0]), "tp", n_tp, by) for by in range(1, n_tp)
    ]
    high0.scatter("zl")
    both1.widen()
    low0.scatter("zh")
    high0.scatter("zh")
    both1.spread()
    low0.meet()
    high0.meet()
    low0.widen()
    both1.cross()
    high0.widen()
    low0.spread()

    conv_struct = struct((layers, taps, part, size), F32)

    grad_conv, rest1 = order(
        pl.pallas_call(
            functools.partial(settle_rest_kernel, 1),
            in_specs=[smem_spec()] + [vmem] * 4,
            out_specs=[any_spec(), vmem],
            out_shape=[conv_struct, struct((part, skip), F32)],
            scratch_shapes=[
                pltpu.VMEM((4, taps, quarter, size), F32),
                pltpu.SemaphoreType.DMA((4,)),
            ],
            compiler_params=params(),
            name="settle_second",
        ),
        where,
        *both1.quarters,
    )
    grad_x = order(
        lambda *pieces: arrange([piece.astype(F32) for piece in pieces], "tp", 0), *x_back
    ).reshape(windows, part, length)
    high0.spread()
    low0.cross()
    high0.cross()
    grad_conv, grad_up_w, grad_down_w, g_conv_b, g_gain, g_bias, g_up_b, g_down_b = order(
        pl.pallas_call(
            functools.partial(settle_last_kernel, 0, split),
            in_specs=[smem_spec()] + [vmem] * 9 + [any_spec()],
            out_specs=[any_spec()] + [vmem] * 7,
            out_shape=[
                conv_struct,
                struct((layers, size, part), F32),
                struct((layers, part, size), F32),
                struct((layers, part), F32),
                struct((layers, 2, part), F32),
                struct((layers, 2, part), F32),
                struct((layers, part), F32),
                struct((layers, part), F32),
            ],
            scratch_shapes=[
                pltpu.VMEM((part, skip), F32),
                pltpu.VMEM((4, split, quarter, size), F32),
                pltpu.VMEM((4, taps - split, quarter, size), F32),
                pltpu.SemaphoreType.DMA((4,)),
                pltpu.SemaphoreType.DMA((4,)),
            ],
            input_output_aliases={10: 0},
            compiler_params=params(),
            name="settle_last",
        ),
        where,
        *low0.quarters,
        *high0.quarters,
        rest1,
        grad_conv,
    )

    grad_conv_w = jnp.transpose(grad_conv, (0, 2, 1, 3))
    species_sum = rest1[: 8 * SPECIES, 2 * size + 7].reshape(SPECIES, 8)[:, :CLASSES] / length
    return (
        y_out,
        grad_x,
        grad_conv_w,
        g_conv_b,
        g_gain,
        g_bias,
        grad_up_w,
        g_up_b,
        grad_down_w,
        g_down_b,
        species_sum,
    )


def solution(mesh):
    dp, tp = mesh.shape["dp"], mesh.shape["tp"]
    n_core = n_y = 2
    n_zl = 2
    n_zh = dp // (n_core * n_y * n_zl)
    fine = Mesh(mesh.devices.reshape(n_zh, n_zl, n_y, n_core, tp), DP + ("tp",))
    placed = (
        P(DP, "tp", None),
        P(None, "tp", None, None),
        P(None, "tp"),
        P(None, None, "tp"),
        P(None, None, "tp"),
        P(None, None, "tp"),
        P(None, "tp"),
        P(None, "tp", None),
        P(None, "tp"),
        P("tp", None),
        P(DP, "tp", None),
        P(DP, None),
        P(DP),
    )
    return jax.shard_map(
        functools.partial(body, (n_zh, n_zl, n_y, n_core, tp)),
        mesh=fine,
        in_specs=placed,
        out_specs=(
            P(DP, "tp", None),
            P(DP, "tp", None),
            P(None, "tp", None, None),
            P(None, "tp"),
            P(None, None, "tp"),
            P(None, None, "tp"),
            P(None, None, "tp"),
            P(None, "tp"),
            P(None, "tp", None),
            P(None, "tp"),
            P(),
        ),
        check_vma=False,
    )
```

```python
import functools

import jax
import jax.numpy as jnp
from jax import lax
from jax.experimental import pallas as pl
from jax.experimental.pallas import tpu as pltpu
from jax.sharding import Mesh
from jax.sharding import PartitionSpec as P

DILATIONS = (2, 32)
SPECIES = 8
CLASSES = 6
EPS = 1e-05
BF = jnp.bfloat16
F32 = jnp.float32
DP = ("zh", "zl", "y", "core")
STEP = 32
HALVES = 2
VMEM_BYTES = 58 * 2**20
CONV_B, GAIN_A, BIAS_A, UP_B, DOWN_B, GAIN_B, BIAS_B = range(7)
COLUMNS = 8


def shifted(rows, by):
    if by == 0:
        return rows
    blank = jnp.zeros((rows.shape[0], abs(by)), rows.dtype)
    if by > 0:
        return jnp.concatenate([rows[:, by:], blank], axis=1)
    return jnp.concatenate([blank, rows[:, :by]], axis=1)


def fold(tile):
    return sum(tile[at : at + 8] for at in range(0, tile.shape[0], 8))


def fold_lanes(tile):
    return sum(tile[:, at : at + 128] for at in range(0, tile.shape[1], 128))


def gelu_pair(x):
    cdf = 0.5 + 0.5 * lax.erf(x * 0.7071067811865476)
    return x * cdf, cdf + x * jnp.exp(-0.5 * x * x) * 0.3989422804014327


def nn(left, right):
    return jnp.dot(left, right, preferred_element_type=F32)


def tn(left, right):
    return lax.dot_general(left, right, (((0,), (0,)), ((), ())), preferred_element_type=F32)


def nt(left, right):
    return lax.dot_general(left, right, (((1,), (1,)), ((), ())), preferred_element_type=F32)


def steps(size):
    return [slice(at, at + STEP) for at in range(0, size, STEP)]


def place(pieces, me, target):
    ways = len(pieces)
    for back, piece in enumerate(pieces):
        size = piece.shape[1]
        spot = lax.rem(me + (ways - back), ways) * size
        target[pl.ds(pl.multiple_of(spot, size), size), :] = piece[0]


def norm_stats(total, square, width):
    mean = jnp.sum(total, axis=0, keepdims=True) / width
    var = jnp.sum(square, axis=0, keepdims=True) / width - mean * mean
    return mean, lax.rsqrt(var + EPS)


def activate_and_sum(pre, col, pc, slope_ref, span):
    size, length = pre.shape
    total = jnp.zeros((8, length), F32)
    square = jnp.zeros((8, length), F32)
    for rows in steps(size):
        value, slope = gelu_pair(pre[rows, :] + pc[rows, col : col + 1])
        pre[rows, :] = value
        slope_ref[0, rows, span] = slope.astype(BF)
        total = total + fold(value)
        square = square + fold(value * value)
    return norm_stats(total, square, size)


def load_weights(layer, where, blocks, pieces, full, w, sems, out_sem):
    tp, y, core = where[0], where[1], where[2]
    conv, up, down = blocks
    taps, part = conv.shape[1], conv.shape[2]
    ways = w.shape[1] // part
    here = pl.program_id(0)

    def rows(owner, at, count):
        return pl.ds(pl.multiple_of(owner * part + at, count), count)

    @pl.when(here == 0)
    def _():
        own = rows(tp, 0, part)
        copies = [
            (conv.at[layer], w.at[0:taps, own]),
            (up.at[layer], w.at[taps, own]),
            (down.at[layer], w.at[taps + 1, own]),
        ]
        quarter = part // 4
        for back in range(1, ways):
            owner = lax.rem(tp + (ways - back), ways)
            for flip in range(4):
                c = core if flip < 2 else 1 - core
                at = c * (2 * quarter) + (y if flip % 2 == 0 else 1 - y) * quarter
                copies.append((pieces[4 * (back - 1) + flip], w.at[:, rows(owner, at, quarter)]))
        moves = [pltpu.make_async_copy(src, dst, sems.at[i]) for i, (src, dst) in enumerate(copies)]
        for move in moves:
            move.start()
        for move in moves:
            move.wait()
        pltpu.make_async_copy(w, full, out_sem).start()

    @pl.when(here == pl.num_programs(0) - 1)
    def _():
        pltpu.make_async_copy(w, full, out_sem).wait()


def first_early_kernel(layer, n_in, n_pieces, taps, *refs):
    where, pc = refs[:2]
    blocks, parts = refs[2:5], refs[5 : 5 + n_pieces]
    at = 5 + n_pieces
    pieces = refs[at : at + n_in]
    at += n_in
    *kept, out = refs[at : at + 9]
    full = refs[at + 9]
    *work, w, sems, out_sem = refs[at + 10 :]
    load_weights(layer, where, blocks, parts, full, w, sems, out_sem)
    forward_window(layer, taps, where, pc, w, pieces, kept, work)
    out[0] = work[0][...]


def first_late_kernel(layer, n_in, taps, n_before, where, pc, w, *refs):
    pieces, refs = refs[:n_in], refs[n_in + n_before :]
    *kept, out = refs[:9]
    work = refs[9:]
    forward_window(layer, taps, where, pc, w, pieces, kept, work)
    out[0] = work[0][...]


def second_kernel(layer, n_in, n_pieces, taps, *refs):
    where, pc = refs[:2]
    blocks, parts = refs[2:5], refs[5 : 5 + n_pieces]
    at = 5 + n_pieces
    hidden, readout, mask_ref, kinds = refs[at : at + 4]
    cots = refs[at + 4 : at + 4 + n_in]
    at += 4 + n_in
    y_refs = refs[at : at + n_in]
    dc_ref, dm_ref, ff_sum, small, full = refs[at + n_in : at + n_in + 5]
    refs = refs[at + n_in + 5 :]
    act, wide, *pairs = refs[: 2 + 2 * HALVES]
    kept = refs[2 + 2 * HALVES : 9 + 2 * HALVES]
    low, high, row_sums, shares, w, sems, out_sem = refs[9 + 2 * HALVES :]
    load_weights(layer, where, blocks, parts, full, w, sems, out_sem)
    here = pl.program_id(0)
    clear(here == 0, ff_sum, row_sums, shares)
    forward_window(layer, taps, where, pc, w, (hidden,), (None,) + kept, (act, wide, *pairs))
    me = where[0]
    part = act.shape[0] // n_in
    for ahead, ref in enumerate(y_refs):
        spot = lax.rem(me + ahead, n_in) * part
        ref[0] = act[pl.ds(pl.multiple_of(spot, part), part), :]
    logits = nn(readout[...], act[...])
    seat = lax.broadcasted_iota(jnp.int32, logits.shape, 0)
    logits = jnp.where(seat < CLASSES, logits, -1e30)
    raised = jnp.exp(logits - jnp.max(logits, axis=0, keepdims=True))
    chance = raised / jnp.sum(raised, axis=0, keepdims=True)
    chance = fold_lanes(chance * mask_ref[0].astype(F32))
    for kind in range(SPECIES):
        shares[8 * kind : 8 * kind + 8, :] += jnp.where(kinds[here] == kind, chance, 0.0)
    grads = pairs[HALVES:]
    for back, piece in enumerate(cots):
        spot = pl.multiple_of(lax.rem(me + (n_in - back), n_in) * part, part)
        for at, grad in enumerate(grads):
            width = grad.shape[1]
            grad[pl.ds(spot, part), :] = piece[0, :, at * width : (at + 1) * width].astype(F32)
    up, down = w.at[pl.ds(taps, 1)], w.at[pl.ds(taps + 1, 1)]
    outs = (dc_ref, dm_ref, ff_sum)
    chain(layer, grads, kept, up, down, pc, outs, (low, high, row_sums, *pairs[:HALVES]))

    @pl.when(here == pl.num_programs(0) - 1)
    def _():
        close(row_sums, small, shares, part)


def forward_window(layer, taps, where, pc, w, pieces, kept, work):
    a_ref, b_ref, n1_ref, s1_ref, su_ref, v_ref, s2_ref, n2_ref = kept
    act, wide, *pairs = work
    size, length = act.shape
    base = layer * COLUMNS
    half = taps // 2
    width = length // HALVES
    spans = [slice(at, at + width) for at in range(0, length, width)]
    pres, mids = pairs[:HALVES], pairs[HALVES:]
    place(pieces, where[0], act)
    if a_ref is not None:
        a_ref[0] = act[...]
    for tap in range(taps):
        wide[tap] = shifted(act[...], (tap - half) * DILATIONS[layer])

    def convolve(pre, span):
        total = nn(w[0], wide[0, :, span])
        for tap in range(1, taps):
            total = total + nn(w[tap], wide[tap, :, span])
        pre[...] = total

    def first_norm(pre, mid, span):
        mean, inv = activate_and_sum(pre, base + CONV_B, pc, s1_ref, span)
        for rows in steps(size):
            normed = (pre[rows, :] - mean) * inv
            m = (
                act[rows, span].astype(F32)
                + normed * pc[rows, base + GAIN_A : base + GAIN_A + 1]
                + pc[rows, base + BIAS_A : base + BIAS_A + 1]
            )
            n1_ref[0, rows, span] = normed.astype(BF)
            s1_ref[0, rows, span] = (s1_ref[0, rows, span].astype(F32) * inv).astype(BF)
            mid[rows, :] = m
            b_ref[0, rows, span] = m.astype(BF)

    def hidden(pre, span):
        for rows in steps(size):
            value, slope = gelu_pair(pre[rows, :] + pc[rows, base + UP_B : base + UP_B + 1])
            v_ref[0, rows, span] = value.astype(BF)
            su_ref[0, rows, span] = slope.astype(BF)

    def second_norm(pre, mid, span):
        mean, inv = activate_and_sum(pre, base + DOWN_B, pc, s2_ref, span)
        for rows in steps(size):
            normed = (pre[rows, :] - mean) * inv
            out = (
                mid[rows, :]
                + normed * pc[rows, base + GAIN_B : base + GAIN_B + 1]
                + pc[rows, base + BIAS_B : base + BIAS_B + 1]
            )
            n2_ref[0, rows, span] = normed.astype(BF)
            s2_ref[0, rows, span] = (s2_ref[0, rows, span].astype(F32) * inv).astype(BF)
            act[rows, span] = out.astype(BF)

    for pre, span in zip(pres, spans):
        convolve(pre, span)
    for pre, mid, span in zip(pres, mids, spans):
        first_norm(pre, mid, span)
        pre[...] = nn(w[taps], b_ref[0, :, span])
        hidden(pre, span)
        pre[...] = tn(w[taps + 1], v_ref[0, :, span])
        second_norm(pre, mid, span)

def clear(first, *sums):
    @pl.when(first)
    def _():
        for ref in sums:
            ref[...] = jnp.zeros_like(ref)


def close(row_sums, small_ref, shares=None, part=0):
    for rows in steps(small_ref.shape[0]):
        seat = lax.broadcasted_iota(jnp.int32, (STEP, 128), 1)
        table = jnp.zeros((STEP, 128), F32)
        for slot in range(7):
            column = jnp.sum(row_sums[slot, rows, :], axis=1, keepdims=True)
            table = jnp.where(seat == slot, column, table)
        if shares is not None and rows.start % part < 8 * SPECIES:
            at = rows.start % part
            column = jnp.sum(shares[at : at + STEP, :], axis=1, keepdims=True)
            table = jnp.where(seat == 7, column, table)
        small_ref[rows, :] = table


def chain(layer, grads, kept, up, down, pc, outs, work):
    b_ref, n1_ref, s1_ref, su_ref, v_ref, s2_ref, n2_ref = kept
    dc_ref, dm_ref, ff_sum = outs
    low, high, row_sums, *pres = work
    size, width = pres[0].shape
    base = layer * COLUMNS
    spans = [slice(at, at + width) for at in range(0, low.shape[1], width)]

    def back(grad, span, gain_col, normed_ref, slope_ref, slot, target):
        total = jnp.zeros((8, width), F32)
        cross = jnp.zeros((8, width), F32)
        for rows in steps(size):
            g = grad[rows, :]
            product = g * normed_ref[0, rows, span].astype(F32)
            row_sums[slot + 1, rows, :] += fold_lanes(product)
            row_sums[slot + 2, rows, :] += fold_lanes(g)
            gain = pc[rows, gain_col : gain_col + 1]
            total = total + fold(g * gain)
            cross = cross + fold(product * gain)
        mean_q = jnp.sum(total, axis=0, keepdims=True) / size
        mean_qn = jnp.sum(cross, axis=0, keepdims=True) / size
        for rows in steps(size):
            q = grad[rows, :] * pc[rows, gain_col : gain_col + 1]
            normed = normed_ref[0, rows, span].astype(F32)
            d = slope_ref[0, rows, span].astype(F32) * (q - mean_q - normed * mean_qn)
            row_sums[slot, rows, :] += fold_lanes(d)
            target[rows, span] = d.astype(BF)

    for grad, pre, span in zip(grads, pres, spans):
        back(grad, span, base + GAIN_B, n2_ref, s2_ref, DOWN_B, low)
        pre[...] = nn(down[0], low[:, span])
        for rows in steps(size):
            du = pre[rows, :] * su_ref[0, rows, span].astype(F32)
            row_sums[UP_B, rows, :] += fold_lanes(du)
            high[rows, span] = du.astype(BF)
        pre[...] = tn(up[0], high[:, span])
        for rows in steps(size):
            dm = grad[rows, :] + pre[rows, :]
            grad[rows, :] = dm
            dm_ref[0, rows, span] = dm.astype(BF)
        back(grad, span, base + GAIN_A, n1_ref, s1_ref, CONV_B, dc_ref.at[0])
    ff_sum[0] += nt(high[...], b_ref[0])
    ff_sum[1] += nt(v_ref[0], low[...])


def conv_back(layer, taps, dc, dm_ref, w, wide, grads):
    half = taps // 2
    width = grads[0].shape[1]
    for tap in range(taps):
        wide[tap] = shifted(dc, -(tap - half) * DILATIONS[layer])
    total = tn(w[0], wide[0])
    for tap in range(1, taps):
        total = total + tn(w[tap], wide[tap])
    for at, grad in enumerate(grads):
        span = slice(at * width, (at + 1) * width)
        grad[...] = total[:, span] + dm_ref[0, :, span].astype(F32)


def middle_kernel(layer, taps, *refs):
    above_w, up, down, pc, dc_in, dm_in = refs[:6]
    kept = refs[6:13]
    dc_ref, dm_ref, ff_sum, small = refs[13:17]
    wide, grads = refs[17], refs[18 : 18 + HALVES]
    low, high, row_sums, *pres = refs[18 + HALVES :]
    here = pl.program_id(0)
    clear(here == 0, ff_sum, row_sums)
    conv_back(layer + 1, taps, dc_in[0], dm_in, above_w, wide, grads)
    outs = (dc_ref, dm_ref, ff_sum)
    chain(layer, grads, kept, up, down, pc, outs, (low, high, row_sums, *pres))

    @pl.when(here == pl.num_programs(0) - 1)
    def _():
        close(row_sums, small)


def bottom_kernel(layer, taps, n_out, where, w, dc_in, dm_in, own_ref, *refs):
    others = refs[: n_out - 1]
    wide, *grads = refs[n_out - 1 :]
    conv_back(layer, taps, dc_in[0], dm_in, w, wide, grads)
    me = where[0]
    part = own_ref.shape[1]
    for at, grad in enumerate(grads):
        width = grad.shape[1]
        span = slice(at * width, (at + 1) * width)
        own_ref[0, :, span] = grad[pl.ds(pl.multiple_of(me * part, part), part), :]
        for ahead, ref in enumerate(others, start=1):
            spot = pl.multiple_of(lax.rem(me + ahead, n_out) * part, part)
            ref[0, :, span] = grad[pl.ds(spot, part), :].astype(BF)


def weight_part(layer, taps, chosen, core, dc, a, rest, keep, send, total):
    half = taps // 2
    blocks, rows, _ = keep.shape
    size = total.shape[1]

    def put(source, at, width):
        for block in range(blocks):
            first = block * 2 * rows
            mine = pl.multiple_of(first + core * rows, rows)
            other = pl.multiple_of(first + (1 - core) * rows, rows)
            keep[block, :, at : at + width] = source[pl.ds(mine, rows), :].astype(BF)
            send[block, :, at : at + width] = source[pl.ds(other, rows), :].astype(BF)

    skip = 0
    if rest:
        ff, small = rest
        put(ff.at[0], 0, size)
        put(ff.at[1], size, size)
        put(small, 2 * size, small.shape[1])
        skip = 2 * size + small.shape[1]
    for at, tap in enumerate(chosen):
        by = -(tap - half) * DILATIONS[layer]
        acc = None
        for window in range(dc.shape[0]):
            part = nt(shifted(dc[window], by), a[window])
            acc = part if acc is None else acc + part
        total[at % 2] = acc
        put(total.at[at % 2], skip + at * size, size)


def weight_kernel(layer, taps, chosen, where, dc, a, *refs):
    rest, (keep, send, total) = refs[:-3], refs[-3:]
    weight_part(layer, taps, chosen, where[2], dc, a, rest, keep, send, total)


def pack_kernel(layers, where, conv, up, down, up_t, *refs):
    shares, sems = refs[:layers], refs[layers]
    tp, y, core, z = where[0], where[1], where[2], where[3]
    taps = conv.shape[1]
    moves = []
    for layer in range(layers):
        count = shares[layer].shape[1]
        quarter = up.shape[2] // 4
        at = core * (2 * quarter) + y * quarter
        if count < quarter:
            at = at + z * count
        rows = pl.ds(pl.multiple_of(at, count), count)
        moves.append((conv.at[layer, :, rows], shares[layer].at[0:taps]))
        moves.append((down.at[layer, rows], shares[layer].at[taps + 1]))
    moves = [pltpu.make_async_copy(src, dst, sems.at[i]) for i, (src, dst) in enumerate(moves)]
    for move in moves:
        move.start()
    for layer in range(layers):
        up_t[layer] = jnp.transpose(up[layer])
    for layer in range(layers):
        count = shares[layer].shape[1]
        quarter = up.shape[2] // 4
        at = core * (2 * quarter) + y * quarter
        if count < quarter:
            at = at + z * count
        shares[layer][taps] = up_t[layer, pl.ds(pl.multiple_of(at, count), count), :]
    for move in moves:
        move.wait()


def settle_conv(layer, first_tap, where, pieces, out, wide, sems, skip):
    count, rows, size = wide.shape[1:]
    moves = []
    for flip, piece in enumerate(pieces):
        c = where[2] if flip < 2 else 1 - where[2]
        y = where[1] if flip % 2 == 0 else 1 - where[1]
        at = pl.multiple_of(c * (2 * rows) + y * rows, rows)
        for tap in range(count):
            begin = skip + tap * size
            wide[flip, tap] = piece[:, begin : begin + size].astype(F32)
        target = out.at[layer, first_tap : first_tap + count, pl.ds(at, rows)]
        moves.append(pltpu.make_async_copy(wide.at[flip], target, sems.at[flip]))
        moves[-1].start()
    return moves


def settle_rest_kernel(layer, where, *refs):
    pieces = refs[:4]
    out, rest, wide, sems = refs[4:]
    skip = rest.shape[1]
    moves = settle_conv(layer, 0, where, pieces, out, wide, sems, skip)
    rows = pieces[0].shape[0]
    for flip, piece in enumerate(pieces):
        c = where[2] if flip < 2 else 1 - where[2]
        y = where[1] if flip % 2 == 0 else 1 - where[1]
        at = pl.multiple_of(c * (2 * rows) + y * rows, rows)
        rest[pl.ds(at, rows), :] = piece[:, :skip].astype(F32)
    for move in moves:
        move.wait()


def settle_last_kernel(layer, split, where, *refs):
    low, high, (other,) = refs[:4], refs[4:8], refs[8:9]
    out, up, down, conv_b, gain, bias, up_b, down_b = refs[10:18]
    rest, wide_low, wide_high, sems_low, sems_high = refs[18:]
    skip = rest.shape[1]
    moves = settle_conv(layer, 0, where, low, out, wide_low, sems_low, skip)
    moves += settle_conv(layer, split, where, high, out, wide_high, sems_high, 0)
    rows = low[0].shape[0]
    for flip, piece in enumerate(low):
        c = where[2] if flip < 2 else 1 - where[2]
        y = where[1] if flip % 2 == 0 else 1 - where[1]
        at = pl.multiple_of(c * (2 * rows) + y * rows, rows)
        rest[pl.ds(at, rows), :] = piece[:, :skip].astype(F32)
    size = down.shape[2]
    for at_layer, source in ((layer, rest), (1 - layer, other)):
        one = slice(at_layer, at_layer + 1)
        up[at_layer] = jnp.transpose(source[:, :size])
        down[at_layer] = source[:, size : 2 * size]
        small = jnp.transpose(source[:, 2 * size :])
        conv_b[one, :] = small[CONV_B : CONV_B + 1]
        up_b[one, :] = small[UP_B : UP_B + 1]
        down_b[one, :] = small[DOWN_B : DOWN_B + 1]
        for at, (g, b) in enumerate(((GAIN_A, BIAS_A), (GAIN_B, BIAS_B))):
            gain[at_layer, at : at + 1, :] = small[g : g + 1]
            bias[at_layer, at : at + 1, :] = small[b : b + 1]
    for move in moves:
        move.wait()


def whole_spec(shape):
    return pl.BlockSpec(
        shape, lambda *_: (0,) * len(shape), pipeline_mode=pl.Buffered(buffer_count=1)
    )


def window_spec(shape, first=0):
    return pl.BlockSpec((1,) + shape[1:], lambda i: (i + first,) + (0,) * (len(shape) - 1))


def plane_spec(block, index):
    return pl.BlockSpec(
        block,
        lambda *_: (index,) + (0,) * (len(block) - 1),
        pipeline_mode=pl.Buffered(buffer_count=1),
    )


def any_spec():
    return pl.BlockSpec(memory_space=pl.ANY)


def smem_spec():
    return pl.BlockSpec(memory_space=pltpu.SMEM)


def params():
    return pltpu.CompilerParams(vmem_limit_bytes=VMEM_BYTES)


def cost(flops, nbytes):
    return pl.CostEstimate(flops=int(8 * flops), bytes_accessed=int(nbytes), transcendentals=0)


def struct(shape, dtype):
    return jax.ShapeDtypeStruct(shape, dtype)


def rotate(value, axis, ways, by):
    return lax.ppermute(value, axis, [(i, (i + by) % ways) for i in range(ways)])


def pick(value, index, dim):
    return lax.dynamic_index_in_dim(value, index, dim, keepdims=False)


def tie(value, *after):
    return lax.optimization_barrier((value,) + after)[0]


def add_up(terms):
    return sum(term.astype(F32) for term in terms).astype(BF)


def arrange(pieces, axis, dim):
    me = lax.axis_index(axis)
    ways = len(pieces)
    if ways == 2:
        low = jnp.where(me == 0, pieces[0], pieces[1])
        high = jnp.where(me == 0, pieces[1], pieces[0])
        return jnp.stack([low, high], axis=dim)
    shape = list(pieces[0].shape)
    shape.insert(dim, ways)
    out = jnp.zeros(shape, pieces[0].dtype)
    for back, piece in enumerate(pieces):
        spot = lax.rem(me + (ways - back), ways)
        out = lax.dynamic_update_index_in_dim(out, piece, spot, dim)
    return out


class Order:
    def __init__(self):
        self.last = ()

    def __call__(self, step, *values):
        values = lax.optimization_barrier(values + self.last)[: len(values)]
        result = step(*values)
        self.last = (jax.tree.leaves(result)[0],)
        return result


class Chunk:
    def __init__(self, order, sizes, keep, send):
        self.order = order
        self.ways = dict(zip(DP + ("tp",), sizes))
        blocks, rows, width = keep.shape
        self.rows, self.width = rows, width
        y, zh, zl = self.ways["y"], self.ways["zh"], self.ways["zl"]
        self.shape = (blocks, y, zh, zl, rows // (y * zh * zl), width)
        self.left = ["tp", "y", "zh", "zl"]
        sent = rotate(send, "core", 2, 1)
        self.terms = [(keep.reshape(self.shape), ()), (sent.reshape(self.shape), ())]

    def total(self, values, *last):
        cut = []
        for value, (_, at) in zip(values, self.terms):
            for dim, index in at + last:
                value = pick(value, index, dim)
            cut.append(value)
        return add_up(cut)

    def scatter(self, axis):
        me, count = lax.axis_index(axis), self.ways[axis]
        dim = self.left.index(axis)

        def step(*values):
            return [self.total(values, (dim, lax.rem(me + by, count))) for by in range(1, count)]

        outs = self.order(step, *[term for term, _ in self.terms])
        got = [rotate(out, axis, count, by) for by, out in enumerate(outs, start=1)]
        self.terms = [(term, at + ((dim, me),)) for term, at in self.terms]
        self.terms += [(g, ()) for g in got]
        self.left.remove(axis)

    def meet(self):
        piece = self.order(lambda *values: self.total(values), *[term for term, _ in self.terms])
        count = self.ways["zh"]
        self.groups = [piece] + [rotate(piece, "zh", count, by) for by in range(1, count)]

    def widen(self):
        pieces = self.order(lambda *groups: arrange(list(groups), "zh", 0), *self.groups)
        self.groups = [pieces, rotate(pieces, "zl", 2, 1)]

    def spread(self):
        quarter = self.order(lambda *groups: arrange(list(groups), "zl", 1), *self.groups)
        quarter = quarter.reshape(self.rows // self.ways["y"], self.width)
        self.quarters = [quarter, rotate(quarter, "y", 2, 1)]

    def cross(self):
        self.quarters += [rotate(quarter, "core", 2, 1) for quarter in self.quarters]


class Pair(Chunk):
    def __init__(self, one, two):
        self.order, self.ways, self.rows = one.order, one.ways, one.rows
        self.width = one.width + two.width
        self.halves = (one, two)
        self.left = list(one.left)
        self.split = len(one.terms)
        self.terms = None

    def scatter(self, axis):
        if self.terms is not None:
            super().scatter(axis)
            return
        one, two = self.halves
        me, count = lax.axis_index(axis), self.ways[axis]
        dim = self.left.index(axis)
        values = [term for term, _ in one.terms + two.terms]

        def joined(values, spot):
            parts = [
                side.total(values[at : at + self.split], (dim, spot))
                for side, at in ((one, 0), (two, self.split))
            ]
            return jnp.concatenate(parts, axis=-1)

        def step(*values):
            sends = [joined(values, lax.rem(me + by, count)) for by in range(1, count)]
            return sends + [joined(values, me)]

        *outs, own = self.order(step, *values)
        got = [rotate(out, axis, count, by) for by, out in enumerate(outs, start=1)]
        self.terms = [(own, ())] + [(g, ()) for g in got]
        self.left.remove(axis)


def body(sizes, *args):
    (
        x_in,
        conv_w,
        conv_b,
        ln_gain,
        ln_bias,
        up_w,
        up_b,
        down_w,
        down_b,
        readout,
        cotangent,
        masked,
        species,
    ) = args
    n_zh, n_zl, n_y, n_core, n_tp = sizes
    n_z = n_zh * n_zl
    layers, part, taps, size = conv_w.shape
    windows, _, length = x_in.shape
    mine = windows // n_tp
    planes = taps + 2
    me, my_y, my_core = (lax.axis_index(axis) for axis in ("tp", "y", "core"))
    my_z = lax.axis_index("zh") * n_zl + lax.axis_index("zl")
    where = jnp.stack([me, my_y, my_core, my_z]).astype(jnp.int32)
    quarter = part // 4
    order = Order()
    conv_t = jnp.transpose(conv_w, (0, 2, 1, 3))

    vmem = pl.BlockSpec(memory_space=pltpu.VMEM)
    z_split = n_z if quarter // n_z >= 16 else 1
    up_t, first_share, second_share = order(
        pl.pallas_call(
            functools.partial(pack_kernel, layers),
            in_specs=[smem_spec(), any_spec(), vmem, any_spec()],
            out_specs=[vmem] * 3,
            out_shape=[
                struct((layers, part, size), BF),
                struct((planes, quarter, size), BF),
                struct((planes, quarter // z_split, size), BF),
            ],
            scratch_shapes=[pltpu.SemaphoreType.DMA((2 * layers,))],
            compiler_params=params(),
            name="pack_shares",
        ),
        where,
        conv_t,
        up_w,
        down_w,
    )

    def to_send(value):
        cut = value.reshape(n_tp, mine, part, length)
        return [pick(cut, me if by == 0 else lax.rem(me + by, n_tp), 0) for by in range(n_tp)]

    def exchange(sends, *after):
        return [
            rotate(tie(piece, *after), "tp", n_tp, by) for by, piece in enumerate(sends, start=1)
        ]

    def beside_quarter(own):
        return [own, rotate(own, "y", 2, 1)]

    def four_quarters(pair, *after):
        return pair + [rotate(tie(piece, *after), "core", 2, 1) for piece in pair]

    second_got = [rotate(second_share, "tp", n_tp, by) for by in range(1, n_tp)]
    first_got = [rotate(tie(first_share, *second_got), "tp", n_tp, by) for by in range(1, n_tp)]

    columns = []
    for layer in range(layers):
        columns += [
            conv_b[layer],
            ln_gain[layer, 0],
            ln_bias[layer, 0],
            up_b[layer],
            down_b[layer],
            ln_gain[layer, 1],
            ln_bias[layer, 1],
            jnp.zeros((part,), BF),
        ]
    table = jnp.concatenate([jnp.stack(columns), jnp.transpose(readout)])
    table = jnp.pad(table, ((0, 2), (0, 0)))
    table = arrange(
        [table] + [rotate(table, "tp", n_tp, by) for by in range(1, n_tp)], "tp", 1
    ).reshape(table.shape[0], size)
    pc = jnp.transpose(table[: layers * COLUMNS]).astype(F32)
    read_rows = table[layers * COLUMNS :]

    early = mine // 2 if mine >= 4 else mine
    x_send = order(to_send, x_in)
    x_early = exchange([piece[:early] for piece in x_send[1:]], *first_got)
    x_late = x_early
    if early < mine:
        x_late = exchange([piece[early:] for piece in x_send[1:]], *x_early)
    first_pairs = [beside_quarter(got) for got in first_got]
    first_parts = [piece for pair in first_pairs for piece in four_quarters(pair, pair[1])]
    second_pairs = []
    for got in second_got:
        if z_split > 1:
            z_axes = ("zh", "zl")
            groups = [got] + [rotate(got, z_axes, n_z, by) for by in range(1, n_z)]
            groups[0] = tie(got, *[pair[1] for pair in first_pairs])
            got = order(lambda *groups: arrange(list(groups), z_axes, 1), *groups)
            got = got.reshape(planes, quarter, size)
        second_pairs.append(beside_quarter(got))
    cot_send = order(to_send, cotangent)
    cot_pieces = [cot_send[0]] + exchange(cot_send[1:], *x_late)

    window = (mine, size, length)
    piece_shape = (mine, part, length)
    n_pieces = 4 * (n_tp - 1)
    kept_struct = [struct(window, BF)] * 8
    w_struct = struct((planes, size, size), BF)
    fwd_scratch = [
        pltpu.VMEM((size, length), BF),
        pltpu.VMEM((taps, size, length), BF),
    ] + [pltpu.VMEM((size, length // HALVES), F32)] * (2 * HALVES)
    load_scratch = [
        pltpu.VMEM((planes, size, size), BF),
        pltpu.SemaphoreType.DMA((3 + n_pieces,)),
        pltpu.SemaphoreType.DMA,
    ]
    conv_flops = 2.0 * taps * size * size * length * mine
    ff_flops = 4.0 * size * size * length * mine
    weight_specs = [smem_spec(), whole_spec(pc.shape)] + [any_spec()] * (3 + n_pieces)
    first = order(
        pl.pallas_call(
            functools.partial(first_early_kernel, 0, n_tp, n_pieces, taps),
            grid=(early,),
            in_specs=weight_specs + [window_spec(piece_shape)] * n_tp,
            out_specs=[window_spec(window)] * 9 + [any_spec()],
            out_shape=kept_struct + [struct(window, BF), w_struct],
            scratch_shapes=fwd_scratch + load_scratch,
            compiler_params=params(),
            cost_estimate=cost((conv_flops + ff_flops) / 2, 20e6),
            name="forward_first_early",
        ),
        where,
        pc,
        conv_t,
        up_t,
        down_w,
        *first_parts,
        x_send[0],
        *x_early,
    )
    w0 = first[9]
    *kept0, hidden = first[:9]
    second_parts = [p for pair in second_pairs for p in four_quarters(pair, hidden)]
    if early < mine:
        *kept0, hidden = order(
            pl.pallas_call(
                functools.partial(first_late_kernel, 0, n_tp, taps, 9),
                grid=(mine - early,),
                in_specs=[smem_spec(), whole_spec(pc.shape), whole_spec(w_struct.shape)]
                + [window_spec(piece_shape, early)]
                + [window_spec(piece_shape)] * (n_tp - 1)
                + [any_spec()] * 9,
                out_specs=[window_spec(window, early)] * 9,
                out_shape=kept_struct + [struct(window, BF)],
                scratch_shapes=fwd_scratch,
                input_output_aliases={3 + n_tp + at: at for at in range(9)},
                compiler_params=params(),
                cost_estimate=cost((conv_flops + ff_flops) / 2, 20e6),
                name="forward_first_late",
            ),
            where,
            pc,
            w0,
            x_send[0],
            *x_late,
            *first[:9],
        )

    mask_rows = lax.dynamic_slice_in_dim(masked, me * mine, mine, 0).reshape(mine, 1, length)
    split = taps // 2
    low_taps, high_taps = tuple(range(split)), tuple(range(split, taps))
    skip = 2 * size + 128
    low_struct = struct((n_tp, part // 2, skip + split * size), BF)
    high_struct = struct((n_tp, part // 2, (taps - split) * size), BF)
    chain_out_specs = [window_spec(window)] * 2 + [
        whole_spec((2, size, size)),
        whole_spec((size, 128)),
    ]
    chain_out = [struct(window, BF)] * 2 + [
        struct((2, size, size), F32),
        struct((size, 128), F32),
    ]
    half_scratch = [pltpu.VMEM((size, length // HALVES), F32)] * HALVES
    chain_scratch = [
        pltpu.VMEM((size, length), BF),
        pltpu.VMEM((size, length), BF),
        pltpu.VMEM((7, size, 128), F32),
    ]
    wide_scratch = [pltpu.VMEM((taps, size, length), BF)]
    ff_specs = [plane_spec((1, size, size), taps), plane_spec((1, size, size), taps + 1)]
    conv_spec = plane_spec((taps, size, size), 0)
    kinds = lax.dynamic_slice_in_dim(species, me * mine, mine, 0)
    *y_pieces, dc1, dm1, ff1, small1, w1 = order(
        pl.pallas_call(
            functools.partial(second_kernel, 1, n_tp, n_pieces, taps),
            grid=(mine,),
            in_specs=weight_specs
            + [window_spec(window), whole_spec(read_rows.shape), window_spec((mine, 1, length))]
            + [smem_spec()]
            + [window_spec(piece_shape)] * n_tp,
            out_specs=[window_spec(piece_shape)] * n_tp
            + chain_out_specs
            + [any_spec()],
            out_shape=[struct(piece_shape, BF)] * n_tp
            + chain_out
            + [w_struct],
            scratch_shapes=fwd_scratch
            + [pltpu.VMEM((1, size, length), BF)] * 7
            + chain_scratch
            + [pltpu.VMEM((8 * SPECIES, 128), F32)]
            + load_scratch,
            compiler_params=params(),
            cost_estimate=cost(conv_flops + 3 * ff_flops, 20e6),
            name="second_layer",
        ),
        where,
        pc,
        conv_t,
        up_t,
        down_w,
        *second_parts,
        hidden,
        read_rows,
        mask_rows,
        kinds,
        *cot_pieces,
    )

    def chunk(layer, chosen, shape, dc, a, rest, name):
        keep, send = order(
            pl.pallas_call(
                functools.partial(weight_kernel, layer, taps, chosen),
                in_specs=[smem_spec()] + [vmem] * (2 + len(rest)),
                out_specs=[vmem] * 2,
                out_shape=[shape] * 2,
                scratch_shapes=[pltpu.VMEM((2, size, size), F32)],
                compiler_params=params(),
                cost_estimate=cost(conv_flops * len(chosen) / taps, 10e6),
                name=name,
            ),
            where,
            dc,
            a,
            *rest,
        )
        return Chunk(order, sizes, keep, send)

    low1 = chunk(1, low_taps, low_struct, dc1, hidden, (ff1, small1), "weights_second_low")
    high1 = chunk(1, high_taps, high_struct, dc1, hidden, (), "weights_second_high")
    low1.scatter("tp")
    high1.scatter("tp")

    dc0, dm0, ff0, small0 = order(
        pl.pallas_call(
            functools.partial(middle_kernel, 0, taps),
            grid=(mine,),
            in_specs=[conv_spec] + ff_specs + [whole_spec(pc.shape)] + [window_spec(window)] * 9,
            out_specs=chain_out_specs,
            out_shape=chain_out,
            scratch_shapes=wide_scratch + half_scratch + chain_scratch + half_scratch,
            compiler_params=params(),
            cost_estimate=cost(conv_flops + 2 * ff_flops, 20e6),
            name="chain_first",
        ),
        w1,
        w0,
        w0,
        pc,
        dc1,
        dm1,
        *kept0[1:],
    )
    y_back = [y_pieces[0]] + [
        rotate(tie(y_pieces[by], high1.terms[2][0]), "tp", n_tp, by) for by in range(1, n_tp)
    ]
    both1 = Pair(low1, high1)
    both1.scatter("y")
    high0 = chunk(0, high_taps, high_struct, dc0, kept0[0], (), "weights_first_high")
    low0 = chunk(0, low_taps, low_struct, dc0, kept0[0], (ff0, small0), "weights_first_low")
    both1.scatter("zl")
    y_out = order(lambda *pieces: arrange(list(pieces), "tp", 0), *y_back)
    y_out = y_out.reshape(windows, part, length)
    high0.scatter("tp")
    low0.scatter("y")
    both1.scatter("zh")
    x_grads = order(
        pl.pallas_call(
            functools.partial(bottom_kernel, 0, taps, n_tp),
            grid=(mine,),
            in_specs=[smem_spec(), conv_spec] + [window_spec(window)] * 2,
            out_specs=[window_spec(piece_shape)] * n_tp,
            out_shape=[struct(piece_shape, F32)] + [struct(piece_shape, BF)] * (n_tp - 1),
            scratch_shapes=wide_scratch + [pltpu.VMEM((size, length), F32)],
            compiler_params=params(),
            cost_estimate=cost(conv_flops, 15e6),
            name="input_grad",
        ),
        where,
        w0,
        dc0,
        dm0,
    )
    high0.scatter("y")
    low0.scatter("tp")
    both1.meet()
    low0.scatter("zl")
    x_back = [x_grads[0]] + [
        rotate(tie(x_grads[by], low0.terms[3][0]), "tp", n_tp, by) for by in range(1, n_tp)
    ]
    high0.scatter("zl")
    both1.widen()
    low0.scatter("zh")
    high0.scatter("zh")
    both1.spread()
    low0.meet()
    high0.meet()
    low0.widen()
    both1.cross()
    high0.widen()
    low0.spread()

    conv_struct = struct((layers, taps, part, size), F32)

    grad_conv, rest1 = order(
        pl.pallas_call(
            functools.partial(settle_rest_kernel, 1),
            in_specs=[smem_spec()] + [vmem] * 4,
            out_specs=[any_spec(), vmem],
            out_shape=[conv_struct, struct((part, skip), F32)],
            scratch_shapes=[
                pltpu.VMEM((4, taps, quarter, size), F32),
                pltpu.SemaphoreType.DMA((4,)),
            ],
            compiler_params=params(),
            name="settle_second",
        ),
        where,
        *both1.quarters,
    )
    grad_x = order(
        lambda *pieces: arrange([piece.astype(F32) for piece in pieces], "tp", 0), *x_back
    ).reshape(windows, part, length)
    high0.spread()
    low0.cross()
    high0.cross()
    grad_conv, grad_up_w, grad_down_w, g_conv_b, g_gain, g_bias, g_up_b, g_down_b = order(
        pl.pallas_call(
            functools.partial(settle_last_kernel, 0, split),
            in_specs=[smem_spec()] + [vmem] * 9 + [any_spec()],
            out_specs=[any_spec()] + [vmem] * 7,
            out_shape=[
                conv_struct,
                struct((layers, size, part), F32),
                struct((layers, part, size), F32),
                struct((layers, part), F32),
                struct((layers, 2, part), F32),
                struct((layers, 2, part), F32),
                struct((layers, part), F32),
                struct((layers, part), F32),
            ],
            scratch_shapes=[
                pltpu.VMEM((part, skip), F32),
                pltpu.VMEM((4, split, quarter, size), F32),
                pltpu.VMEM((4, taps - split, quarter, size), F32),
                pltpu.SemaphoreType.DMA((4,)),
                pltpu.SemaphoreType.DMA((4,)),
            ],
            input_output_aliases={10: 0},
            compiler_params=params(),
            name="settle_last",
        ),
        where,
        *low0.quarters,
        *high0.quarters,
        rest1,
        grad_conv,
    )

    grad_conv_w = jnp.transpose(grad_conv, (0, 2, 1, 3))
    species_sum = rest1[: 8 * SPECIES, 2 * size + 7].reshape(SPECIES, 8)[:, :CLASSES] / length
    return (
        y_out,
        grad_x,
        grad_conv_w,
        g_conv_b,
        g_gain,
        g_bias,
        grad_up_w,
        g_up_b,
        grad_down_w,
        g_down_b,
        species_sum,
    )


def solution(mesh):
    dp, tp = mesh.shape["dp"], mesh.shape["tp"]
    n_core = n_y = 2
    n_zl = 2
    n_zh = dp // (n_core * n_y * n_zl)
    fine = Mesh(mesh.devices.reshape(n_zh, n_zl, n_y, n_core, tp), DP + ("tp",))
    placed = (
        P(DP, "tp", None),
        P(None, "tp", None, None),
        P(None, "tp"),
        P(None, None, "tp"),
        P(None, None, "tp"),
        P(None, None, "tp"),
        P(None, "tp"),
        P(None, "tp", None),
        P(None, "tp"),
        P("tp", None),
        P(DP, "tp", None),
        P(DP, None),
        P(DP),
    )
    return jax.shard_map(
        functools.partial(body, (n_zh, n_zl, n_y, n_core, tp)),
        mesh=fine,
        in_specs=placed,
        out_specs=(
            P(DP, "tp", None),
            P(DP, "tp", None),
            P(None, "tp", None, None),
            P(None, "tp"),
            P(None, None, "tp"),
            P(None, None, "tp"),
            P(None, None, "tp"),
            P(None, "tp"),
            P(None, "tp", None),
            P(None, "tp"),
            P(),
        ),
        check_vma=False,
    )
```
